512 devices in a mesh: row: 16 (over x, y), col: 32 (over z, core).
Axes of the slice: x: 4, y: 4, z: 16, core: 2. Of those that a mesh axis runs over, the one named last changes fastest.
Arguments:
- distances: float32 [4096, 4096], P('row', 'col'), may hold values from 0.5 to 8
- neighbor_ids: int32 [10, 4096], replicated, may hold values from 0 to 4095
- edge_lengths: float32 [10, 4096], P(None, ('row', 'col')), may hold values from 0.125 to 1
- pivots: int32 [2], replicated, may hold values from 0 to 127
Outputs:
- geodesic: float32 [4096, 4096], P('row', 'col')
The draws below stay inside these ranges and needn't reach their ends.
All inputs are finite; a program needn't handle non-finite values.
Results may differ from the reference program's by a relative error of at most 0.00002.
Values sent between devices are 32-bit elements; how exact they have to be, the bound alone decides.
No kernel may reach another device: no remote copies, remote signals or barrier semaphores. Data moves between devices by JAX's collectives and lax.ppermute only.
A program may use at most 64 MiB of HBM per device.

```python
import jax
import jax.numpy as jnp
from jax import lax

NEIGHBORS = 10
PIVOT = 32
NV = 4096
BLOCKS = 128


def draw_distances(key, part):
    key = jax.random.fold_in(key, 11)
    unit = jax.random.uniform(key, (NV, NV), jnp.float32, 0.0, 1.0)
    return 0.5 + 7.5 * unit


def plant(values, own_key, least, largest):
    place = [jax.random.randint(jax.random.fold_in(own_key, axis), (), 0, length) for axis, length in enumerate(values.shape)]
    longest = values.shape.index(max(values.shape))
    beside = place[:longest] + [(place[longest] + 1) % values.shape[longest]] + place[longest + 1:]
    return values.at[tuple(place)].set(least).at[tuple(beside)].set(largest)


def block_levels(own_key, dims, shards, least, top_value):
    def one(position, blocks):
        steps = jax.random.uniform(jax.random.fold_in(jax.random.fold_in(own_key, 6), position), (blocks,), jnp.float32, least / len(shards), top_value / len(shards))
        return jnp.repeat(jnp.exp(steps), dims[position] // blocks).reshape((-1,) + (1,) * (len(dims) - position - 1))

    loudness = one(*shards[0])
    for cut in shards[1:]:
        loudness = loudness * one(*cut)
    return loudness


def setup_inputs(seed: int = 0) -> dict:
    seeds = jax.random.split(jax.random.key(seed), 5)
    distances = draw_distances(jax.random.fold_in(seeds[4], 71), 0)
    neighbor_ids = plant(jax.random.randint(seeds[1], (NEIGHBORS, NV), 0, NV), jax.random.fold_in(seeds[1], 1), 0, NV - 1).astype(jnp.int32)
    edge_lengths = jnp.clip(0.125 + 0.875 * jax.random.uniform(seeds[2], (NEIGHBORS, NV), jnp.float32) ** block_levels(seeds[2], (NEIGHBORS, NV), ((1, 512),), -0.2, 0.2), 0.125, 1.0)
    pivots = jax.random.randint(seeds[3], (2,), 0, BLOCKS).astype(jnp.int32)
    return {"distances": distances, "neighbor_ids": neighbor_ids, "edge_lengths": edge_lengths, "pivots": pivots}


def reference(distances, neighbor_ids, edge_lengths, pivots):
    vertex = jnp.arange(NV, dtype=jnp.int32)
    matrix = distances
    for k in range(NEIGHBORS):
        target = neighbor_ids[k].astype(jnp.int32)
        weight = edge_lengths[k]
        matrix = matrix.at[vertex, target].min(weight)
        matrix = matrix.at[target, vertex].min(weight)
    matrix = matrix.at[vertex, vertex].set(jnp.zeros((NV,), matrix.dtype))
    for q in range(2):
        base = (pivots[q] * PIVOT).astype(jnp.int32)

        def update(t, current):
            middle = (base + t).astype(jnp.int32)
            column = lax.dynamic_slice_in_dim(current, middle, 1, 1)
            row_line = lax.dynamic_slice_in_dim(current, middle, 1, 0)
            return jnp.minimum(current, column + row_line)

        matrix = lax.fori_loop(0, PIVOT, update, matrix)
    return matrix
```

```python
import jax
import jax.numpy as jnp
from jax import lax
from jax.experimental import pallas as pl
from jax.experimental.pallas import tpu as pltpu
from jax.sharding import Mesh, PartitionSpec as P

NEIGHBORS = 10
PIVOT = 32
ROWS = 256
COLS = 128
NXY = 16
NZ = 16
F32 = jnp.float32
INF = float("inf")
VMEM_LIMIT = 48 * 1024 * 1024

XY_RQ, XY_K, XY_L, XY_ROWS = 32, 64, 80, 96
Z_K, Z_L, Z_ROWS = 16, 32, 48


def lanes(rows):
    return lax.broadcasted_iota(jnp.int32, (rows, 128), 1)


def shift_lanes(x, amount):
    return pltpu.roll(x, lax.rem(amount + 1024, 128), 1)


def role(piv):
    core = lax.axis_index("core")
    p, q = piv[0], piv[1]
    first = core == 0
    return core, p, q, jnp.where(first, p, q), jnp.where(first, q, p)


def pack_kernel(piv, dist, keep, send):
    _, _, _, mine, other = role(piv)
    block = lanes(64) // PIVOT
    for ref, pivot in ((keep, mine), (send, other)):
        off = lax.rem(pivot, 4) * PIVOT
        packed = shift_lanes(dist[0:64, :], 0 - off)
        for b in range(1, 4):
            part = shift_lanes(dist[64 * b : 64 * b + 64, :], 32 * b - off)
            packed = jnp.where(block == b, part, packed)
        ref[...] = packed


def spread_kernel(piv, dist, keep, got, lengths, xy, piece0, piece1, piece2, piece3, cols, held):
    core, p, q, mine, _ = role(piv)
    z = lax.axis_index("z")
    row = lax.axis_index("row")
    own = lax.rem(mine // 4, 2) == core
    cols[...] = jnp.where(own, keep[...], got[1 - core])
    for m, piece in enumerate((piece0, piece1, piece2, piece3)):
        part = lax.rem(z, 4) ^ m
        piece[...] = cols[pl.ds(pl.multiple_of(16 * part, 16), 16), :]
    block = lanes(16) // PIVOT
    corner = jnp.zeros((16, 128), F32)
    for i, pivot in enumerate((p, q)):
        off = lax.rem(pivot, 8) * PIVOT
        b = off // 64
        a = off - 64 * b
        for h in range(2):
            part = cols[pl.ds(pl.multiple_of(a + 16 * h, 16), 16), :]
            part = shift_lanes(part, 32 * (2 * i + h) - 32 * b)
            corner = jnp.where(block == 2 * i + h, part, corner)
    held[...] = jnp.zeros_like(held)
    held[0:NEIGHBORS, 0:8] = lengths[...]
    own_lengths = shift_lanes(held[...], 8 * row)
    rows_p = dist[pl.ds(pl.multiple_of(lax.rem(p, 8) * PIVOT, 32), 32), :]
    rows_q = dist[pl.ds(pl.multiple_of(lax.rem(q, 8) * PIVOT, 32), 32), :]
    for d in range(NXY):
        xy[d, 0:XY_RQ] = rows_p
        xy[d, XY_RQ:XY_K] = rows_q
        xy[d, XY_K:XY_L] = corner
        xy[d, XY_L:XY_ROWS] = own_lengths


def gather_kernel(piv, xy, piece0, piece1, piece2, piece3, zchunk, rows):
    _, p, q, mine, _ = role(piv)
    z = lax.axis_index("z")
    row_p, row_q = p // 8, q // 8
    rows[0:32] = xy[row_p, 0:XY_RQ]
    rows[32:64] = xy[row_q, XY_RQ:XY_K]
    m = (mine // 8) ^ z
    piece = piece0[...]
    for i, ref in ((1, piece1), (2, piece2), (3, piece3)):
        piece = jnp.where(m == i, ref[...], piece)
    corner = jnp.where(lanes(16) < 64, xy[row_p, XY_K:XY_L], xy[row_q, XY_K:XY_L])
    lengths = xy[0, XY_L:XY_ROWS]
    for d in range(1, NXY):
        lengths = jnp.maximum(lengths, xy[d, XY_L:XY_ROWS])
    for d in range(NZ):
        zchunk[d, 0:Z_K] = piece
        zchunk[d, Z_K:Z_L] = corner
        zchunk[d, Z_L:Z_ROWS] = lengths


def take_lengths(zed, first, row, count, at):
    out = None
    for u in range(count):
        col = first + u
        part = shift_lanes(zed[lax.rem(col, 2), col // 2, Z_L:Z_ROWS], at + 8 * u - 8 * row)
        out = part if out is None else jnp.where(lanes(16) // 8 >= at // 8 + u, part, out)
    return out


def relax(entry, col_v, row_v, row_ids, row_len, col_ids, col_len):
    for k in range(NEIGHBORS):
        forward = jnp.where(row_ids[k] == col_v, row_len[k], INF)
        backward = jnp.where(col_ids[k : k + 1, :] == row_v, col_len[k : k + 1, :], INF)
        entry = jnp.minimum(entry, jnp.minimum(forward, backward))
    return jnp.where(row_v == col_v, 0.0, entry)


def final_kernel(piv, dist, rows, zed, ids, out, turned, cids, clen, pids, plen, cpan, rstar):
    p, q = piv[0], piv[1]
    row = lax.axis_index("row")
    z = lax.axis_index("z")
    core = lax.axis_index("core")
    col = 2 * z + core
    lane16 = lanes(16)

    def pad_ids(x):
        return jnp.concatenate([x.astype(F32), jnp.zeros((6, 128), F32)], 0)

    def pivot_ids(pivot, at):
        base = pl.multiple_of(pivot // 4 * 128, 128)
        return shift_lanes(pad_ids(ids[:, pl.ds(base, 128)]), at - lax.rem(pivot, 4) * PIVOT)

    cids[...] = pad_ids(ids[:, pl.ds(pl.multiple_of(128 * col, 128), 128)])
    clen[...] = take_lengths(zed, 16 * core, z, 16, 0)
    pids[...] = jnp.where(lane16 < 32, pivot_ids(p, 0), pivot_ids(q, 32))
    plen[...] = jnp.where(
        lane16 < 32,
        take_lengths(zed, lax.rem(p, 8) * 4, p // 8, 4, 0),
        take_lengths(zed, lax.rem(q, 8) * 4, q // 8, 4, 32),
    )
    for h in range(2):
        base = pl.multiple_of(256 * row + 128 * h, 128)
        square = jnp.concatenate(
            [
                pad_ids(ids[:, pl.ds(base, 128)]),
                take_lengths(zed, 16 * h, row, 16, 0),
                pids[...],
                plen[...],
                jnp.zeros((64, 128), F32),
            ],
            0,
        )
        turned[128 * h : 128 * h + 128, :] = square.T

    lane = lanes(8)
    sub = lax.broadcasted_iota(jnp.int32, (8, 128), 0)
    col_v0 = (128 * col + lane).astype(F32)
    col_v1 = jnp.where(lane < 32, 32 * p + lane, jnp.where(lane < 64, 32 * q + lane - 32, -1)).astype(F32)

    def columns(tile, at):
        return [jnp.broadcast_to(tile[:, at + k : at + k + 1], (8, 128)) for k in range(NEIGHBORS)]

    group_p, group_q = p // 32 * 4, q // 32 * 4
    for quarter in range(4):
        part_p = zed[0, group_p + quarter, 0:Z_K]
        part_q = zed[1, group_q + quarter, 0:Z_K]
        for b in range(4):
            left = shift_lanes(part_p, -32 * b)
            right = shift_lanes(part_q, 32 - 32 * b)
            at = 64 * b + 16 * quarter
            cpan[at : at + 16, :] = jnp.where(lane16 < 32, left, right)
    corner_p = zed[0, p // 8, Z_K:Z_L]
    corner_q = zed[1, q // 8, Z_K:Z_L]
    corner, line = [], []
    for b in range(4):
        both = jnp.where(lane16 < 32, shift_lanes(corner_p, -32 * b), shift_lanes(corner_q, 32 - 32 * b))
        both = jnp.where(lane16 < 64, both, INF)
        for h in range(2):
            tile = 2 * b + h
            vertex = (32 * p + 8 * tile) if tile < 4 else (32 * q + 8 * tile - 32)
            row_v = (vertex + sub).astype(F32)
            turn = turned[8 * tile : 8 * tile + 8, :]
            row_ids, row_len = columns(turn, 32), columns(turn, 48)
            corner.append(
                relax(both[8 * h : 8 * h + 8], col_v1, row_v, row_ids, row_len, pids[...], plen[...])
            )
            line.append(
                relax(rows[8 * tile : 8 * tile + 8, :], col_v0, row_v, row_ids, row_len, cids[...], clen[...])
            )
    corner = jnp.concatenate(corner, 0)
    line = jnp.concatenate(line, 0)
    for t in range(2 * PIVOT):
        step = corner[:, t : t + 1]
        line = jnp.minimum(line, step + line[t : t + 1, :])
        corner = jnp.minimum(corner, step + corner[t : t + 1, :])
    rstar[...] = line

    def body(i, carry):
        for j in range(2):
            at = pl.multiple_of(16 * i + 8 * j, 8)
            turn = turned[pl.ds(at, 8), :]
            row_v = (256 * row + at + sub).astype(F32)
            row_ids, row_len = columns(turn, 0), columns(turn, 16)
            here = relax(dist[pl.ds(at, 8), :], col_v0, row_v, row_ids, row_len, cids[...], clen[...])
            panel = relax(cpan[pl.ds(at, 8), :], col_v1, row_v, row_ids, row_len, pids[...], plen[...])
            for t in range(2 * PIVOT):
                here = jnp.minimum(here, panel[:, t : t + 1] + rstar[t : t + 1, :])
            out[pl.ds(at, 8), :] = here
        return carry

    lax.fori_loop(0, ROWS // 16, body, 0)


VM = pl.BlockSpec(memory_space=pltpu.VMEM)
SM = pl.BlockSpec(memory_space=pltpu.SMEM)


def call(kernel, shapes, scratch, n_in):
    return pl.pallas_call(
        kernel,
        out_shape=[jax.ShapeDtypeStruct(s, F32) for s in shapes],
        in_specs=[SM] + [VM] * n_in,
        out_specs=[VM] * len(shapes),
        scratch_shapes=[pltpu.VMEM(s, F32) for s in scratch],
        compiler_params=pltpu.CompilerParams(vmem_limit_bytes=VMEM_LIMIT),
    )


def on_device(distances, neighbor_ids, edge_lengths, pivots):
    keep, send = call(pack_kernel, [(64, 128)] * 2, [], 1)(pivots, distances)
    got = lax.all_gather(send, "core")
    xy, *pieces = call(
        spread_kernel, [(NXY, XY_ROWS, 128)] + [(16, 128)] * 4, [(64, 128), (16, 128)], 4
    )(pivots, distances, keep, got, edge_lengths)
    pieces = [pieces[0]] + [
        lax.ppermute(pieces[m], "z", [(i, i ^ m) for i in range(NZ)]) for m in range(1, 4)
    ]
    xy = lax.all_to_all(xy, "row", 0, 0)
    zed, rows = call(gather_kernel, [(NZ, Z_ROWS, 128), (64, 128)], [], 5)(pivots, xy, *pieces)
    zed = lax.all_to_all(zed, "z", 0, 0)
    zed = lax.all_gather(zed, "core")
    (out,) = call(
        final_kernel,
        [(ROWS, COLS)],
        [(256, 128)] + [(16, 128)] * 4 + [(256, 128), (64, 128)],
        4,
    )(pivots, distances, rows, zed, neighbor_ids)
    return out


def solution(mesh):
    fine = Mesh(mesh.devices.reshape(16, 16, 2), ("row", "z", "core"))
    placed = (P("row", ("z", "core")), P(), P(None, ("row", "z", "core")), P())
    return jax.shard_map(
        on_device, mesh=fine, in_specs=placed, out_specs=P("row", ("z", "core")), check_vma=False
    )
```

```python
import jax
import jax.numpy as jnp
from jax import lax
from jax.experimental import pallas as pl
from jax.experimental.pallas import tpu as pltpu
from jax.sharding import Mesh, PartitionSpec as P

NEIGHBORS = 10
PIVOT = 32
ROWS = 256
COLS = 128
NXY = 16
NZ = 16
F32 = jnp.float32
INF = float("inf")
VMEM_LIMIT = 48 * 1024 * 1024

XY_RQ, XY_K, XY_L, XY_ROWS = 32, 64, 80, 96
Z_K, Z_L, Z_ROWS = 16, 32, 40


def lanes(rows):
    return lax.broadcasted_iota(jnp.int32, (rows, 128), 1)


def shift_lanes(x, amount):
    if isinstance(amount, int):
        return pltpu.roll(x, amount % 128, 1) if amount % 128 else x
    return pltpu.roll(x, lax.rem(amount + 1024, 128), 1)


def role(piv):
    core = lax.axis_index("core")
    p, q = piv[0], piv[1]
    first = core == 0
    return core, p, q, jnp.where(first, p, q), jnp.where(first, q, p)


def pack_kernel(piv, dist, keep, send, mt):
    _, _, _, mine, other = role(piv)
    for h in range(2):
        mt[:, 128 * h : 128 * h + 128] = dist[128 * h : 128 * h + 128, :].T
    for ref, pivot in ((keep, mine), (send, other)):
        off = pl.multiple_of(lax.rem(pivot, 4) * PIVOT, 32)
        for h in range(2):
            ref[32 * h : 32 * h + 32, :] = mt[pl.ds(off, 32), 128 * h : 128 * h + 128]


def spread_kernel(piv, dist, keep, got, lengths, xy, piece0, piece1, piece2, piece3, cols, held):
    core, p, q, mine, _ = role(piv)
    z = lax.axis_index("z")
    row = lax.axis_index("row")
    own = lax.rem(mine // 4, 2) == core
    cols[...] = jnp.where(own, keep[...], got[1 - core])
    for m, piece in enumerate((piece0, piece1, piece2, piece3)):
        part = lax.rem(z, 4) ^ m
        piece[...] = cols[pl.ds(pl.multiple_of(16 * part, 16), 16), :]
    part_of = lanes(16) // PIVOT
    corner = None
    for i, pivot in enumerate((p, q)):
        off = lax.rem(pivot, 8) * PIVOT
        half = off // 128
        for h in range(2):
            part = cols[pl.ds(pl.multiple_of(32 * half + 16 * h, 16), 16), :]
            part = shift_lanes(part, 64 * h + 32 * i - off)
            corner = part if corner is None else jnp.where(part_of == 2 * h + i, part, corner)
    held[...] = jnp.zeros_like(held)
    held[0:8, 0:NEIGHBORS] = lengths[...]
    own_lengths = shift_lanes(held[...].T[0:16], 8 * row)
    rows_p = dist[pl.ds(pl.multiple_of(lax.rem(p, 8) * PIVOT, 32), 32), :]
    rows_q = dist[pl.ds(pl.multiple_of(lax.rem(q, 8) * PIVOT, 32), 32), :]
    for d in range(NXY):
        xy[d, 0:XY_RQ] = rows_p
        xy[d, XY_RQ:XY_K] = rows_q
        xy[d, XY_K:XY_L] = corner
        xy[d, XY_L:XY_ROWS] = own_lengths


def gather_kernel(piv, xy, piece0, piece1, piece2, piece3, zchunk, rows):
    _, p, q, mine, _ = role(piv)
    z = lax.axis_index("z")
    row = lax.axis_index("row")
    row_p, row_q = p // 8, q // 8
    rows[0:32] = xy[row_p, 0:XY_RQ]
    rows[32:64] = xy[row_q, XY_RQ:XY_K]
    m = (mine // 8) ^ z
    piece = piece0[...]
    for i, ref in ((1, piece1), (2, piece2), (3, piece3)):
        piece = jnp.where(m == i, ref[...], piece)
    corner = jnp.where(lax.rem(lanes(16), 64) < 32, xy[row_p, XY_K:XY_L], xy[row_q, XY_K:XY_L])
    lengths = xy[0, XY_L:XY_ROWS]
    for d in range(1, NXY):
        lengths = jnp.maximum(lengths, xy[d, XY_L:XY_ROWS])
    group = lanes(8) // 8
    fixed = None
    for h in range(2):
        part = lengths[8 * h : 8 * h + 8]
        for g, src in ((0, row), (2, row_p), (3, row_q)):
            moved = shift_lanes(part, 32 * h + 8 * g - 8 * src)
            fixed = moved if fixed is None else jnp.where(group == 4 * h + g, moved, fixed)
    for d in range(NZ):
        low = shift_lanes(lengths[0:8], 8 - 8 * d)
        high = shift_lanes(lengths[8:16], 40 - 8 * d)
        zchunk[d, 0:Z_K] = piece
        zchunk[d, Z_K:Z_L] = corner
        zchunk[d, Z_L:Z_ROWS] = jnp.where(group == 1, low, jnp.where(group == 5, high, fixed))


def ids_kernel(piv, ids, lane_ids, sub_ids, held):
    p, q = piv[0], piv[1]
    row = lax.axis_index("row")
    col = 2 * lax.axis_index("z") + lax.axis_index("core")

    def block(base):
        x = ids[:, pl.ds(pl.multiple_of(base, 128), 128)].astype(F32)
        return jnp.concatenate([x, jnp.zeros((6, 128), F32)], 0)

    for h in range(2):
        lane_ids[h] = block(256 * row + 128 * h)
    pivot_p = shift_lanes(block(p // 4 * 128), 0 - lax.rem(p, 4) * PIVOT)
    pivot_q = shift_lanes(block(q // 4 * 128), 32 - lax.rem(q, 4) * PIVOT)
    pivots = jnp.where(lanes(16) < 32, pivot_p, pivot_q)
    lane_ids[2] = pivots
    held[...] = jnp.zeros_like(held)
    held[0:16] = block(128 * col)
    held[16:32] = pivots
    turned = held[...].T
    for tile in range(24):
        at = 8 * (tile % 16)
        for k in range(NEIGHBORS):
            lane = 16 * (tile // 16) + k
            sub_ids[tile, k] = jnp.broadcast_to(turned[at : at + 8, lane : lane + 1], (8, 128))


def final_kernel(piv, mt, rows, zed, lane_ids, sub_ids, out, lane_len, turned, ct, kt, rt, spread, new):
    p, q = piv[0], piv[1]
    row = lax.axis_index("row")
    z = lax.axis_index("z")
    core = lax.axis_index("core")
    col = 2 * z + core

    def lengths_at(first, count, group, at):
        parts = []
        for h in range(2):
            out = None
            for u in range(count):
                device = first + u
                tile = zed[lax.rem(device, 2), device // 2, Z_L:Z_ROWS]
                tile = shift_lanes(tile, at + 8 * u - 8 * group - 32 * h)
                out = tile if out is None else jnp.where(lanes(8) // 8 >= at // 8 + u, tile, out)
            parts.append(out)
        return jnp.concatenate(parts, 0)

    lane_len[0] = lengths_at(0, 16, 0, 0)
    lane_len[1] = lengths_at(16, 16, 0, 0)
    lane_len[2] = jnp.where(
        lanes(16) < 32,
        lengths_at(lax.rem(p, 8) * 4, 4, 2, 0),
        lengths_at(lax.rem(q, 8) * 4, 4, 3, 32),
    )
    square = jnp.concatenate([lengths_at(16 * core, 16, 1, 0), lane_len[2], jnp.zeros((96, 128), F32)], 0)
    turned[...] = square.T
    rt[:, 0:64] = rows[...].T

    group_p, group_q = p // 32 * 4, q // 32 * 4
    for i, (pivot, group) in enumerate(((p, group_p), (q, group_q))):
        for quarter in range(4):
            at = 32 * i + 16 * (quarter % 2)
            half = 128 * (quarter // 2)
            ct[at : at + 16, half : half + 128] = zed[i, group + quarter, 0:Z_K]
        corner = zed[i, pivot // 8, Z_K:Z_L]
        kt[32 * i : 32 * i + 16, :] = corner
        kt[32 * i + 16 : 32 * i + 32, :] = shift_lanes(corner, 64)

    lane = lanes(8)
    sub = lax.broadcasted_iota(jnp.int32, (8, 128), 0)
    vertex = [
        (256 * row + lane).astype(F32),
        (256 * row + 128 + lane).astype(F32),
        jnp.where(lane < 32, 32 * p + lane, jnp.where(lane < 64, 32 * q + lane - 32, -1)).astype(F32),
    ]

    def relax(entries, vertices, tile, base):
        own = (base + sub).astype(F32)
        at, shift = 8 * (tile % 16), 16 * (tile // 16)
        turn = turned[at : at + 8, :]
        entries = list(entries)
        for k in range(NEIGHBORS):
            own_ids = sub_ids[tile, k]
            own_len = jnp.broadcast_to(turn[:, shift + k : shift + k + 1], (8, 128))
            for n, kind in enumerate(vertices):
                there = jnp.where(own_ids == vertex[kind], own_len, INF)
                back = jnp.where(lane_ids[kind, k : k + 1, :] == own, lane_len[kind, k : k + 1, :], INF)
                entries[n] = jnp.minimum(entries[n], jnp.minimum(there, back))
        return [jnp.where(own == vertex[kind], 0.0, e) for kind, e in zip(vertices, entries)]

    left, right, corner = [], [], []
    for tile in range(8):
        at = 8 * tile
        base = (32 * p + at) if tile < 4 else (32 * q + at - 32)
        a, b, c = relax(
            [ct[at : at + 8, 0:128], ct[at : at + 8, 128:256], kt[at : at + 8, :]], (0, 1, 2), 16 + tile, base
        )
        left.append(a)
        right.append(b)
        corner.append(c)
    left = jnp.concatenate(left, 0)
    right = jnp.concatenate(right, 0)
    corner = jnp.concatenate(corner, 0)
    for tile in range(16):
        for t in range(4 * tile, 4 * tile + 4):
            step = corner[:, t : t + 1]
            left = jnp.minimum(left, step + left[t : t + 1, :])
            right = jnp.minimum(right, step + right[t : t + 1, :])
            corner = jnp.minimum(corner, step + corner[t : t + 1, :])
        at = 8 * tile
        a, b, c = relax(
            [mt[at : at + 8, 0:128], mt[at : at + 8, 128:256], rt[at : at + 8, :]], (0, 1, 2), tile, 128 * col + at
        )
        new[at : at + 8, 0:128] = a
        new[at : at + 8, 128:256] = b
        for t in range(2 * PIVOT):
            spread[t, at : at + 8, :] = jnp.broadcast_to(c[:, t : t + 1], (8, 128))
    ct[:, 0:128] = left
    ct[:, 128:256] = right

    def body(i, carry):
        at = pl.multiple_of(32 * i, 32)
        for half in (0, 128):
            here = new[pl.ds(at, 32), half : half + 128]
            for t in range(2 * PIVOT):
                here = jnp.minimum(here, spread[t, pl.ds(at, 32), :] + ct[t : t + 1, half : half + 128])
            new[pl.ds(at, 32), half : half + 128] = here
        return carry

    lax.fori_loop(0, COLS // 32, body, 0)
    for h in range(2):
        out[128 * h : 128 * h + 128, :] = new[:, 128 * h : 128 * h + 128].T


VM = pl.BlockSpec(memory_space=pltpu.VMEM)
SM = pl.BlockSpec(memory_space=pltpu.SMEM)


def call(kernel, shapes, scratch, n_in):
    return pl.pallas_call(
        kernel,
        out_shape=[jax.ShapeDtypeStruct(s, F32) for s in shapes],
        in_specs=[SM] + [VM] * n_in,
        out_specs=[VM] * len(shapes),
        scratch_shapes=[pltpu.VMEM(s, F32) for s in scratch],
        compiler_params=pltpu.CompilerParams(vmem_limit_bytes=VMEM_LIMIT),
    )


FINAL_SCRATCH = [(3, 16, 128), (128, 128), (64, 256), (64, 128), (128, 128), (64, 128, 128), (128, 256)]


def on_device(distances, neighbor_ids, edge_lengths, pivots):
    keep, send, mt = call(pack_kernel, [(64, 128)] * 2 + [(COLS, ROWS)], [], 1)(pivots, distances)
    got = lax.all_gather(send, "core")
    xy, *pieces = call(
        spread_kernel, [(NXY, XY_ROWS, 128)] + [(16, 128)] * 4, [(64, 128), (128, 128)], 4
    )(pivots, distances, keep, got, edge_lengths.T)
    pieces = [pieces[0]] + [
        lax.ppermute(pieces[m], "z", [(i, i ^ m) for i in range(NZ)]) for m in range(1, 4)
    ]
    lane_ids, sub_ids = call(ids_kernel, [(3, 16, 128), (24, NEIGHBORS, 8, 128)], [(128, 128)], 1)(
        pivots, neighbor_ids
    )
    xy = lax.all_to_all(xy, "row", 0, 0)
    zed, rows = call(gather_kernel, [(NZ, Z_ROWS, 128), (64, 128)], [], 5)(pivots, xy, *pieces)
    zed = lax.all_to_all(zed, "z", 0, 0)
    zed = lax.all_gather(zed, "core")
    (out,) = call(final_kernel, [(ROWS, COLS)], FINAL_SCRATCH, 5)(pivots, mt, rows, zed, lane_ids, sub_ids)
    return out


def solution(mesh):
    fine = Mesh(mesh.devices.reshape(16, 16, 2), ("row", "z", "core"))
    placed = (P("row", ("z", "core")), P(), P(None, ("row", "z", "core")), P())
    return jax.shard_map(
        on_device, mesh=fine, in_specs=placed, out_specs=P("row", ("z", "core")), check_vma=False
    )
```

```python
import jax
import jax.numpy as jnp
from jax import lax
from jax.experimental import pallas as pl
from jax.experimental.pallas import tpu as pltpu
from jax.sharding import Mesh, PartitionSpec as P

NEIGHBORS = 10
PIVOT = 32
ROWS = 256
COLS = 128
NXY = 16
NZ = 16
F32 = jnp.float32
INF = float("inf")
VMEM_LIMIT = 48 * 1024 * 1024

XY_RQ, XY_K, XY_L, XY_ROWS = 32, 64, 80, 96
Z_K, Z_L, Z_ROWS = 16, 32, 40


def lanes(rows):
    return lax.broadcasted_iota(jnp.int32, (rows, 128), 1)


def shift_lanes(x, amount):
    if isinstance(amount, int):
        return pltpu.roll(x, amount % 128, 1) if amount % 128 else x
    return pltpu.roll(x, lax.rem(amount + 1024, 128), 1)


def role(piv):
    core = lax.axis_index("core")
    p, q = piv[0], piv[1]
    first = core == 0
    return core, p, q, jnp.where(first, p, q), jnp.where(first, q, p)


def pack_kernel(piv, dist, keep, send, mt):
    _, _, _, mine, other = role(piv)
    for h in range(2):
        mt[:, 128 * h : 128 * h + 128] = dist[128 * h : 128 * h + 128, :].T
    for ref, pivot in ((keep, mine), (send, other)):
        off = pl.multiple_of(lax.rem(pivot, 4) * PIVOT, 32)
        for h in range(2):
            ref[32 * h : 32 * h + 32, :] = mt[pl.ds(off, 32), 128 * h : 128 * h + 128]


def spread_kernel(piv, dist, keep, got, lengths, xy, piece0, piece1, piece2, piece3, cols, held):
    core, p, q, mine, _ = role(piv)
    z = lax.axis_index("z")
    row = lax.axis_index("row")
    own = lax.rem(mine // 4, 2) == core
    cols[...] = jnp.where(own, keep[...], got[1 - core])
    for m, piece in enumerate((piece0, piece1, piece2, piece3)):
        part = lax.rem(z, 4) ^ m
        piece[...] = cols[pl.ds(pl.multiple_of(16 * part, 16), 16), :]
    part_of = lanes(16) // PIVOT
    corner = None
    for i, pivot in enumerate((p, q)):
        off = lax.rem(pivot, 8) * PIVOT
        half = off // 128
        for h in range(2):
            part = cols[pl.ds(pl.multiple_of(32 * half + 16 * h, 16), 16), :]
            part = shift_lanes(part, 64 * h + 32 * i - off)
            corner = part if corner is None else jnp.where(part_of == 2 * h + i, part, corner)
    held[...] = jnp.zeros_like(held)
    held[0:8, 0:NEIGHBORS] = lengths[...]
    own_lengths = shift_lanes(held[...].T[0:16], 8 * row)
    rows_p = dist[pl.ds(pl.multiple_of(lax.rem(p, 8) * PIVOT, 32), 32), :]
    rows_q = dist[pl.ds(pl.multiple_of(lax.rem(q, 8) * PIVOT, 32), 32), :]
    for d in range(NXY):
        xy[d, 0:XY_RQ] = rows_p
        xy[d, XY_RQ:XY_K] = rows_q
        xy[d, XY_K:XY_L] = corner
        xy[d, XY_L:XY_ROWS] = own_lengths


def gather_kernel(piv, xy, piece0, piece1, piece2, piece3, zchunk, rows):
    _, p, q, mine, _ = role(piv)
    z = lax.axis_index("z")
    row = lax.axis_index("row")
    row_p, row_q = p // 8, q // 8
    rows[0:32] = xy[row_p, 0:XY_RQ]
    rows[32:64] = xy[row_q, XY_RQ:XY_K]
    m = (mine // 8) ^ z
    piece = piece0[...]
    for i, ref in ((1, piece1), (2, piece2), (3, piece3)):
        piece = jnp.where(m == i, ref[...], piece)
    corner = jnp.where(lax.rem(lanes(16), 64) < 32, xy[row_p, XY_K:XY_L], xy[row_q, XY_K:XY_L])
    lengths = xy[0, XY_L:XY_ROWS]
    for d in range(1, NXY):
        lengths = jnp.maximum(lengths, xy[d, XY_L:XY_ROWS])
    group = lanes(8) // 8
    fixed = None
    for h in range(2):
        part = lengths[8 * h : 8 * h + 8]
        for g, src in ((0, row), (2, row_p), (3, row_q)):
            moved = shift_lanes(part, 32 * h + 8 * g - 8 * src)
            fixed = moved if fixed is None else jnp.where(group == 4 * h + g, moved, fixed)
    for d in range(NZ):
        low = shift_lanes(lengths[0:8], 8 - 8 * d)
        high = shift_lanes(lengths[8:16], 40 - 8 * d)
        zchunk[d, 0:Z_K] = piece
        zchunk[d, Z_K:Z_L] = corner
        zchunk[d, Z_L:Z_ROWS] = jnp.where(group == 1, low, jnp.where(group == 5, high, fixed))


def ids_kernel(piv, ids, lane_ids, sub_ids, onehot, held):
    p, q = piv[0], piv[1]
    row = lax.axis_index("row")
    col = 2 * lax.axis_index("z") + lax.axis_index("core")

    def block(base):
        x = ids[:, pl.ds(pl.multiple_of(base, 128), 128)].astype(F32)
        return jnp.concatenate([x, jnp.zeros((6, 128), F32)], 0)

    for h in range(2):
        lane_ids[h] = block(256 * row + 128 * h)
    pivot_p = shift_lanes(block(p // 4 * 128), 0 - lax.rem(p, 4) * PIVOT)
    pivot_q = shift_lanes(block(q // 4 * 128), 32 - lax.rem(q, 4) * PIVOT)
    pivots = jnp.where(lanes(16) < 32, pivot_p, pivot_q)
    lane_ids[2] = pivots
    held[...] = jnp.zeros_like(held)
    held[0:16] = block(128 * col)
    held[16:32] = pivots
    turned = held[...].T
    for tile in range(24):
        at = 8 * (tile % 16)
        for k in range(NEIGHBORS):
            lane = 16 * (tile // 16) + k
            sub_ids[tile, k] = jnp.broadcast_to(turned[at : at + 8, lane : lane + 1], (8, 128))
    term = lax.broadcasted_iota(jnp.int32, (256, 128), 0)

    def fill(t, carry):
        picked = (lax.rem(term, 64) == t) & (term < 192)
        onehot[:, pl.ds(pl.multiple_of(128 * t, 128), 128)] = jnp.where(picked, 1.0, 0.0).astype(jnp.bfloat16)
        return carry

    lax.fori_loop(0, 2 * PIVOT, fill, 0)


def over_lanes(x, lane):
    return jnp.broadcast_to(x[:, lane : lane + 1], (8, 128))


def over_rows(x, row):
    return jnp.broadcast_to(x[row : row + 1, :], (8, 128))


def eliminate(state, b):
    corner = state[2]
    columns = [over_lanes(corner[b], 8 * b + j) for j in range(8)]
    rows = [state[kind][b] for kind in range(3)]
    for j in range(8):
        for u in range(j + 1, 8):
            columns[u] = jnp.minimum(columns[u], columns[j] + over_rows(columns[u], j))
        rows = [jnp.minimum(r, columns[j] + over_rows(r, j)) for r in rows]
    closed = [[over_rows(r, j) for j in range(8)] for r in rows]
    for i in range(8):
        if i == b:
            continue
        columns = [over_lanes(corner[i], 8 * b + j) for j in range(8)]
        for kind in range(3):
            paths = [columns[j] + closed[kind][j] for j in range(8)]
            while len(paths) > 1:
                paths = [jnp.minimum(paths[n], paths[n + 1]) for n in range(0, len(paths), 2)]
            state[kind][i] = jnp.minimum(state[kind][i], paths[0])
    for kind in range(3):
        state[kind][b] = rows[kind]


def thirds(x):
    x = x[:, 0:64]
    high = x.astype(jnp.bfloat16)
    rest = x - high.astype(F32)
    mid = rest.astype(jnp.bfloat16)
    low = (rest - mid.astype(F32)).astype(jnp.bfloat16)
    return jnp.concatenate([high, mid, low, low], 1)


def final_kernel(piv, mt, rows, zed, lane_ids, sub_ids, onehot, out, lane_len, turned, ct, kt, rt, spread, new):
    p, q = piv[0], piv[1]
    row = lax.axis_index("row")
    z = lax.axis_index("z")
    core = lax.axis_index("core")
    col = 2 * z + core

    def lengths_at(first, count, group, at):
        parts = []
        for h in range(2):
            out = None
            for u in range(count):
                device = first + u
                tile = zed[lax.rem(device, 2), device // 2, Z_L:Z_ROWS]
                tile = shift_lanes(tile, at + 8 * u - 8 * group - 32 * h)
                out = tile if out is None else jnp.where(lanes(8) // 8 >= at // 8 + u, tile, out)
            parts.append(out)
        return jnp.concatenate(parts, 0)

    lane_len[0] = lengths_at(0, 16, 0, 0)
    lane_len[1] = lengths_at(16, 16, 0, 0)
    lane_len[2] = jnp.where(
        lanes(16) < 32,
        lengths_at(lax.rem(p, 8) * 4, 4, 2, 0),
        lengths_at(lax.rem(q, 8) * 4, 4, 3, 32),
    )
    square = jnp.concatenate([lengths_at(16 * core, 16, 1, 0), lane_len[2], jnp.zeros((96, 128), F32)], 0)
    turned[...] = square.T
    rt[:, 0:64] = rows[...].T

    group_p, group_q = p // 32 * 4, q // 32 * 4
    for i, (pivot, group) in enumerate(((p, group_p), (q, group_q))):
        for quarter in range(4):
            at = 32 * i + 16 * (quarter % 2)
            half = 128 * (quarter // 2)
            ct[at : at + 16, half : half + 128] = zed[i, group + quarter, 0:Z_K]
        corner = zed[i, pivot // 8, Z_K:Z_L]
        kt[32 * i : 32 * i + 16, :] = corner
        kt[32 * i + 16 : 32 * i + 32, :] = shift_lanes(corner, 64)

    lane = lanes(8)
    sub = lax.broadcasted_iota(jnp.int32, (8, 128), 0)
    vertex = [
        (256 * row + lane).astype(F32),
        (256 * row + 128 + lane).astype(F32),
        jnp.where(lane < 32, 32 * p + lane, jnp.where(lane < 64, 32 * q + lane - 32, -1)).astype(F32),
    ]

    def relax(entries, vertices, tile, base):
        own = (base + sub).astype(F32)
        at, shift = 8 * (tile % 16), 16 * (tile // 16)
        turn = turned[at : at + 8, :]
        entries = list(entries)
        for k in range(NEIGHBORS):
            own_ids = sub_ids[tile, k]
            own_len = jnp.broadcast_to(turn[:, shift + k : shift + k + 1], (8, 128))
            for n, kind in enumerate(vertices):
                there = jnp.where(own_ids == vertex[kind], own_len, INF)
                back = jnp.where(lane_ids[kind, k : k + 1, :] == own, lane_len[kind, k : k + 1, :], INF)
                entries[n] = jnp.minimum(entries[n], jnp.minimum(there, back))
        return [jnp.where(own == vertex[kind], 0.0, e) for kind, e in zip(vertices, entries)]

    state = [[], [], []]
    for tile in range(8):
        at = 8 * tile
        base = (32 * p + at) if tile < 4 else (32 * q + at - 32)
        done = relax(
            [ct[at : at + 8, 0:128], ct[at : at + 8, 128:256], kt[at : at + 8, :]], (0, 1, 2), 16 + tile, base
        )
        for kind in range(3):
            state[kind].append(done[kind])
    for b in range(8):
        eliminate(state, b)
        if b < 4:
            for tile in range(4 * b, 4 * b + 4):
                at = 8 * tile
                entries = [mt[at : at + 8, 0:128], mt[at : at + 8, 128:256], rt[at : at + 8, :]]
                entries = relax(entries, (0, 1, 2), tile, 128 * col + at)
                new[at : at + 8, 0:128] = entries[0]
                new[at : at + 8, 128:256] = entries[1]
                rt[at : at + 8, :] = entries[2]
        else:
            if b == 4:
                parts = thirds(rt[...])
            for c in range(4 * b - 16, 4 * b - 12):
                spread[:, 512 * c : 512 * c + 512] = jnp.dot(
                    parts, onehot[:, 512 * c : 512 * c + 512], preferred_element_type=F32
                )
    for tile in range(8):
        at = 8 * tile
        ct[at : at + 8, 0:128] = state[0][tile]
        ct[at : at + 8, 128:256] = state[1][tile]

    def body(i, carry):
        at = pl.multiple_of(32 * i, 32)
        for half in (0, 128):
            here = new[pl.ds(at, 32), half : half + 128]
            for t in range(2 * PIVOT):
                here = jnp.minimum(here, spread[pl.ds(at, 32), 128 * t : 128 * t + 128] + ct[t : t + 1, half : half + 128])
            new[pl.ds(at, 32), half : half + 128] = here
        return carry

    lax.fori_loop(0, COLS // 32, body, 0)
    for h in range(2):
        out[128 * h : 128 * h + 128, :] = new[:, 128 * h : 128 * h + 128].T


VM = pl.BlockSpec(memory_space=pltpu.VMEM)
SM = pl.BlockSpec(memory_space=pltpu.SMEM)


def call(kernel, shapes, scratch, n_in):
    return pl.pallas_call(
        kernel,
        out_shape=[s if isinstance(s, jax.ShapeDtypeStruct) else jax.ShapeDtypeStruct(s, F32) for s in shapes],
        in_specs=[SM] + [VM] * n_in,
        out_specs=[VM] * len(shapes),
        scratch_shapes=[pltpu.VMEM(s, F32) for s in scratch],
        compiler_params=pltpu.CompilerParams(vmem_limit_bytes=VMEM_LIMIT),
    )


FINAL_SCRATCH = [(3, 16, 128), (128, 128), (64, 256), (64, 128), (128, 128), (128, 8192), (128, 256)]
ONEHOT = jax.ShapeDtypeStruct((256, 2 * PIVOT * 128), jnp.bfloat16)


def on_device(distances, neighbor_ids, edge_lengths, pivots):
    keep, send, mt = call(pack_kernel, [(64, 128)] * 2 + [(COLS, ROWS)], [], 1)(pivots, distances)
    got = lax.all_gather(send, "core")
    xy, *pieces = call(
        spread_kernel, [(NXY, XY_ROWS, 128)] + [(16, 128)] * 4, [(64, 128), (128, 128)], 4
    )(pivots, distances, keep, got, edge_lengths.T)
    pieces = [pieces[0]] + [
        lax.ppermute(pieces[m], "z", [(i, i ^ m) for i in range(NZ)]) for m in range(1, 4)
    ]
    lane_ids, sub_ids, onehot = call(
        ids_kernel, [(3, 16, 128), (24, NEIGHBORS, 8, 128), ONEHOT], [(128, 128)], 1
    )(pivots, neighbor_ids)
    xy = lax.all_to_all(xy, "row", 0, 0)
    zed, rows = call(gather_kernel, [(NZ, Z_ROWS, 128), (64, 128)], [], 5)(pivots, xy, *pieces)
    zed = lax.all_to_all(zed, "z", 0, 0)
    zed = lax.all_gather(zed, "core")
    (out,) = call(final_kernel, [(ROWS, COLS)], FINAL_SCRATCH, 6)(
        pivots, mt, rows, zed, lane_ids, sub_ids, onehot
    )
    return out


def solution(mesh):
    fine = Mesh(mesh.devices.reshape(16, 16, 2), ("row", "z", "core"))
    placed = (P("row", ("z", "core")), P(), P(None, ("row", "z", "core")), P())
    return jax.shard_map(
        on_device, mesh=fine, in_specs=placed, out_specs=P("row", ("z", "core")), check_vma=False
    )
```

```python
import jax
import jax.numpy as jnp
from jax import lax
from jax.experimental import pallas as pl
from jax.experimental.pallas import tpu as pltpu
from jax.sharding import Mesh, PartitionSpec as P

NEIGHBORS = 10
PIVOT = 32
ROWS = 256
COLS = 128
NXY = 16
NZ = 16
F32 = jnp.float32
INF = float("inf")

XY_K, XY_L, XY_ROWS = 4, 8, 16
Z_L, Z_K, Z_ROWS = 16, 20, 24
HOLDERS = 8


def lanes(rows):
    return lax.broadcasted_iota(jnp.int32, (rows, 128), 1)


def shift_lanes(x, amount):
    if isinstance(amount, int):
        return pltpu.roll(x, amount % 128, 1) if amount % 128 else x
    return pltpu.roll(x, lax.rem(amount + 1024, 128), 1)


def place():
    return lax.axis_index("row"), 4 * lax.axis_index("zh") + lax.axis_index("zl"), lax.axis_index("core")


def pack_kernel(piv, dist, lengths, mt, scatter, panel, own_lengths, block, held, sems):
    row, _, _ = place()
    copies = [
        pltpu.make_async_copy(dist, block, sems.at[0]),
        pltpu.make_async_copy(lengths, held, sems.at[1]),
    ]
    for copy in copies:
        copy.start()
    for copy in copies:
        copy.wait()
    for h in range(2):
        mt[:, 128 * h : 128 * h + 128] = block[128 * h : 128 * h + 128, :].T
    for i in range(2):
        off = lax.rem(piv[i], 4) * PIVOT
        for n in range(0, HOLDERS, 2):
            lines = mt[pl.ds(pl.multiple_of(off + 4 * n, 8), 8), :]
            for m in range(2):
                for h in range(2):
                    at = 8 * i + 4 * h
                    scatter[n + m, at : at + 4, :] = lines[4 * m : 4 * m + 4, 128 * h : 128 * h + 128]
        panel[32 * i : 32 * i + 32, :] = block[pl.ds(pl.multiple_of(lax.rem(piv[i], 8) * PIVOT, 32), 32), :]
    spaced = jnp.concatenate([held[...], jnp.zeros((8, 128 - NEIGHBORS), F32)], 1)
    own_lengths[...] = shift_lanes(spaced, 16 * lax.rem(row, 8))


def spread_kernel(piv, got, own_lengths, xy, piece):
    p, q = piv[0], piv[1]
    corner = None
    for i, pivot in enumerate((p, q)):
        holder = lax.rem(pivot // 8, 4) * 2 + lax.rem(pivot // 4, 2)
        mine = got[holder, 8 * i : 8 * i + 8]
        piece[8 * i : 8 * i + 8, :] = mine
        for j, other in enumerate((p, q)):
            half = jnp.where(lax.rem(other // 4, 2) == 0, mine, pltpu.roll(mine, 4, 0))
            half = shift_lanes(half, 64 * i + 32 * j - lax.rem(other, 4) * PIVOT)
            corner = half if corner is None else jnp.where(lanes(8) // PIVOT == 2 * i + j, half, corner)
    corner = pltpu.roll(corner, 4, 0)
    for d in range(NXY):
        xy[d, 0:XY_L] = corner
        xy[d, XY_L:XY_ROWS] = own_lengths[...]


def gather_kernel(piv, xy, piece, zchunk, turned):
    p, q = piv[0], piv[1]
    row, _, _ = place()
    row_p, row_q = p // 8, q // 8
    corner = jnp.where(lax.rem(lanes(8) // PIVOT, 2) == 0, xy[row_p, 0:XY_L], xy[row_q, 0:XY_L])
    low = xy[0, XY_L:XY_ROWS]
    high = xy[8, XY_L:XY_ROWS]
    for d in range(1, 8):
        low = jnp.maximum(low, xy[d, XY_L:XY_ROWS])
        high = jnp.maximum(high, xy[8 + d, XY_L:XY_ROWS])
    turned[...] = jnp.concatenate([low, high, jnp.zeros((112, 128), F32)], 0).T
    group = lanes(8) // 8

    def take(device, at, lengths):
        start = 16 * (device % 8)
        from_lane = 8 * (device // 8)
        first = turned[pl.ds(pl.multiple_of(start, 8), 8), :]
        second = turned[pl.ds(pl.multiple_of(start + 8, 8), 8), :]
        for g, part in ((0, first), (1, pltpu.roll(first, 4, 0)), (2, second)):
            moved = shift_lanes(part, 32 * g + 8 * at - from_lane)
            lengths = moved if lengths is None else jnp.where(group == 4 * g + at, moved, lengths)
        return lengths

    fixed = take(row_q, 3, take(row_p, 2, take(row, 0, None)))
    upper = lax.broadcasted_iota(jnp.int32, (8, 128), 0) < 4
    for d in range(NZ):
        zchunk[d, 0:Z_L] = piece[...]
        zchunk[d, Z_L:Z_ROWS] = jnp.where(upper, take(d, 1, fixed), corner)


def ids_kernel(piv, ids, lane_ids, sub_ids, onehot, held):
    p, q = piv[0], piv[1]
    row, z, core = place()
    col = 2 * z + core

    def block(base):
        x = ids[:, pl.ds(pl.multiple_of(base, 128), 128)].astype(F32)
        return jnp.concatenate([x, jnp.zeros((6, 128), F32)], 0)

    for h in range(2):
        lane_ids[h] = block(256 * row + 128 * h)
    pivot_p = shift_lanes(block(p // 4 * 128), 0 - lax.rem(p, 4) * PIVOT)
    pivot_q = shift_lanes(block(q // 4 * 128), 32 - lax.rem(q, 4) * PIVOT)
    pivots = jnp.where(lanes(16) < 32, pivot_p, pivot_q)
    lane_ids[2] = pivots
    held[...] = jnp.zeros_like(held)
    held[0:16] = block(128 * col)
    held[16:32] = pivots
    turned = held[...].T
    for tile in range(24):
        at = 8 * (tile % 16)
        for k in range(NEIGHBORS):
            lane = 16 * (tile // 16) + k
            sub_ids[tile, k] = jnp.broadcast_to(turned[at : at + 8, lane : lane + 1], (8, 128))
    term = lax.broadcasted_iota(jnp.int32, (256, 128), 0)

    def fill(t, carry):
        picked = (lax.rem(term, 64) == t) & (term < 192)
        onehot[:, pl.ds(pl.multiple_of(128 * t, 128), 128)] = jnp.where(picked, 1.0, 0.0).astype(jnp.bfloat16)
        return carry

    lax.fori_loop(0, 2 * PIVOT, fill, 0)


def over_lanes(x, lane):
    return jnp.broadcast_to(x[:, lane : lane + 1], (8, 128))


def over_rows(x, row):
    return jnp.broadcast_to(x[row : row + 1, :], (8, 128))


def eliminate(state, b):
    corner = state[2]
    columns = [over_lanes(corner[b], 8 * b + j) for j in range(8)]
    rows = [state[kind][b] for kind in range(3)]
    for j in range(8):
        for u in range(j + 1, 8):
            columns[u] = jnp.minimum(columns[u], columns[j] + over_rows(columns[u], j))
        rows = [jnp.minimum(r, columns[j] + over_rows(r, j)) for r in rows]
    closed = [[over_rows(r, j) for j in range(8)] for r in rows]
    for i in range(8):
        if i == b:
            continue
        columns = [over_lanes(corner[i], 8 * b + j) for j in range(8)]
        for kind in range(3):
            paths = [columns[j] + closed[kind][j] for j in range(8)]
            while len(paths) > 1:
                paths = [jnp.minimum(paths[n], paths[n + 1]) for n in range(0, len(paths), 2)]
            state[kind][i] = jnp.minimum(state[kind][i], paths[0])
    for kind in range(3):
        state[kind][b] = rows[kind]


def thirds(x):
    x = x[:, 0:64]
    high = x.astype(jnp.bfloat16)
    rest = x - high.astype(F32)
    mid = rest.astype(jnp.bfloat16)
    low = (rest - mid.astype(F32)).astype(jnp.bfloat16)
    return jnp.concatenate([high, mid, low, low], 1)


def final_kernel(piv, mt, rows, zed, lane_ids, sub_ids, onehot, out, lane_len, turned, ct, kt, rt, spread, new):
    p, q = piv[0], piv[1]
    row, z, core = place()
    col = 2 * z + core
    upper = lax.broadcasted_iota(jnp.int32, (8, 128), 0) < 4

    def lengths_at(first, count, group, at):
        parts = []
        for g in range(3):
            out = None
            for u in range(count):
                device = first + u
                tile = zed[lax.rem(device, 2), device // 2, Z_L:Z_ROWS]
                tile = shift_lanes(tile, at + 8 * u - 8 * group - 32 * g)
                out = tile if out is None else jnp.where(lanes(8) // 8 >= at // 8 + u, tile, out)
            parts.append(out)
        return jnp.concatenate([jnp.where(upper, parts[0], pltpu.roll(parts[1], 4, 0)), parts[2]], 0)

    lane_len[0] = lengths_at(0, 16, 0, 0)
    lane_len[1] = lengths_at(16, 16, 0, 0)
    lane_len[2] = jnp.where(
        lanes(16) < 32,
        lengths_at(lax.rem(p, 8) * 4, 4, 2, 0),
        lengths_at(lax.rem(q, 8) * 4, 4, 3, 32),
    )
    square = jnp.concatenate([lengths_at(16 * core, 16, 1, 0), lane_len[2], jnp.zeros((96, 128), F32)], 0)
    turned[...] = square.T
    rt[:, 0:64] = rows[...].T

    for i, pivot in enumerate((p, q)):
        for n in range(HOLDERS):
            holder = 4 * (pivot // 32) + n // 2
            at = 32 * i + 4 * n
            part = zed[n % 2, holder, 8 * i : 8 * i + 8]
            ct[at : at + 4, 0:128] = part[0:4]
            ct[at : at + 4, 128:256] = part[4:8]
            kt[at : at + 4, :] = shift_lanes(zed[n % 2, holder, Z_L:Z_ROWS], 64 * i)[4:8]

    lane = lanes(8)
    sub = lax.broadcasted_iota(jnp.int32, (8, 128), 0)
    vertex = [
        (256 * row + lane).astype(F32),
        (256 * row + 128 + lane).astype(F32),
        jnp.where(lane < 32, 32 * p + lane, jnp.where(lane < 64, 32 * q + lane - 32, -1)).astype(F32),
    ]

    def relax(entries, vertices, tile, base):
        own = (base + sub).astype(F32)
        at, shift = 8 * (tile % 16), 16 * (tile // 16)
        turn = turned[at : at + 8, :]
        entries = list(entries)
        for k in range(NEIGHBORS):
            own_ids = sub_ids[tile, k]
            own_len = jnp.broadcast_to(turn[:, shift + k : shift + k + 1], (8, 128))
            for n, kind in enumerate(vertices):
                there = jnp.where(own_ids == vertex[kind], own_len, INF)
                back = jnp.where(lane_ids[kind, k : k + 1, :] == own, lane_len[kind, k : k + 1, :], INF)
                entries[n] = jnp.minimum(entries[n], jnp.minimum(there, back))
        return [jnp.where(own == vertex[kind], 0.0, e) for kind, e in zip(vertices, entries)]

    state = [[], [], []]
    for tile in range(8):
        at = 8 * tile
        base = (32 * p + at) if tile < 4 else (32 * q + at - 32)
        done = relax(
            [ct[at : at + 8, 0:128], ct[at : at + 8, 128:256], kt[at : at + 8, :]], (0, 1, 2), 16 + tile, base
        )
        for kind in range(3):
            state[kind].append(done[kind])
    for b in range(8):
        eliminate(state, b)
        if b < 4:
            for tile in range(4 * b, 4 * b + 4):
                at = 8 * tile
                entries = [mt[at : at + 8, 0:128], mt[at : at + 8, 128:256], rt[at : at + 8, :]]
                entries = relax(entries, (0, 1, 2), tile, 128 * col + at)
                new[at : at + 8, 0:128] = entries[0]
                new[at : at + 8, 128:256] = entries[1]
                rt[at : at + 8, :] = entries[2]
        else:
            if b == 4:
                parts = thirds(rt[...])
            for c in range(4 * b - 16, 4 * b - 12):
                spread[:, 512 * c : 512 * c + 512] = jnp.dot(
                    parts, onehot[:, 512 * c : 512 * c + 512], preferred_element_type=F32
                )
    for tile in range(8):
        at = 8 * tile
        ct[at : at + 8, 0:128] = state[0][tile]
        ct[at : at + 8, 128:256] = state[1][tile]

    def body(i, carry):
        at = pl.multiple_of(32 * i, 32)
        for half in (0, 128):
            here = new[pl.ds(at, 32), half : half + 128]
            for t in range(2 * PIVOT):
                here = jnp.minimum(here, spread[pl.ds(at, 32), 128 * t : 128 * t + 128] + ct[t : t + 1, half : half + 128])
            new[pl.ds(at, 32), half : half + 128] = here
        return carry

    lax.fori_loop(0, COLS // 32, body, 0)
    for h in range(2):
        out[128 * h : 128 * h + 128, :] = new[:, 128 * h : 128 * h + 128].T


VM = pl.BlockSpec(memory_space=pltpu.VMEM)
SM = pl.BlockSpec(memory_space=pltpu.SMEM)
ANY = pl.BlockSpec(memory_space=pl.ANY)
MIB = 1024 * 1024


def call(kernel, shapes, scratch, ins, mib):
    return pl.pallas_call(
        kernel,
        out_shape=[s if isinstance(s, jax.ShapeDtypeStruct) else jax.ShapeDtypeStruct(s, F32) for s in shapes],
        in_specs=[SM] + ins,
        out_specs=[VM] * len(shapes),
        scratch_shapes=[pltpu.VMEM(s, F32) if isinstance(s, tuple) else s for s in scratch],
        compiler_params=pltpu.CompilerParams(vmem_limit_bytes=mib * MIB),
    )


FINAL_SCRATCH = [(3, 16, 128), (128, 128), (64, 256), (64, 128), (128, 128), (128, 8192), (128, 256)]
ONEHOT = jax.ShapeDtypeStruct((256, 2 * PIVOT * 128), jnp.bfloat16)


def on_device(distances, neighbor_ids, edge_lengths, pivots):
    mt, scatter, panel, own_lengths = call(
        pack_kernel,
        [(COLS, ROWS), (HOLDERS, 16, 128), (64, 128), (8, 128)],
        [(ROWS, COLS), (8, NEIGHBORS), pltpu.SemaphoreType.DMA((2,))],
        [ANY, ANY],
        8,
    )(pivots, distances, edge_lengths.T)
    home = jnp.repeat(pivots // 8, PIVOT)[:, None] ^ lax.axis_index("row")
    for m in (1, 2, 4, 8):
        other = lax.ppermute(panel, "row", [(i, i ^ m) for i in range(NXY)])
        panel = jnp.where((home & m) != 0, other, panel)
    scatter = lax.all_to_all(scatter, ("zl", "core"), 0, 0)
    xy, piece = call(spread_kernel, [(NXY, XY_ROWS, 128), (16, 128)], [], [VM] * 2, 8)(
        pivots, scatter, own_lengths
    )
    lane_ids, sub_ids, onehot = call(
        ids_kernel, [(3, 16, 128), (24, NEIGHBORS, 8, 128), ONEHOT], [(128, 128)], [VM], 16
    )(pivots, neighbor_ids)
    xy = lax.all_to_all(xy, "row", 0, 0)
    (zed,) = call(gather_kernel, [(NZ, Z_ROWS, 128)], [(128, 128)], [VM] * 2, 8)(pivots, xy, piece)
    zed = lax.all_to_all(zed, ("zh", "zl"), 0, 0)
    zed = lax.all_gather(zed, "core")
    (out,) = call(final_kernel, [(ROWS, COLS)], FINAL_SCRATCH, [VM] * 6, 24)(
        pivots, mt, panel, zed, lane_ids, sub_ids, onehot
    )
    return out


def solution(mesh):
    fine = Mesh(mesh.devices.reshape(16, 4, 4, 2), ("row", "zh", "zl", "core"))
    cols = ("zh", "zl", "core")
    placed = (P("row", cols), P(), P(None, ("row", *cols)), P())
    return jax.shard_map(on_device, mesh=fine, in_specs=placed, out_specs=P("row", cols), check_vma=False)
```

```python
import jax
import jax.numpy as jnp
from jax import lax
from jax.experimental import pallas as pl
from jax.experimental.pallas import tpu as pltpu
from jax.sharding import Mesh, PartitionSpec as P

NEIGHBORS = 10
PIVOT = 32
ROWS = 256
COLS = 128
NXY = 16
NZ = 16
F32 = jnp.float32
INF = float("inf")

XY_K, XY_L, XY_ROWS = 4, 8, 16
Z_L, Z_K, Z_ROWS = 16, 20, 24
HOLDERS = 8


def lanes(rows):
    return lax.broadcasted_iota(jnp.int32, (rows, 128), 1)


def shift_lanes(x, amount):
    if isinstance(amount, int):
        return pltpu.roll(x, amount % 128, 1) if amount % 128 else x
    return pltpu.roll(x, lax.rem(amount + 1024, 128), 1)


def place():
    return lax.axis_index("row"), 4 * lax.axis_index("zh") + lax.axis_index("zl"), lax.axis_index("core")


def pack_kernel(pivots, dist, lengths, piv, mt, scatter, panel, home, own_lengths, block, held, sems):
    row, _, _ = place()
    copies = [
        pltpu.make_async_copy(dist, block, sems.at[0]),
        pltpu.make_async_copy(lengths, held, sems.at[1]),
        pltpu.make_async_copy(pivots, piv, sems.at[2]),
    ]
    for copy in copies:
        copy.start()
    for copy in copies:
        copy.wait()
    for h in range(2):
        mt[:, 128 * h : 128 * h + 128] = block[128 * h : 128 * h + 128, :].T
    for i in range(2):
        off = lax.rem(piv[i], 4) * PIVOT
        for n in range(0, HOLDERS, 2):
            lines = mt[pl.ds(pl.multiple_of(off + 4 * n, 8), 8), :]
            for m in range(2):
                for h in range(2):
                    at = 8 * i + 4 * h
                    scatter[n + m, at : at + 4, :] = lines[4 * m : 4 * m + 4, 128 * h : 128 * h + 128]
        home[32 * i : 32 * i + 32, :] = jnp.full((32, 128), piv[i] // 8 ^ row)
        panel[32 * i : 32 * i + 32, :] = block[pl.ds(pl.multiple_of(lax.rem(piv[i], 8) * PIVOT, 32), 32), :]
    spaced = jnp.concatenate([held[...], jnp.zeros((8, 128 - NEIGHBORS), F32)], 1)
    own_lengths[...] = shift_lanes(spaced, 16 * lax.rem(row, 8))


def spread_kernel(piv, got, own_lengths, xy, piece):
    p, q = piv[0], piv[1]
    corner = None
    for i, pivot in enumerate((p, q)):
        holder = lax.rem(pivot // 8, 4) * 2 + lax.rem(pivot // 4, 2)
        mine = got[holder, 8 * i : 8 * i + 8]
        piece[8 * i : 8 * i + 8, :] = mine
        for j, other in enumerate((p, q)):
            half = jnp.where(lax.rem(other // 4, 2) == 0, mine, pltpu.roll(mine, 4, 0))
            half = shift_lanes(half, 64 * i + 32 * j - lax.rem(other, 4) * PIVOT)
            corner = half if corner is None else jnp.where(lanes(8) // PIVOT == 2 * i + j, half, corner)
    corner = pltpu.roll(corner, 4, 0)
    for d in range(NXY):
        xy[d, 0:XY_L] = corner
        xy[d, XY_L:XY_ROWS] = own_lengths[...]


def gather_kernel(piv, xy, piece, zchunk, turned):
    p, q = piv[0], piv[1]
    row, _, _ = place()
    row_p, row_q = p // 8, q // 8
    corner = jnp.where(lax.rem(lanes(8) // PIVOT, 2) == 0, xy[row_p, 0:XY_L], xy[row_q, 0:XY_L])
    low = xy[0, XY_L:XY_ROWS]
    high = xy[8, XY_L:XY_ROWS]
    for d in range(1, 8):
        low = jnp.maximum(low, xy[d, XY_L:XY_ROWS])
        high = jnp.maximum(high, xy[8 + d, XY_L:XY_ROWS])
    turned[...] = jnp.concatenate([low, high, jnp.zeros((112, 128), F32)], 0).T
    group = lanes(8) // 8

    def take(device, at, lengths):
        start = 16 * (device % 8)
        from_lane = 8 * (device // 8)
        first = turned[pl.ds(pl.multiple_of(start, 8), 8), :]
        second = turned[pl.ds(pl.multiple_of(start + 8, 8), 8), :]
        for g, part in ((0, first), (1, pltpu.roll(first, 4, 0)), (2, second)):
            moved = shift_lanes(part, 32 * g + 8 * at - from_lane)
            lengths = moved if lengths is None else jnp.where(group == 4 * g + at, moved, lengths)
        return lengths

    fixed = take(row_q, 3, take(row_p, 2, take(row, 0, None)))
    upper = lax.broadcasted_iota(jnp.int32, (8, 128), 0) < 4
    for d in range(NZ):
        zchunk[d, 0:Z_L] = piece[...]
        zchunk[d, Z_L:Z_ROWS] = jnp.where(upper, take(d, 1, fixed), corner)


def ids_kernel(piv, ids, lane_ids, sub_ids, onehot, held):
    p, q = piv[0], piv[1]
    row, z, core = place()
    col = 2 * z + core

    def block(base):
        x = ids[:, pl.ds(pl.multiple_of(base, 128), 128)].astype(F32)
        return jnp.concatenate([x, jnp.zeros((6, 128), F32)], 0)

    for h in range(2):
        lane_ids[h] = block(256 * row + 128 * h)
    pivot_p = shift_lanes(block(p // 4 * 128), 0 - lax.rem(p, 4) * PIVOT)
    pivot_q = shift_lanes(block(q // 4 * 128), 32 - lax.rem(q, 4) * PIVOT)
    pivots = jnp.where(lanes(16) < 32, pivot_p, pivot_q)
    lane_ids[2] = pivots
    held[...] = jnp.zeros_like(held)
    held[0:16] = block(128 * col)
    held[16:32] = pivots
    turned = held[...].T
    for tile in range(24):
        at = 8 * (tile % 16)
        for k in range(NEIGHBORS):
            lane = 16 * (tile // 16) + k
            sub_ids[tile, k] = jnp.broadcast_to(turned[at : at + 8, lane : lane + 1], (8, 128))
    term = lax.broadcasted_iota(jnp.int32, (64, 128), 0)
    for t in range(16):
        picked = (lax.rem(term, 16) == t) & (term < 48)
        onehot[:, 128 * t : 128 * t + 128] = jnp.where(picked, 1.0, 0.0).astype(jnp.bfloat16)


def over_lanes(x, lane):
    return jnp.broadcast_to(x[:, lane : lane + 1], (8, 128))


def over_rows(x, row):
    return jnp.broadcast_to(x[row : row + 1, :], (8, 128))


def eliminate(state, b):
    corner = state[2]
    columns = [over_lanes(corner[b], 8 * b + j) for j in range(8)]
    rows = [state[kind][b] for kind in range(3)]
    for j in range(8):
        for u in range(j + 1, 8):
            columns[u] = jnp.minimum(columns[u], columns[j] + over_rows(columns[u], j))
        rows = [jnp.minimum(r, columns[j] + over_rows(r, j)) for r in rows]
    closed = [[over_rows(r, j) for j in range(8)] for r in rows]
    for i in range(8):
        if i == b:
            continue
        columns = [over_lanes(corner[i], 8 * b + j) for j in range(8)]
        for kind in range(3):
            paths = [columns[j] + closed[kind][j] for j in range(8)]
            while len(paths) > 1:
                paths = [jnp.minimum(paths[n], paths[n + 1]) for n in range(0, len(paths), 2)]
            state[kind][i] = jnp.minimum(state[kind][i], paths[0])
    for kind in range(3):
        state[kind][b] = rows[kind]


def thirds(x):
    high = x.astype(jnp.bfloat16)
    rest = x - high.astype(F32)
    mid = rest.astype(jnp.bfloat16)
    low = (rest - mid.astype(F32)).astype(jnp.bfloat16)
    return [
        jnp.concatenate([term[:, 16 * n : 16 * n + 16] for term in (high, mid, low, low)], 1) for n in range(4)
    ]


def final_kernel(piv, mt, rows, zed, lane_ids, sub_ids, onehot, out, lane_len, turned, ct, kt, rt, spread, new):
    p, q = piv[0], piv[1]
    row, z, core = place()
    col = 2 * z + core
    upper = lax.broadcasted_iota(jnp.int32, (8, 128), 0) < 4

    def lengths_at(first, count, group, at):
        parts = []
        for g in range(3):
            out = None
            for u in range(count):
                device = first + u
                tile = zed[lax.rem(device, 2), device // 2, Z_L:Z_ROWS]
                tile = shift_lanes(tile, at + 8 * u - 8 * group - 32 * g)
                out = tile if out is None else jnp.where(lanes(8) // 8 >= at // 8 + u, tile, out)
            parts.append(out)
        return jnp.concatenate([jnp.where(upper, parts[0], pltpu.roll(parts[1], 4, 0)), parts[2]], 0)

    lane_len[0] = lengths_at(0, 16, 0, 0)
    lane_len[1] = lengths_at(16, 16, 0, 0)
    lane_len[2] = jnp.where(
        lanes(16) < 32,
        lengths_at(lax.rem(p, 8) * 4, 4, 2, 0),
        lengths_at(lax.rem(q, 8) * 4, 4, 3, 32),
    )
    square = jnp.concatenate([lengths_at(16 * core, 16, 1, 0), lane_len[2], jnp.zeros((96, 128), F32)], 0)
    turned[...] = square.T
    rt[:, 0:64] = rows[...].T

    for i, pivot in enumerate((p, q)):
        for n in range(HOLDERS):
            holder = 4 * (pivot // 32) + n // 2
            at = 32 * i + 4 * n
            part = zed[n % 2, holder, 8 * i : 8 * i + 8]
            ct[at : at + 4, 0:128] = part[0:4]
            ct[at : at + 4, 128:256] = part[4:8]
            kt[at : at + 4, :] = shift_lanes(zed[n % 2, holder, Z_L:Z_ROWS], 64 * i)[4:8]

    lane = lanes(8)
    sub = lax.broadcasted_iota(jnp.int32, (8, 128), 0)
    vertex = [
        (256 * row + lane).astype(F32),
        (256 * row + 128 + lane).astype(F32),
        jnp.where(lane < 32, 32 * p + lane, jnp.where(lane < 64, 32 * q + lane - 32, -1)).astype(F32),
    ]

    def relax(entries, vertices, tile, base):
        own = (base + sub).astype(F32)
        at, shift = 8 * (tile % 16), 16 * (tile // 16)
        turn = turned[at : at + 8, :]
        entries = list(entries)
        for k in range(NEIGHBORS):
            own_ids = sub_ids[tile, k]
            own_len = jnp.broadcast_to(turn[:, shift + k : shift + k + 1], (8, 128))
            for n, kind in enumerate(vertices):
                there = jnp.where(own_ids == vertex[kind], own_len, INF)
                back = jnp.where(lane_ids[kind, k : k + 1, :] == own, lane_len[kind, k : k + 1, :], INF)
                entries[n] = jnp.minimum(entries[n], jnp.minimum(there, back))
        return [jnp.where(own == vertex[kind], 0.0, e) for kind, e in zip(vertices, entries)]

    state = [[], [], []]
    for tile in range(8):
        at = 8 * tile
        base = (32 * p + at) if tile < 4 else (32 * q + at - 32)
        done = relax(
            [ct[at : at + 8, 0:128], ct[at : at + 8, 128:256], kt[at : at + 8, :]], (0, 1, 2), 16 + tile, base
        )
        for kind in range(3):
            state[kind].append(done[kind])
    for b in range(8):
        eliminate(state, b)
        if b < 4:
            for tile in range(4 * b, 4 * b + 4):
                at = 8 * tile
                entries = [mt[at : at + 8, 0:128], mt[at : at + 8, 128:256], rt[at : at + 8, :]]
                entries = relax(entries, (0, 1, 2), tile, 128 * col + at)
                new[at : at + 8, 0:128] = entries[0]
                new[at : at + 8, 128:256] = entries[1]
                rt[at : at + 8, :] = entries[2]
        else:
            if b == 4:
                parts = thirds(rt[...])
            for c in range(4):
                at = 2048 * (b - 4) + 512 * c
                spread[:, at : at + 512] = jnp.dot(
                    parts[b - 4], onehot[:, 512 * c : 512 * c + 512], preferred_element_type=F32
                )
    for tile in range(8):
        at = 8 * tile
        ct[at : at + 8, 0:128] = state[0][tile]
        ct[at : at + 8, 128:256] = state[1][tile]

    def body(i, carry):
        at = pl.multiple_of(32 * i, 32)
        for half in (0, 128):
            here = new[pl.ds(at, 32), half : half + 128]
            for t in range(2 * PIVOT):
                here = jnp.minimum(here, spread[pl.ds(at, 32), 128 * t : 128 * t + 128] + ct[t : t + 1, half : half + 128])
            new[pl.ds(at, 32), half : half + 128] = here
        return carry

    lax.fori_loop(0, COLS // 32, body, 0)
    for h in range(2):
        out[128 * h : 128 * h + 128, :] = new[:, 128 * h : 128 * h + 128].T


VM = pl.BlockSpec(memory_space=pltpu.VMEM)
SM = pl.BlockSpec(memory_space=pltpu.SMEM)
HBM = pl.BlockSpec(memory_space=pltpu.HBM)
MIB = 1024 * 1024


def call(kernel, shapes, scratch, ins, mib, outs=None):
    return pl.pallas_call(
        kernel,
        out_shape=[s if isinstance(s, jax.ShapeDtypeStruct) else jax.ShapeDtypeStruct(s, F32) for s in shapes],
        in_specs=ins,
        out_specs=outs or [VM] * len(shapes),
        scratch_shapes=[pltpu.VMEM(s, F32) if isinstance(s, tuple) else s for s in scratch],
        compiler_params=pltpu.CompilerParams(vmem_limit_bytes=mib * MIB),
    )


FINAL_SCRATCH = [(3, 16, 128), (128, 128), (64, 256), (64, 128), (128, 128), (128, 8192), (128, 256)]
ONEHOT = jax.ShapeDtypeStruct((64, 16 * 128), jnp.bfloat16)
INTS = jax.ShapeDtypeStruct((64, 128), jnp.int32)
PIVOTS = jax.ShapeDtypeStruct((2,), jnp.int32)


def on_device(distances, neighbor_ids, edge_lengths, pivots):
    piv, mt, scatter, panel, home, own_lengths = call(
        pack_kernel,
        [PIVOTS, (COLS, ROWS), (HOLDERS, 16, 128), (64, 128), INTS, (8, 128)],
        [(ROWS, COLS), (8, NEIGHBORS), pltpu.SemaphoreType.DMA((3,))],
        [HBM] * 3,
        8,
        [SM] + [VM] * 5,
    )(*[pltpu.with_memory_space_constraint(x, pltpu.HBM) for x in (pivots, distances, edge_lengths.T)])
    for m in (1, 2, 4, 8):
        other = lax.ppermute(panel, "row", [(i, i ^ m) for i in range(NXY)])
        panel = jnp.where((home & m) != 0, other, panel)
    scatter = lax.all_to_all(scatter, ("zl", "core"), 0, 0)
    xy, piece = call(spread_kernel, [(NXY, XY_ROWS, 128), (16, 128)], [], [SM] + [VM] * 2, 8)(
        piv, scatter, own_lengths
    )
    lane_ids, sub_ids, onehot = call(
        ids_kernel, [(3, 16, 128), (24, NEIGHBORS, 8, 128), ONEHOT], [(128, 128)], [SM, VM], 16
    )(piv, neighbor_ids)
    xy = lax.all_to_all(xy, "row", 0, 0)
    (zed,) = call(gather_kernel, [(NZ, Z_ROWS, 128)], [(128, 128)], [SM] + [VM] * 2, 8)(piv, xy, piece)
    zed = lax.all_to_all(zed, ("zh", "zl"), 0, 0)
    zed = lax.all_gather(zed, "core")
    (out,) = call(final_kernel, [(ROWS, COLS)], FINAL_SCRATCH, [SM] + [VM] * 6, 24)(
        piv, mt, panel, zed, lane_ids, sub_ids, onehot
    )
    return out


def solution(mesh):
    fine = Mesh(mesh.devices.reshape(16, 4, 4, 2), ("row", "zh", "zl", "core"))
    cols = ("zh", "zl", "core")
    placed = (P("row", cols), P(), P(None, ("row", *cols)), P())
    return jax.shard_map(on_device, mesh=fine, in_specs=placed, out_specs=P("row", cols), check_vma=False)
```

```python
import jax
import jax.numpy as jnp
from jax import lax
from jax.experimental import pallas as pl
from jax.experimental.pallas import tpu as pltpu
from jax.sharding import Mesh, PartitionSpec as P

NEIGHBORS = 10
PIVOT = 32
ROWS = 256
COLS = 128
NXY = 16
NZ = 16
F32 = jnp.float32
INF = float("inf")

XY_L, XY_R, XY_ROWS = 8, 16, 80
Z_L, Z_K, Z_ROWS = 16, 20, 24
HOLDERS = 8


def lanes(rows):
    return lax.broadcasted_iota(jnp.int32, (rows, 128), 1)


def shift_lanes(x, amount):
    if isinstance(amount, int):
        return pltpu.roll(x, amount % 128, 1) if amount % 128 else x
    return pltpu.roll(x, lax.rem(amount + 1024, 128), 1)


def place():
    return lax.axis_index("row"), 4 * lax.axis_index("zh") + lax.axis_index("zl"), lax.axis_index("core")


def pack_kernel(pivots, dist, lengths, piv, mt, scatter, panel, own_lengths, block, held, sems):
    row, _, _ = place()
    copies = [
        pltpu.make_async_copy(dist, block, sems.at[0]),
        pltpu.make_async_copy(lengths, held, sems.at[1]),
        pltpu.make_async_copy(pivots, piv, sems.at[2]),
    ]
    for copy in copies:
        copy.start()
    for copy in copies:
        copy.wait()
    for h in range(2):
        mt[:, 128 * h : 128 * h + 128] = block[128 * h : 128 * h + 128, :].T
    for i in range(2):
        off = lax.rem(piv[i], 4) * PIVOT
        for n in range(0, HOLDERS, 2):
            lines = mt[pl.ds(pl.multiple_of(off + 4 * n, 8), 8), :]
            for m in range(2):
                for h in range(2):
                    at = 8 * i + 4 * h
                    scatter[n + m, at : at + 4, :] = lines[4 * m : 4 * m + 4, 128 * h : 128 * h + 128]
        panel[32 * i : 32 * i + 32, :] = block[pl.ds(pl.multiple_of(lax.rem(piv[i], 8) * PIVOT, 32), 32), :]
    spaced = jnp.concatenate([held[...], jnp.zeros((8, 128 - NEIGHBORS), F32)], 1)
    own_lengths[...] = shift_lanes(spaced, 16 * lax.rem(row, 8))


def spread_kernel(piv, got, own_lengths, panel, xy, piece):
    p, q = piv[0], piv[1]
    corner = None
    for i, pivot in enumerate((p, q)):
        holder = lax.rem(pivot // 8, 4) * 2 + lax.rem(pivot // 4, 2)
        mine = got[holder, 8 * i : 8 * i + 8]
        piece[8 * i : 8 * i + 8, :] = mine
        for j, other in enumerate((p, q)):
            half = jnp.where(lax.rem(other // 4, 2) == 0, mine, pltpu.roll(mine, 4, 0))
            half = shift_lanes(half, 64 * i + 32 * j - lax.rem(other, 4) * PIVOT)
            corner = half if corner is None else jnp.where(lanes(8) // PIVOT == 2 * i + j, half, corner)
    corner = pltpu.roll(corner, 4, 0)
    for d in range(NXY):
        xy[d, 0:XY_L] = corner
        xy[d, XY_L:XY_R] = own_lengths[...]
        xy[d, XY_R:XY_ROWS] = panel[...]


def gather_kernel(piv, xy, piece, zchunk, rows, turned):
    p, q = piv[0], piv[1]
    row, _, _ = place()
    row_p, row_q = p // 8, q // 8
    rows[0:32] = xy[row_p, XY_R : XY_R + 32]
    rows[32:64] = xy[row_q, XY_R + 32 : XY_ROWS]
    corner = jnp.where(lax.rem(lanes(8) // PIVOT, 2) == 0, xy[row_p, 0:XY_L], xy[row_q, 0:XY_L])
    low = xy[0, XY_L:XY_R]
    high = xy[8, XY_L:XY_R]
    for d in range(1, 8):
        low = jnp.maximum(low, xy[d, XY_L:XY_R])
        high = jnp.maximum(high, xy[8 + d, XY_L:XY_R])
    turned[...] = jnp.concatenate([low, high, jnp.zeros((112, 128), F32)], 0).T
    group = lanes(8) // 8

    def take(device, at, lengths):
        start = 16 * (device % 8)
        from_lane = 8 * (device // 8)
        first = turned[pl.ds(pl.multiple_of(start, 8), 8), :]
        second = turned[pl.ds(pl.multiple_of(start + 8, 8), 8), :]
        for g, part in ((0, first), (1, pltpu.roll(first, 4, 0)), (2, second)):
            moved = shift_lanes(part, 32 * g + 8 * at - from_lane)
            lengths = moved if lengths is None else jnp.where(group == 4 * g + at, moved, lengths)
        return lengths

    fixed = take(row_q, 3, take(row_p, 2, take(row, 0, None)))
    upper = lax.broadcasted_iota(jnp.int32, (8, 128), 0) < 4
    for d in range(NZ):
        zchunk[d, 0:Z_L] = piece[...]
        zchunk[d, Z_L:Z_ROWS] = jnp.where(upper, take(d, 1, fixed), corner)


def ids_kernel(piv, ids, lane_ids, sub_ids, onehot, held):
    p, q = piv[0], piv[1]
    row, z, core = place()
    col = 2 * z + core

    def block(base):
        x = ids[:, pl.ds(pl.multiple_of(base, 128), 128)].astype(F32)
        return jnp.concatenate([x, jnp.zeros((6, 128), F32)], 0)

    for h in range(2):
        lane_ids[h] = block(256 * row + 128 * h)
    pivot_p = shift_lanes(block(p // 4 * 128), 0 - lax.rem(p, 4) * PIVOT)
    pivot_q = shift_lanes(block(q // 4 * 128), 32 - lax.rem(q, 4) * PIVOT)
    pivots = jnp.where(lanes(16) < 32, pivot_p, pivot_q)
    lane_ids[2] = pivots
    held[...] = jnp.zeros_like(held)
    held[0:16] = block(128 * col)
    held[16:32] = pivots
    turned = held[...].T
    for tile in range(24):
        at = 8 * (tile % 16)
        for k in range(NEIGHBORS):
            lane = 16 * (tile // 16) + k
            sub_ids[tile, k] = jnp.broadcast_to(turned[at : at + 8, lane : lane + 1], (8, 128))
    term = lax.broadcasted_iota(jnp.int32, (64, 128), 0)
    for t in range(16):
        picked = (lax.rem(term, 16) == t) & (term < 48)
        onehot[:, 128 * t : 128 * t + 128] = jnp.where(picked, 1.0, 0.0).astype(jnp.bfloat16)


def over_lanes(x, lane):
    return jnp.broadcast_to(x[:, lane : lane + 1], (8, 128))


def over_rows(x, row):
    return jnp.broadcast_to(x[row : row + 1, :], (8, 128))


def eliminate(state, b):
    corner = state[2]
    columns = [over_lanes(corner[b], 8 * b + j) for j in range(8)]
    rows = [state[kind][b] for kind in range(3)]
    for j in range(8):
        for u in range(j + 1, 8):
            columns[u] = jnp.minimum(columns[u], columns[j] + over_rows(columns[u], j))
        rows = [jnp.minimum(r, columns[j] + over_rows(r, j)) for r in rows]
    closed = [[over_rows(r, j) for j in range(8)] for r in rows]
    for i in range(8):
        if i == b:
            continue
        columns = [over_lanes(corner[i], 8 * b + j) for j in range(8)]
        for kind in range(3):
            paths = [columns[j] + closed[kind][j] for j in range(8)]
            while len(paths) > 1:
                paths = [jnp.minimum(paths[n], paths[n + 1]) for n in range(0, len(paths), 2)]
            state[kind][i] = jnp.minimum(state[kind][i], paths[0])
    for kind in range(3):
        state[kind][b] = rows[kind]


def thirds(x):
    high = x.astype(jnp.bfloat16)
    rest = x - high.astype(F32)
    mid = rest.astype(jnp.bfloat16)
    low = (rest - mid.astype(F32)).astype(jnp.bfloat16)
    return [
        jnp.concatenate([term[:, 16 * n : 16 * n + 16] for term in (high, mid, low, low)], 1) for n in range(4)
    ]


def final_kernel(piv, mt, rows, zed, lane_ids, sub_ids, onehot, out, lane_len, turned, ct, kt, rt, spread, new):
    p, q = piv[0], piv[1]
    row, z, core = place()
    col = 2 * z + core
    upper = lax.broadcasted_iota(jnp.int32, (8, 128), 0) < 4

    def lengths_at(first, count, group, at):
        parts = []
        for g in range(3):
            out = None
            for u in range(count):
                device = first + u
                tile = zed[lax.rem(device, 2), device // 2, Z_L:Z_ROWS]
                tile = shift_lanes(tile, at + 8 * u - 8 * group - 32 * g)
                out = tile if out is None else jnp.where(lanes(8) // 8 >= at // 8 + u, tile, out)
            parts.append(out)
        return jnp.concatenate([jnp.where(upper, parts[0], pltpu.roll(parts[1], 4, 0)), parts[2]], 0)

    lane_len[0] = lengths_at(0, 16, 0, 0)
    lane_len[1] = lengths_at(16, 16, 0, 0)
    lane_len[2] = jnp.where(
        lanes(16) < 32,
        lengths_at(lax.rem(p, 8) * 4, 4, 2, 0),
        lengths_at(lax.rem(q, 8) * 4, 4, 3, 32),
    )
    square = jnp.concatenate([lengths_at(16 * core, 16, 1, 0), lane_len[2], jnp.zeros((96, 128), F32)], 0)
    turned[...] = square.T
    rt[:, 0:64] = rows[...].T

    for i, pivot in enumerate((p, q)):
        for n in range(HOLDERS):
            holder = 4 * (pivot // 32) + n // 2
            at = 32 * i + 4 * n
            part = zed[n % 2, holder, 8 * i : 8 * i + 8]
            ct[at : at + 4, 0:128] = part[0:4]
            ct[at : at + 4, 128:256] = part[4:8]
            kt[at : at + 4, :] = shift_lanes(zed[n % 2, holder, Z_L:Z_ROWS], 64 * i)[4:8]

    lane = lanes(8)
    sub = lax.broadcasted_iota(jnp.int32, (8, 128), 0)
    vertex = [
        (256 * row + lane).astype(F32),
        (256 * row + 128 + lane).astype(F32),
        jnp.where(lane < 32, 32 * p + lane, jnp.where(lane < 64, 32 * q + lane - 32, -1)).astype(F32),
    ]

    def relax(entries, vertices, tile, base):
        own = (base + sub).astype(F32)
        at, shift = 8 * (tile % 16), 16 * (tile // 16)
        turn = turned[at : at + 8, :]
        entries = list(entries)
        for k in range(NEIGHBORS):
            own_ids = sub_ids[tile, k]
            own_len = jnp.broadcast_to(turn[:, shift + k : shift + k + 1], (8, 128))
            for n, kind in enumerate(vertices):
                there = jnp.where(own_ids == vertex[kind], own_len, INF)
                back = jnp.where(lane_ids[kind, k : k + 1, :] == own, lane_len[kind, k : k + 1, :], INF)
                entries[n] = jnp.minimum(entries[n], jnp.minimum(there, back))
        return [jnp.where(own == vertex[kind], 0.0, e) for kind, e in zip(vertices, entries)]

    state = [[], [], []]
    for tile in range(8):
        at = 8 * tile
        base = (32 * p + at) if tile < 4 else (32 * q + at - 32)
        done = relax(
            [ct[at : at + 8, 0:128], ct[at : at + 8, 128:256], kt[at : at + 8, :]], (0, 1, 2), 16 + tile, base
        )
        for kind in range(3):
            state[kind].append(done[kind])
    for b in range(8):
        eliminate(state, b)
        if b < 4:
            for tile in range(4 * b, 4 * b + 4):
                at = 8 * tile
                entries = [mt[at : at + 8, 0:128], mt[at : at + 8, 128:256], rt[at : at + 8, :]]
                entries = relax(entries, (0, 1, 2), tile, 128 * col + at)
                new[at : at + 8, 0:128] = entries[0]
                new[at : at + 8, 128:256] = entries[1]
                rt[at : at + 8, :] = entries[2]
        else:
            if b == 4:
                parts = thirds(rt[...])
            for c in range(4):
                at = 2048 * (b - 4) + 512 * c
                spread[:, at : at + 512] = jnp.dot(
                    parts[b - 4], onehot[:, 512 * c : 512 * c + 512], preferred_element_type=F32
                )
    for tile in range(8):
        at = 8 * tile
        ct[at : at + 8, 0:128] = state[0][tile]
        ct[at : at + 8, 128:256] = state[1][tile]

    def body(i, carry):
        at = pl.multiple_of(32 * i, 32)
        for half in (0, 128):
            here = new[pl.ds(at, 32), half : half + 128]
            for t in range(2 * PIVOT):
                here = jnp.minimum(here, spread[pl.ds(at, 32), 128 * t : 128 * t + 128] + ct[t : t + 1, half : half + 128])
            new[pl.ds(at, 32), half : half + 128] = here
        return carry

    lax.fori_loop(0, COLS // 32, body, 0)
    for h in range(2):
        out[128 * h : 128 * h + 128, :] = new[:, 128 * h : 128 * h + 128].T


VM = pl.BlockSpec(memory_space=pltpu.VMEM)
SM = pl.BlockSpec(memory_space=pltpu.SMEM)
HBM = pl.BlockSpec(memory_space=pltpu.HBM)
MIB = 1024 * 1024


def call(kernel, shapes, scratch, ins, mib, outs=None):
    return pl.pallas_call(
        kernel,
        out_shape=[s if isinstance(s, jax.ShapeDtypeStruct) else jax.ShapeDtypeStruct(s, F32) for s in shapes],
        in_specs=ins,
        out_specs=outs or [VM] * len(shapes),
        scratch_shapes=[pltpu.VMEM(s, F32) if isinstance(s, tuple) else s for s in scratch],
        compiler_params=pltpu.CompilerParams(vmem_limit_bytes=mib * MIB),
    )


FINAL_SCRATCH = [(3, 16, 128), (128, 128), (64, 256), (64, 128), (128, 128), (128, 8192), (128, 256)]
ONEHOT = jax.ShapeDtypeStruct((64, 16 * 128), jnp.bfloat16)
PIVOTS = jax.ShapeDtypeStruct((2,), jnp.int32)


def on_device(distances, neighbor_ids, edge_lengths, pivots):
    piv, mt, scatter, panel, own_lengths = call(
        pack_kernel,
        [PIVOTS, (COLS, ROWS), (HOLDERS, 16, 128), (64, 128), (8, 128)],
        [(ROWS, COLS), (8, NEIGHBORS), pltpu.SemaphoreType.DMA((3,))],
        [HBM] * 3,
        8,
        [SM] + [VM] * 4,
    )(*[pltpu.with_memory_space_constraint(x, pltpu.HBM) for x in (pivots, distances, edge_lengths.T)])
    scatter = lax.all_to_all(scatter, ("zl", "core"), 0, 0)
    xy, piece = call(spread_kernel, [(NXY, XY_ROWS, 128), (16, 128)], [], [SM] + [VM] * 3, 8)(
        piv, scatter, own_lengths, panel
    )
    lane_ids, sub_ids, onehot = call(
        ids_kernel, [(3, 16, 128), (24, NEIGHBORS, 8, 128), ONEHOT], [(128, 128)], [SM, VM], 16
    )(piv, neighbor_ids)
    xy = lax.all_to_all(xy, "row", 0, 0)
    zed, rows = call(gather_kernel, [(NZ, Z_ROWS, 128), (64, 128)], [(128, 128)], [SM] + [VM] * 2, 8)(piv, xy, piece)
    zed = lax.all_to_all(zed, ("zh", "zl"), 0, 0)
    zed = lax.all_gather(zed, "core")
    (out,) = call(final_kernel, [(ROWS, COLS)], FINAL_SCRATCH, [SM] + [VM] * 6, 24)(
        piv, mt, rows, zed, lane_ids, sub_ids, onehot
    )
    return out


def solution(mesh):
    fine = Mesh(mesh.devices.reshape(16, 4, 4, 2), ("row", "zh", "zl", "core"))
    cols = ("zh", "zl", "core")
    placed = (P("row", cols), P(), P(None, ("row", *cols)), P())
    return jax.shard_map(on_device, mesh=fine, in_specs=placed, out_specs=P("row", cols), check_vma=False)
```

```python
import jax
import jax.numpy as jnp
from jax import lax
from jax.experimental import pallas as pl
from jax.experimental.pallas import tpu as pltpu
from jax.sharding import Mesh, PartitionSpec as P

NEIGHBORS = 10
PIVOT = 32
ROWS = 256
COLS = 128
NXY = 16
NZ = 16
F32 = jnp.float32
INF = float("inf")

XY_L, XY_P, XY_Q, XY_ROWS = 8, 16, 32, 48
Z_L, Z_ROWS = 8, 16
HOLDERS = 8


def lanes(rows):
    return lax.broadcasted_iota(jnp.int32, (rows, 128), 1)


def shift_lanes(x, amount):
    if isinstance(amount, int):
        return pltpu.roll(x, amount % 128, 1) if amount % 128 else x
    return pltpu.roll(x, lax.rem(amount + 1024, 128), 1)


def place():
    return lax.axis_index("row"), 4 * lax.axis_index("zh") + lax.axis_index("zl"), lax.axis_index("core")


def pack_kernel(pivots, dist, lengths, piv, mt, scatter, panel, own_lengths, block, held, sems):
    row, _, _ = place()
    copies = [
        pltpu.make_async_copy(dist, block, sems.at[0]),
        pltpu.make_async_copy(lengths, held, sems.at[1]),
        pltpu.make_async_copy(pivots, piv, sems.at[2]),
    ]
    for copy in copies:
        copy.start()
    for copy in copies:
        copy.wait()
    for h in range(2):
        mt[:, 128 * h : 128 * h + 128] = block[128 * h : 128 * h + 128, :].T
    for i in range(2):
        off = lax.rem(piv[i], 4) * PIVOT
        for n in range(0, HOLDERS, 2):
            lines = mt[pl.ds(pl.multiple_of(off + 4 * n, 8), 8), :]
            for m in range(2):
                for h in range(2):
                    at = 8 * i + 4 * h
                    scatter[n + m, at : at + 4, :] = lines[4 * m : 4 * m + 4, 128 * h : 128 * h + 128]
        panel[32 * i : 32 * i + 32, :] = block[pl.ds(pl.multiple_of(lax.rem(piv[i], 8) * PIVOT, 32), 32), :]
    spaced = jnp.concatenate([held[...], jnp.zeros((8, 128 - NEIGHBORS), F32)], 1)
    own_lengths[...] = shift_lanes(spaced, 16 * lax.rem(row, 8))


def spread_kernel(piv, got, own_lengths, panel, other_panel, xy, keep, send):
    p, q = piv[0], piv[1]
    row, z, _ = place()
    corner, halves = None, [[], []]
    for i, pivot in enumerate((p, q)):
        holder = lax.rem(pivot // 8, 4) * 2 + lax.rem(pivot // 4, 2)
        mine = got[holder, 8 * i : 8 * i + 8]
        for b in range(2):
            halves[b] += [mine[2 * b : 2 * b + 2], mine[4 + 2 * b : 6 + 2 * b]]
        for j, other in enumerate((p, q)):
            half = jnp.where(lax.rem(other // 4, 2) == 0, mine, pltpu.roll(mine, 4, 0))
            half = shift_lanes(half, 64 * i + 32 * j - lax.rem(other, 4) * PIVOT)
            corner = half if corner is None else jnp.where(lanes(8) // PIVOT == 2 * i + j, half, corner)
    first, second = [jnp.concatenate(parts, 0) for parts in halves]
    even = lax.rem(z // 4, 2) == 0
    keep[...] = jnp.where(even, first, second)
    send[...] = jnp.where(even, second, first)
    corner = pltpu.roll(corner, 4, 0)
    part = pl.multiple_of(16 * lax.rem(row, 2), 16)
    lines = [
        jnp.where(
            lax.rem(pivot // 8 + row, 2) == 0,
            panel[pl.ds(32 * i + part, 16), :],
            other_panel[pl.ds(32 * i + part, 16), :],
        )
        for i, pivot in enumerate((p, q))
    ]
    for d in range(NXY):
        xy[d, 0:XY_L] = corner
        xy[d, XY_L:XY_P] = own_lengths[...]
        xy[d, XY_P:XY_Q] = lines[0]
        xy[d, XY_Q:XY_ROWS] = lines[1]


def gather_kernel(piv, xy, keep, other, zchunk, rows, turned):
    p, q = piv[0], piv[1]
    row, z, _ = place()
    row_p, row_q = p // 8, q // 8
    for b in range(2):
        rows[16 * b : 16 * b + 16] = xy[row_p // 2 * 2 + b, XY_P:XY_Q]
        rows[32 + 16 * b : 48 + 16 * b] = xy[row_q // 2 * 2 + b, XY_Q:XY_ROWS]
    upper = lax.broadcasted_iota(jnp.int32, (8, 128), 0) < 4
    piece = jnp.where(
        upper,
        jnp.where(p // 32 == z // 4, keep[...], other[...]),
        jnp.where(q // 32 == z // 4, keep[...], other[...]),
    )
    corner = jnp.where(lax.rem(lanes(8) // PIVOT, 2) == 0, xy[row_p, 0:XY_L], xy[row_q, 0:XY_L])
    low = xy[0, XY_L:XY_P]
    high = xy[8, XY_L:XY_P]
    for d in range(1, 8):
        low = jnp.maximum(low, xy[d, XY_L:XY_P])
        high = jnp.maximum(high, xy[8 + d, XY_L:XY_P])
    turned[...] = jnp.concatenate([low, high, jnp.zeros((112, 128), F32)], 0).T
    group = lanes(8) // 8

    def take(device, at, lengths):
        start = 16 * (device % 8)
        from_lane = 8 * (device // 8)
        first = turned[pl.ds(pl.multiple_of(start, 8), 8), :]
        second = turned[pl.ds(pl.multiple_of(start + 8, 8), 8), :]
        for g, part in ((0, first), (1, pltpu.roll(first, 4, 0)), (2, second)):
            moved = shift_lanes(part, 32 * g + 8 * at - from_lane)
            lengths = moved if lengths is None else jnp.where(group == 4 * g + at, moved, lengths)
        return lengths

    fixed = take(row_q, 3, take(row_p, 2, take(row, 0, None)))
    for d in range(NZ):
        zchunk[d, 0:Z_L] = piece
        zchunk[d, Z_L:Z_ROWS] = jnp.where(upper, take(d, 1, fixed), corner)


def ids_kernel(piv, ids, lane_ids, sub_ids, onehot, held):
    p, q = piv[0], piv[1]
    row, z, core = place()
    col = 2 * z + core

    def block(base):
        x = ids[:, pl.ds(pl.multiple_of(base, 128), 128)].astype(F32)
        return jnp.concatenate([x, jnp.zeros((6, 128), F32)], 0)

    for h in range(2):
        lane_ids[h] = block(256 * row + 128 * h)
    pivot_p = shift_lanes(block(p // 4 * 128), 0 - lax.rem(p, 4) * PIVOT)
    pivot_q = shift_lanes(block(q // 4 * 128), 32 - lax.rem(q, 4) * PIVOT)
    pivots = jnp.where(lanes(16) < 32, pivot_p, pivot_q)
    lane_ids[2] = pivots
    held[...] = jnp.zeros_like(held)
    held[0:16] = block(128 * col)
    held[16:32] = pivots
    turned = held[...].T
    for tile in range(24):
        at = 8 * (tile % 16)
        for k in range(NEIGHBORS):
            lane = 16 * (tile // 16) + k
            sub_ids[tile, k] = jnp.broadcast_to(turned[at : at + 8, lane : lane + 1], (8, 128))
    term = lax.broadcasted_iota(jnp.int32, (64, 128), 0)
    for t in range(16):
        picked = (lax.rem(term, 16) == t) & (term < 48)
        onehot[:, 128 * t : 128 * t + 128] = jnp.where(picked, 1.0, 0.0).astype(jnp.bfloat16)


def over_lanes(x, lane):
    return jnp.broadcast_to(x[:, lane : lane + 1], (8, 128))


def over_rows(x, row):
    return jnp.broadcast_to(x[row : row + 1, :], (8, 128))


def eliminate(state, b):
    corner = state[2]
    columns = [over_lanes(corner[b], 8 * b + j) for j in range(8)]
    rows = [state[kind][b] for kind in range(3)]
    for j in range(8):
        for u in range(j + 1, 8):
            columns[u] = jnp.minimum(columns[u], columns[j] + over_rows(columns[u], j))
        rows = [jnp.minimum(r, columns[j] + over_rows(r, j)) for r in rows]
    closed = [[over_rows(r, j) for j in range(8)] for r in rows]
    for i in range(8):
        if i == b:
            continue
        columns = [over_lanes(corner[i], 8 * b + j) for j in range(8)]
        for kind in range(3):
            paths = [columns[j] + closed[kind][j] for j in range(8)]
            while len(paths) > 1:
                paths = [jnp.minimum(paths[n], paths[n + 1]) for n in range(0, len(paths), 2)]
            state[kind][i] = jnp.minimum(state[kind][i], paths[0])
    for kind in range(3):
        state[kind][b] = rows[kind]


def thirds(x):
    high = x.astype(jnp.bfloat16)
    rest = x - high.astype(F32)
    mid = rest.astype(jnp.bfloat16)
    low = (rest - mid.astype(F32)).astype(jnp.bfloat16)
    return [
        jnp.concatenate([term[:, 16 * n : 16 * n + 16] for term in (high, mid, low, low)], 1) for n in range(4)
    ]


def final_kernel(piv, mt, rows, zed, lane_ids, sub_ids, onehot, out, lane_len, turned, ct, kt, rt, spread, new):
    p, q = piv[0], piv[1]
    row, z, core = place()
    col = 2 * z + core
    upper = lax.broadcasted_iota(jnp.int32, (8, 128), 0) < 4

    def lengths_at(first, count, group, at):
        parts = []
        for g in range(3):
            out = None
            for u in range(count):
                device = first + u
                tile = zed[lax.rem(device, 2), device // 2, Z_L:Z_ROWS]
                tile = shift_lanes(tile, at + 8 * u - 8 * group - 32 * g)
                out = tile if out is None else jnp.where(lanes(8) // 8 >= at // 8 + u, tile, out)
            parts.append(out)
        return jnp.concatenate([jnp.where(upper, parts[0], pltpu.roll(parts[1], 4, 0)), parts[2]], 0)

    lane_len[0] = lengths_at(0, 16, 0, 0)
    lane_len[1] = lengths_at(16, 16, 0, 0)
    lane_len[2] = jnp.where(
        lanes(16) < 32,
        lengths_at(lax.rem(p, 8) * 4, 4, 2, 0),
        lengths_at(lax.rem(q, 8) * 4, 4, 3, 32),
    )
    square = jnp.concatenate([lengths_at(16 * core, 16, 1, 0), lane_len[2], jnp.zeros((96, 128), F32)], 0)
    turned[...] = square.T
    rt[:, 0:64] = rows[...].T

    for i, pivot in enumerate((p, q)):
        for n in range(HOLDERS):
            at = 32 * i + 4 * n
            group = pivot // 32
            for b in range(2):
                part = zed[n % 2, 4 * (group // 2 * 2 + b) + n // 2, 0:Z_L]
                ct[at + 2 * b : at + 2 * b + 2, 0:128] = part[4 * i : 4 * i + 2]
                ct[at + 2 * b : at + 2 * b + 2, 128:256] = part[4 * i + 2 : 4 * i + 4]
            kt[at : at + 4, :] = shift_lanes(zed[n % 2, 4 * group + n // 2, Z_L:Z_ROWS], 64 * i)[4:8]

    lane = lanes(8)
    sub = lax.broadcasted_iota(jnp.int32, (8, 128), 0)
    vertex = [
        (256 * row + lane).astype(F32),
        (256 * row + 128 + lane).astype(F32),
        jnp.where(lane < 32, 32 * p + lane, jnp.where(lane < 64, 32 * q + lane - 32, -1)).astype(F32),
    ]

    def relax(entries, vertices, tile, base):
        own = (base + sub).astype(F32)
        at, shift = 8 * (tile % 16), 16 * (tile // 16)
        turn = turned[at : at + 8, :]
        entries = list(entries)
        for k in range(NEIGHBORS):
            own_ids = sub_ids[tile, k]
            own_len = jnp.broadcast_to(turn[:, shift + k : shift + k + 1], (8, 128))
            for n, kind in enumerate(vertices):
                there = jnp.where(own_ids == vertex[kind], own_len, INF)
                back = jnp.where(lane_ids[kind, k : k + 1, :] == own, lane_len[kind, k : k + 1, :], INF)
                entries[n] = jnp.minimum(entries[n], jnp.minimum(there, back))
        return [jnp.where(own == vertex[kind], 0.0, e) for kind, e in zip(vertices, entries)]

    state = [[], [], []]
    for tile in range(8):
        at = 8 * tile
        base = (32 * p + at) if tile < 4 else (32 * q + at - 32)
        done = relax(
            [ct[at : at + 8, 0:128], ct[at : at + 8, 128:256], kt[at : at + 8, :]], (0, 1, 2), 16 + tile, base
        )
        for kind in range(3):
            state[kind].append(done[kind])
    for b in range(8):
        eliminate(state, b)
        if b < 4:
            for tile in range(4 * b, 4 * b + 4):
                at = 8 * tile
                entries = [mt[at : at + 8, 0:128], mt[at : at + 8, 128:256], rt[at : at + 8, :]]
                entries = relax(entries, (0, 1, 2), tile, 128 * col + at)
                new[at : at + 8, 0:128] = entries[0]
                new[at : at + 8, 128:256] = entries[1]
                rt[at : at + 8, :] = entries[2]
        else:
            if b == 4:
                parts = thirds(rt[...])
            for c in range(4):
                at = 2048 * (b - 4) + 512 * c
                spread[:, at : at + 512] = jnp.dot(
                    parts[b - 4], onehot[:, 512 * c : 512 * c + 512], preferred_element_type=F32
                )
    for tile in range(8):
        at = 8 * tile
        ct[at : at + 8, 0:128] = state[0][tile]
        ct[at : at + 8, 128:256] = state[1][tile]

    def body(i, carry):
        at = pl.multiple_of(32 * i, 32)
        for half in (0, 128):
            here = new[pl.ds(at, 32), half : half + 128]
            for t in range(2 * PIVOT):
                here = jnp.minimum(here, spread[pl.ds(at, 32), 128 * t : 128 * t + 128] + ct[t : t + 1, half : half + 128])
            new[pl.ds(at, 32), half : half + 128] = here
        return carry

    lax.fori_loop(0, COLS // 32, body, 0)
    for h in range(2):
        out[128 * h : 128 * h + 128, :] = new[:, 128 * h : 128 * h + 128].T


VM = pl.BlockSpec(memory_space=pltpu.VMEM)
SM = pl.BlockSpec(memory_space=pltpu.SMEM)
HBM = pl.BlockSpec(memory_space=pltpu.HBM)
MIB = 1024 * 1024


def call(kernel, shapes, scratch, ins, mib, outs=None):
    return pl.pallas_call(
        kernel,
        out_shape=[s if isinstance(s, jax.ShapeDtypeStruct) else jax.ShapeDtypeStruct(s, F32) for s in shapes],
        in_specs=ins,
        out_specs=outs or [VM] * len(shapes),
        scratch_shapes=[pltpu.VMEM(s, F32) if isinstance(s, tuple) else s for s in scratch],
        compiler_params=pltpu.CompilerParams(vmem_limit_bytes=mib * MIB),
    )


FINAL_SCRATCH = [(3, 16, 128), (128, 128), (64, 256), (64, 128), (128, 128), (128, 8192), (128, 256)]
ONEHOT = jax.ShapeDtypeStruct((64, 16 * 128), jnp.bfloat16)
PIVOTS = jax.ShapeDtypeStruct((2,), jnp.int32)


def on_device(distances, neighbor_ids, edge_lengths, pivots):
    piv, mt, scatter, panel, own_lengths = call(
        pack_kernel,
        [PIVOTS, (COLS, ROWS), (HOLDERS, 16, 128), (64, 128), (8, 128)],
        [(ROWS, COLS), (8, NEIGHBORS), pltpu.SemaphoreType.DMA((3,))],
        [HBM] * 3,
        8,
        [SM] + [VM] * 4,
    )(*[pltpu.with_memory_space_constraint(x, pltpu.HBM) for x in (pivots, distances, edge_lengths.T)])
    other_panel = lax.ppermute(panel, "row", [(i, i ^ 1) for i in range(NXY)])
    scatter = lax.all_to_all(scatter, ("zl", "core"), 0, 0)
    xy, keep, send = call(spread_kernel, [(NXY, XY_ROWS, 128), (8, 128), (8, 128)], [], [SM] + [VM] * 4, 8)(
        piv, scatter, own_lengths, panel, other_panel
    )
    other_half = lax.ppermute(send, "zh", [(i, i ^ 1) for i in range(4)])
    lane_ids, sub_ids, onehot = call(
        ids_kernel, [(3, 16, 128), (24, NEIGHBORS, 8, 128), ONEHOT], [(128, 128)], [SM, VM], 16
    )(piv, neighbor_ids)
    xy = lax.all_to_all(xy, "row", 0, 0)
    zed, rows = call(gather_kernel, [(NZ, Z_ROWS, 128), (64, 128)], [(128, 128)], [SM] + [VM] * 3, 8)(
        piv, xy, keep, other_half
    )
    zed = lax.all_to_all(zed, ("zh", "zl"), 0, 0)
    zed = lax.all_gather(zed, "core")
    (out,) = call(final_kernel, [(ROWS, COLS)], FINAL_SCRATCH, [SM] + [VM] * 6, 24)(
        piv, mt, rows, zed, lane_ids, sub_ids, onehot
    )
    return out


def solution(mesh):
    fine = Mesh(mesh.devices.reshape(16, 4, 4, 2), ("row", "zh", "zl", "core"))
    cols = ("zh", "zl", "core")
    placed = (P("row", cols), P(), P(None, ("row", *cols)), P())
    return jax.shard_map(on_device, mesh=fine, in_specs=placed, out_specs=P("row", cols), check_vma=False)
```

```python
import jax
import jax.numpy as jnp
from jax import lax
from jax.experimental import pallas as pl
from jax.experimental.pallas import tpu as pltpu
from jax.sharding import Mesh, PartitionSpec as P

NEIGHBORS = 10
PIVOT = 32
ROWS = 256
COLS = 128
NXY = 16
NZ = 16
F32 = jnp.float32
INF = float("inf")

XY_P, XY_Q, XY_ROWS = 8, 24, 40
Z_L, Z_ROWS = 8, 16
HOLDERS = 8


def lanes(rows):
    return lax.broadcasted_iota(jnp.int32, (rows, 128), 1)


def shift_lanes(x, amount):
    if isinstance(amount, int):
        return pltpu.roll(x, amount % 128, 1) if amount % 128 else x
    return pltpu.roll(x, lax.rem(amount + 1024, 128), 1)


def place():
    z = 0
    for bit in ("z3", "z2", "z1", "z0"):
        z = 2 * z + lax.axis_index(bit)
    return lax.axis_index("row"), z, lax.axis_index("core")


def upper_half():
    return lax.broadcasted_iota(jnp.int32, (8, 128), 0) < 4


def pack_kernel(pivots, dist, lengths, piv, mt, scatter, panel, own_lengths, block, held, sems):
    copies = [
        pltpu.make_async_copy(dist, block, sems.at[0]),
        pltpu.make_async_copy(lengths, held, sems.at[1]),
        pltpu.make_async_copy(pivots, piv, sems.at[2]),
    ]
    for copy in copies:
        copy.start()
    for copy in copies:
        copy.wait()
    for h in range(2):
        mt[:, 128 * h : 128 * h + 128] = block[128 * h : 128 * h + 128, :].T
    for i in range(2):
        off = lax.rem(piv[i], 4) * PIVOT
        for n in range(0, HOLDERS, 2):
            lines = mt[pl.ds(pl.multiple_of(off + 4 * n, 8), 8), :]
            for m in range(2):
                for h in range(2):
                    at = 8 * i + 4 * h
                    scatter[n + m, at : at + 4, :] = lines[4 * m : 4 * m + 4, 128 * h : 128 * h + 128]
        panel[32 * i : 32 * i + 32, :] = block[pl.ds(pl.multiple_of(lax.rem(piv[i], 8) * PIVOT, 32), 32), :]
    spaced = jnp.concatenate([held[...], jnp.zeros((8, 128 - NEIGHBORS), F32)], 1)
    lines = jnp.concatenate([spaced, jnp.zeros((120, 128), F32)], 0).T
    low, high = lines[0:8], lines[8:16]
    own_lengths[...] = low + shift_lanes(pltpu.roll(low, 4, 0), 32) + shift_lanes(high, 64)


def spread_kernel(piv, got, own_lengths, panel, other_panel, xy, keep, send):
    p, q = piv[0], piv[1]
    row, z, _ = place()
    corner, halves = None, [[], []]
    for i, pivot in enumerate((p, q)):
        holder = lax.rem(pivot // 32, 2) * 4 + lax.rem(pivot // 8, 2) * 2 + lax.rem(pivot // 4, 2)
        mine = got[holder, 8 * i : 8 * i + 8]
        for b in range(2):
            halves[b] += [mine[2 * b : 2 * b + 2], mine[4 + 2 * b : 6 + 2 * b]]
        for j, other in enumerate((p, q)):
            half = jnp.where(lax.rem(other // 4, 2) == 0, mine, pltpu.roll(mine, 4, 0))
            half = shift_lanes(half, 64 * i + 32 * j - lax.rem(other, 4) * PIVOT)
            corner = half if corner is None else jnp.where(lanes(8) // PIVOT == 2 * i + j, half, corner)
    first, second = [jnp.concatenate(parts, 0) for parts in halves]
    even = lax.rem(z // 2, 2) == 0
    keep[...] = jnp.where(even, first, second)
    send[...] = jnp.where(even, second, first)
    small = jnp.where(upper_half(), own_lengths[...], pltpu.roll(corner, 4, 0))
    part = pl.multiple_of(16 * lax.rem(row, 2), 16)
    lines = [
        jnp.where(
            lax.rem(pivot // 8 + row, 2) == 0,
            panel[pl.ds(32 * i + part, 16), :],
            other_panel[pl.ds(32 * i + part, 16), :],
        )
        for i, pivot in enumerate((p, q))
    ]
    for d in range(NXY):
        xy[d, 0:XY_P] = small
        xy[d, XY_P:XY_Q] = lines[0]
        xy[d, XY_Q:XY_ROWS] = lines[1]


def gather_kernel(piv, xy, keep, other, zchunk, rows):
    p, q = piv[0], piv[1]
    row, z, core = place()
    row_p, row_q = p // 8, q // 8
    for b in range(2):
        rows[16 * b : 16 * b + 16] = xy[row_p // 2 * 2 + b, XY_P:XY_Q]
        rows[32 + 16 * b : 48 + 16 * b] = xy[row_q // 2 * 2 + b, XY_Q:XY_ROWS]
    upper = upper_half()
    bit = lax.rem(z // 2, 2)
    piece = jnp.where(
        upper,
        jnp.where(lax.rem(p // 16, 2) == bit, keep[...], other[...]),
        jnp.where(lax.rem(q // 16, 2) == bit, keep[...], other[...]),
    )
    corner = jnp.where(lax.rem(lanes(8) // PIVOT, 2) == 0, xy[row_p, 0:XY_P], xy[row_q, 0:XY_P])
    turn = 2 * lax.rem(z, 2) + core

    def take(device, at):
        return shift_lanes(xy[device, 0:XY_P], 8 * lax.rem(turn + at, 4))

    fixed = take(row, 0) + take(row_p, 2) + take(row_q, 3)
    for d in range(NZ):
        zchunk[d, 0:Z_L] = piece
        zchunk[d, Z_L:Z_ROWS] = jnp.where(upper, fixed + take(d, 1), corner)


def ids_kernel(piv, ids, lane_ids, sub_ids, onehot, held):
    p, q = piv[0], piv[1]
    row, z, core = place()
    col = 2 * z + core

    def block(base):
        x = ids[:, pl.ds(pl.multiple_of(base, 128), 128)].astype(F32)
        return jnp.concatenate([x, jnp.zeros((6, 128), F32)], 0)

    for h in range(2):
        lane_ids[h] = block(256 * row + 128 * h)
    pivot_p = shift_lanes(block(p // 4 * 128), 0 - lax.rem(p, 4) * PIVOT)
    pivot_q = shift_lanes(block(q // 4 * 128), 32 - lax.rem(q, 4) * PIVOT)
    pivots = jnp.where(lanes(16) < 32, pivot_p, pivot_q)
    lane_ids[2] = pivots
    held[...] = jnp.zeros_like(held)
    held[0:16] = block(128 * col)
    held[16:32] = pivots
    turned = held[...].T
    for tile in range(24):
        at = 8 * (tile % 16)
        for k in range(NEIGHBORS):
            lane = 16 * (tile // 16) + k
            sub_ids[tile, k] = jnp.broadcast_to(turned[at : at + 8, lane : lane + 1], (8, 128))
    term = lax.broadcasted_iota(jnp.int32, (64, 128), 0)
    for t in range(16):
        picked = (lax.rem(term, 16) == t) & (term < 48)
        onehot[:, 128 * t : 128 * t + 128] = jnp.where(picked, 1.0, 0.0).astype(jnp.bfloat16)


def over_lanes(x, lane):
    return jnp.broadcast_to(x[:, lane : lane + 1], (8, 128))


def over_rows(x, row):
    return jnp.broadcast_to(x[row : row + 1, :], (8, 128))


def eliminate(state, b):
    corner = state[2]
    columns = [over_lanes(corner[b], 8 * b + j) for j in range(8)]
    rows = [state[kind][b] for kind in range(3)]
    for j in range(8):
        for u in range(j + 1, 8):
            columns[u] = jnp.minimum(columns[u], columns[j] + over_rows(columns[u], j))
        rows = [jnp.minimum(r, columns[j] + over_rows(r, j)) for r in rows]
    closed = [[over_rows(r, j) for j in range(8)] for r in rows]
    for i in range(8):
        if i == b:
            continue
        columns = [over_lanes(corner[i], 8 * b + j) for j in range(8)]
        for kind in range(3):
            paths = [columns[j] + closed[kind][j] for j in range(8)]
            while len(paths) > 1:
                paths = [jnp.minimum(paths[n], paths[n + 1]) for n in range(0, len(paths), 2)]
            state[kind][i] = jnp.minimum(state[kind][i], paths[0])
    for kind in range(3):
        state[kind][b] = rows[kind]


def thirds(x):
    high = x.astype(jnp.bfloat16)
    rest = x - high.astype(F32)
    mid = rest.astype(jnp.bfloat16)
    low = (rest - mid.astype(F32)).astype(jnp.bfloat16)
    return [
        jnp.concatenate([term[:, 16 * n : 16 * n + 16] for term in (high, mid, low, low)], 1) for n in range(4)
    ]


def final_kernel(piv, mt, rows, zed, lane_ids, sub_ids, onehot, out, lane_len, turned, ct, kt, rt, spread, new):
    p, q = piv[0], piv[1]
    row, z, core = place()
    col = 2 * z + core
    slot = lax.rem(lanes(8) // 8, 4)

    def lengths_at(first, count, at):
        parts = [None] * 3
        for v in range(count):
            merged = None
            for w in range(4):
                device = first + 4 * v + w
                tile = zed[w % 2, device // 2, Z_L:Z_ROWS]
                merged = tile if w == 0 else jnp.where(slot == (at + w) % 4, tile, merged)
            for g in range(3):
                moved = shift_lanes(merged, 32 * (v - g))
                parts[g] = moved if v == 0 else jnp.where(lanes(8) // 32 >= v, moved, parts[g])
        both = [jnp.where(upper_half(), parts[0], pltpu.roll(parts[1], 4, 0)), parts[2]]
        if at:
            both = [
                jnp.where(slot < 4 - at, shift_lanes(part, -8 * at), shift_lanes(part, 32 - 8 * at)) for part in both
            ]
        return jnp.concatenate(both, 0)

    lane_len[0] = lengths_at(0, 4, 0)
    lane_len[1] = lengths_at(16, 4, 0)
    lane_len[2] = jnp.where(
        lanes(16) < 32,
        lengths_at(lax.rem(p, 8) * 4, 1, 2),
        shift_lanes(lengths_at(lax.rem(q, 8) * 4, 1, 3), 32),
    )
    square = jnp.concatenate([lengths_at(16 * core, 4, 1), lane_len[2], jnp.zeros((96, 128), F32)], 0)
    turned[...] = square.T
    rt[:, 0:64] = rows[...].T

    for i, pivot in enumerate((p, q)):
        home = pivot // 64 * 8
        for n in range(HOLDERS):
            at = 32 * i + 4 * n
            base = home + 4 * (n // 4) + n // 2 % 2
            for b in range(2):
                part = zed[n % 2, base + 2 * b, 0:Z_L]
                ct[at + 2 * b : at + 2 * b + 2, 0:128] = part[4 * i : 4 * i + 2]
                ct[at + 2 * b : at + 2 * b + 2, 128:256] = part[4 * i + 2 : 4 * i + 4]
            corner = zed[n % 2, base + 2 * lax.rem(pivot // 16, 2), Z_L:Z_ROWS]
            kt[at : at + 4, :] = shift_lanes(corner, 64 * i)[4:8]

    lane = lanes(8)
    sub = lax.broadcasted_iota(jnp.int32, (8, 128), 0)
    vertex = [
        (256 * row + lane).astype(F32),
        (256 * row + 128 + lane).astype(F32),
        jnp.where(lane < 32, 32 * p + lane, jnp.where(lane < 64, 32 * q + lane - 32, -1)).astype(F32),
    ]

    def relax(entries, vertices, tile, base):
        own = (base + sub).astype(F32)
        at, shift = 8 * (tile % 16), 16 * (tile // 16)
        turn = turned[at : at + 8, :]
        entries = list(entries)
        for k in range(NEIGHBORS):
            own_ids = sub_ids[tile, k]
            own_len = jnp.broadcast_to(turn[:, shift + k : shift + k + 1], (8, 128))
            for n, kind in enumerate(vertices):
                there = jnp.where(own_ids == vertex[kind], own_len, INF)
                back = jnp.where(lane_ids[kind, k : k + 1, :] == own, lane_len[kind, k : k + 1, :], INF)
                entries[n] = jnp.minimum(entries[n], jnp.minimum(there, back))
        return [jnp.where(own == vertex[kind], 0.0, e) for kind, e in zip(vertices, entries)]

    state = [[], [], []]
    for tile in range(8):
        at = 8 * tile
        base = (32 * p + at) if tile < 4 else (32 * q + at - 32)
        done = relax(
            [ct[at : at + 8, 0:128], ct[at : at + 8, 128:256], kt[at : at + 8, :]], (0, 1, 2), 16 + tile, base
        )
        for kind in range(3):
            state[kind].append(done[kind])
    for b in range(8):
        eliminate(state, b)
        if b < 4:
            for tile in range(4 * b, 4 * b + 4):
                at = 8 * tile
                entries = [mt[at : at + 8, 0:128], mt[at : at + 8, 128:256], rt[at : at + 8, :]]
                entries = relax(entries, (0, 1, 2), tile, 128 * col + at)
                new[at : at + 8, 0:128] = entries[0]
                new[at : at + 8, 128:256] = entries[1]
                rt[at : at + 8, :] = entries[2]
        else:
            if b == 4:
                parts = thirds(rt[...])
            for c in range(4):
                at = 2048 * (b - 4) + 512 * c
                spread[:, at : at + 512] = jnp.dot(
                    parts[b - 4], onehot[:, 512 * c : 512 * c + 512], preferred_element_type=F32
                )
    for tile in range(8):
        at = 8 * tile
        ct[at : at + 8, 0:128] = state[0][tile]
        ct[at : at + 8, 128:256] = state[1][tile]

    def body(i, carry):
        at = pl.multiple_of(32 * i, 32)
        for half in (0, 128):
            here = new[pl.ds(at, 32), half : half + 128]
            for t in range(2 * PIVOT):
                here = jnp.minimum(here, spread[pl.ds(at, 32), 128 * t : 128 * t + 128] + ct[t : t + 1, half : half + 128])
            new[pl.ds(at, 32), half : half + 128] = here
        return carry

    lax.fori_loop(0, COLS // 32, body, 0)
    for h in range(2):
        out[128 * h : 128 * h + 128, :] = new[:, 128 * h : 128 * h + 128].T


VM = pl.BlockSpec(memory_space=pltpu.VMEM)
SM = pl.BlockSpec(memory_space=pltpu.SMEM)
HBM = pl.BlockSpec(memory_space=pltpu.HBM)
MIB = 1024 * 1024


def call(kernel, shapes, scratch, ins, mib, outs=None):
    return pl.pallas_call(
        kernel,
        out_shape=[s if isinstance(s, jax.ShapeDtypeStruct) else jax.ShapeDtypeStruct(s, F32) for s in shapes],
        in_specs=ins,
        out_specs=outs or [VM] * len(shapes),
        scratch_shapes=[pltpu.VMEM(s, F32) if isinstance(s, tuple) else s for s in scratch],
        compiler_params=pltpu.CompilerParams(vmem_limit_bytes=mib * MIB),
    )


FINAL_SCRATCH = [(3, 16, 128), (128, 128), (64, 256), (64, 128), (128, 128), (128, 8192), (128, 256)]
ONEHOT = jax.ShapeDtypeStruct((64, 16 * 128), jnp.bfloat16)
PIVOTS = jax.ShapeDtypeStruct((2,), jnp.int32)


def on_device(distances, neighbor_ids, edge_lengths, pivots):
    piv, mt, scatter, panel, own_lengths = call(
        pack_kernel,
        [PIVOTS, (COLS, ROWS), (HOLDERS, 16, 128), (64, 128), (8, 128)],
        [(ROWS, COLS), (8, NEIGHBORS), pltpu.SemaphoreType.DMA((3,))],
        [HBM] * 3,
        8,
        [SM] + [VM] * 4,
    )(*[pltpu.with_memory_space_constraint(x, pltpu.HBM) for x in (pivots, distances, edge_lengths.T)])
    other_panel = lax.ppermute(panel, "row", [(i, i ^ 1) for i in range(NXY)])
    scatter = lax.all_to_all(scatter, ("z2", "z0", "core"), 0, 0)
    xy, keep, send = call(spread_kernel, [(NXY, XY_ROWS, 128), (8, 128), (8, 128)], [], [SM] + [VM] * 4, 8)(
        piv, scatter, own_lengths, panel, other_panel
    )
    other_half = lax.ppermute(send, "z1", [(0, 1), (1, 0)])
    lane_ids, sub_ids, onehot = call(
        ids_kernel, [(3, 16, 128), (24, NEIGHBORS, 8, 128), ONEHOT], [(128, 128)], [SM, VM], 16
    )(piv, neighbor_ids)
    xy = lax.all_to_all(xy, "row", 0, 0)
    xy, lane_ids, sub_ids, onehot = lax.optimization_barrier((xy, lane_ids, sub_ids, onehot))
    zed, rows = call(gather_kernel, [(NZ, Z_ROWS, 128), (64, 128)], [], [SM] + [VM] * 3, 8)(
        piv, xy, keep, other_half
    )
    zed = lax.all_to_all(zed, ("z3", "z2", "z1", "z0"), 0, 0)
    zed = lax.all_gather(zed, "core")
    (out,) = call(final_kernel, [(ROWS, COLS)], FINAL_SCRATCH, [SM] + [VM] * 6, 24)(
        piv, mt, rows, zed, lane_ids, sub_ids, onehot
    )
    return out


def solution(mesh):
    fine = Mesh(mesh.devices.reshape(16, 2, 2, 2, 2, 2), ("row", "z3", "z2", "z1", "z0", "core"))
    cols = ("z3", "z2", "z1", "z0", "core")
    placed = (P("row", cols), P(), P(None, ("row", *cols)), P())
    return jax.shard_map(on_device, mesh=fine, in_specs=placed, out_specs=P("row", cols), check_vma=False)
```

```python
import jax
import jax.numpy as jnp
from jax import lax
from jax.experimental import pallas as pl
from jax.experimental.pallas import tpu as pltpu
from jax.sharding import Mesh, PartitionSpec as P

NEIGHBORS = 10
PIVOT = 32
ROWS = 256
COLS = 128
NXY = 16
NZ = 16
F32 = jnp.float32
INF = float("inf")

XY_P, XY_Q, XY_ROWS = 8, 40, 72
Z_L, Z_ROWS = 8, 16
HOLDERS = 8


def lanes(rows):
    return lax.broadcasted_iota(jnp.int32, (rows, 128), 1)


def shift_lanes(x, amount):
    if isinstance(amount, int):
        return pltpu.roll(x, amount % 128, 1) if amount % 128 else x
    return pltpu.roll(x, lax.rem(amount + 1024, 128), 1)


def place():
    z = 0
    for bit in ("z3", "z2", "z1", "z0"):
        z = 2 * z + lax.axis_index(bit)
    return lax.axis_index("row"), z, lax.axis_index("core")


def upper_half():
    return lax.broadcasted_iota(jnp.int32, (8, 128), 0) < 4


def pack_kernel(pivots, dist, lengths, piv, mt, scatter, panel, own_lengths, block, held, sems):
    copies = [
        pltpu.make_async_copy(dist, block, sems.at[0]),
        pltpu.make_async_copy(lengths, held, sems.at[1]),
        pltpu.make_async_copy(pivots, piv, sems.at[2]),
    ]
    for copy in copies:
        copy.start()
    for copy in copies:
        copy.wait()
    for h in range(2):
        mt[:, 128 * h : 128 * h + 128] = block[128 * h : 128 * h + 128, :].T
    for i in range(2):
        off = lax.rem(piv[i], 4) * PIVOT
        for n in range(0, HOLDERS, 2):
            lines = mt[pl.ds(pl.multiple_of(off + 4 * n, 8), 8), :]
            for m in range(2):
                for h in range(2):
                    at = 8 * i + 4 * h
                    scatter[n + m, at : at + 4, :] = lines[4 * m : 4 * m + 4, 128 * h : 128 * h + 128]
        panel[32 * i : 32 * i + 32, :] = block[pl.ds(pl.multiple_of(lax.rem(piv[i], 8) * PIVOT, 32), 32), :]
    spaced = jnp.concatenate([held[...], jnp.zeros((8, 128 - NEIGHBORS), F32)], 1)
    lines = jnp.concatenate([spaced, jnp.zeros((120, 128), F32)], 0).T
    low, high = lines[0:8], lines[8:16]
    own_lengths[...] = low + shift_lanes(pltpu.roll(low, 4, 0), 32) + shift_lanes(high, 64)


def spread_kernel(piv, got, own_lengths, panel, xy, keep, send):
    p, q = piv[0], piv[1]
    _, z, _ = place()
    corner, halves = None, [[], []]
    for i, pivot in enumerate((p, q)):
        holder = lax.rem(pivot // 4, HOLDERS)
        mine = got[holder, 8 * i : 8 * i + 8]
        for b in range(2):
            halves[b] += [mine[2 * b : 2 * b + 2], mine[4 + 2 * b : 6 + 2 * b]]
        for j, other in enumerate((p, q)):
            half = jnp.where(lax.rem(other // 4, 2) == 0, mine, pltpu.roll(mine, 4, 0))
            half = shift_lanes(half, 64 * i + 32 * j - lax.rem(other, 4) * PIVOT)
            corner = half if corner is None else jnp.where(lanes(8) // PIVOT == 2 * i + j, half, corner)
    first, second = [jnp.concatenate(parts, 0) for parts in halves]
    even = lax.rem(z // 4, 2) == 0
    keep[...] = jnp.where(even, first, second)
    send[...] = jnp.where(even, second, first)
    small = jnp.where(upper_half(), own_lengths[...], pltpu.roll(corner, 4, 0))
    for d in range(NXY):
        xy[d, 0:XY_P] = small
        xy[d, XY_P:XY_ROWS] = panel[...]


def gather_kernel(piv, xy, keep, other, zchunk, rows):
    p, q = piv[0], piv[1]
    row, z, core = place()
    row_p, row_q = p // 8, q // 8
    rows[0:32] = xy[row_p, XY_P:XY_Q]
    rows[32:64] = xy[row_q, XY_Q:XY_ROWS]
    upper = upper_half()
    bit = lax.rem(z // 4, 2)
    piece = jnp.where(
        upper,
        jnp.where(lax.rem(p // 32, 2) == bit, keep[...], other[...]),
        jnp.where(lax.rem(q // 32, 2) == bit, keep[...], other[...]),
    )
    corner = jnp.where(lax.rem(lanes(8) // PIVOT, 2) == 0, xy[row_p, 0:XY_P], xy[row_q, 0:XY_P])
    turn = 2 * lax.rem(z, 2) + core

    def take(device, at):
        return shift_lanes(xy[device, 0:XY_P], 8 * lax.rem(turn + at, 4))

    fixed = take(row, 0) + take(row_p, 2) + take(row_q, 3)
    for d in range(NZ):
        zchunk[d, 0:Z_L] = piece
        zchunk[d, Z_L:Z_ROWS] = jnp.where(upper, fixed + take(d, 1), corner)


def ids_kernel(piv, ids, lane_ids, sub_ids, onehot, held):
    p, q = piv[0], piv[1]
    row, z, core = place()
    col = 2 * z + core

    def block(base):
        x = ids[:, pl.ds(pl.multiple_of(base, 128), 128)].astype(F32)
        return jnp.concatenate([x, jnp.zeros((6, 128), F32)], 0)

    for h in range(2):
        lane_ids[h] = block(256 * row + 128 * h)
    pivot_p = shift_lanes(block(p // 4 * 128), 0 - lax.rem(p, 4) * PIVOT)
    pivot_q = shift_lanes(block(q // 4 * 128), 32 - lax.rem(q, 4) * PIVOT)
    pivots = jnp.where(lanes(16) < 32, pivot_p, pivot_q)
    lane_ids[2] = pivots
    held[...] = jnp.zeros_like(held)
    held[0:16] = block(128 * col)
    held[16:32] = pivots
    turned = held[...].T
    for tile in range(24):
        at = 8 * (tile % 16)
        for k in range(NEIGHBORS):
            lane = 16 * (tile // 16) + k
            sub_ids[tile, k] = jnp.broadcast_to(turned[at : at + 8, lane : lane + 1], (8, 128))
    term = lax.broadcasted_iota(jnp.int32, (64, 128), 0)
    for t in range(16):
        picked = (lax.rem(term, 16) == t) & (term < 48)
        onehot[:, 128 * t : 128 * t + 128] = jnp.where(picked, 1.0, 0.0).astype(jnp.bfloat16)


def over_lanes(x, lane):
    return jnp.broadcast_to(x[:, lane : lane + 1], (8, 128))


def over_rows(x, row):
    return jnp.broadcast_to(x[row : row + 1, :], (8, 128))


def eliminate(state, b):
    corner = state[2]
    columns = [over_lanes(corner[b], 8 * b + j) for j in range(8)]
    rows = [state[kind][b] for kind in range(3)]
    for j in range(8):
        for u in range(j + 1, 8):
            columns[u] = jnp.minimum(columns[u], columns[j] + over_rows(columns[u], j))
        rows = [jnp.minimum(r, columns[j] + over_rows(r, j)) for r in rows]
    closed = [[over_rows(r, j) for j in range(8)] for r in rows]
    for i in range(8):
        if i == b:
            continue
        columns = [over_lanes(corner[i], 8 * b + j) for j in range(8)]
        for kind in range(3):
            paths = [columns[j] + closed[kind][j] for j in range(8)]
            while len(paths) > 1:
                paths = [jnp.minimum(paths[n], paths[n + 1]) for n in range(0, len(paths), 2)]
            state[kind][i] = jnp.minimum(state[kind][i], paths[0])
    for kind in range(3):
        state[kind][b] = rows[kind]


def thirds(x):
    high = x.astype(jnp.bfloat16)
    rest = x - high.astype(F32)
    mid = rest.astype(jnp.bfloat16)
    low = (rest - mid.astype(F32)).astype(jnp.bfloat16)
    return [
        jnp.concatenate([term[:, 16 * n : 16 * n + 16] for term in (high, mid, low, low)], 1) for n in range(4)
    ]


def final_kernel(piv, mt, rows, zed, lane_ids, sub_ids, onehot, out, lane_len, turned, ct, kt, rt, spread, new):
    p, q = piv[0], piv[1]
    row, z, core = place()
    col = 2 * z + core
    slot = lax.rem(lanes(8) // 8, 4)

    def lengths_at(first, count, at):
        parts = [None] * 3
        for v in range(count):
            merged = None
            for w in range(4):
                device = first + 4 * v + w
                tile = zed[w % 2, device // 2, Z_L:Z_ROWS]
                merged = tile if w == 0 else jnp.where(slot == (at + w) % 4, tile, merged)
            for g in range(3):
                moved = shift_lanes(merged, 32 * (v - g))
                parts[g] = moved if v == 0 else jnp.where(lanes(8) // 32 >= v, moved, parts[g])
        both = [jnp.where(upper_half(), parts[0], pltpu.roll(parts[1], 4, 0)), parts[2]]
        if at:
            both = [
                jnp.where(slot < 4 - at, shift_lanes(part, -8 * at), shift_lanes(part, 32 - 8 * at)) for part in both
            ]
        return jnp.concatenate(both, 0)

    lane_len[0] = lengths_at(0, 4, 0)
    lane_len[1] = lengths_at(16, 4, 0)
    lane_len[2] = jnp.where(
        lanes(16) < 32,
        lengths_at(lax.rem(p, 8) * 4, 1, 2),
        shift_lanes(lengths_at(lax.rem(q, 8) * 4, 1, 3), 32),
    )
    square = jnp.concatenate([lengths_at(16 * core, 4, 1), lane_len[2], jnp.zeros((96, 128), F32)], 0)
    turned[...] = square.T
    rt[:, 0:64] = rows[...].T

    for i, pivot in enumerate((p, q)):
        home = pivot // 64 * 8
        for n in range(HOLDERS):
            at = 32 * i + 4 * n
            base = home + n // 2
            for b in range(2):
                part = zed[n % 2, base + 4 * b, 0:Z_L]
                ct[at + 2 * b : at + 2 * b + 2, 0:128] = part[4 * i : 4 * i + 2]
                ct[at + 2 * b : at + 2 * b + 2, 128:256] = part[4 * i + 2 : 4 * i + 4]
            corner = zed[n % 2, base + 4 * lax.rem(pivot // 32, 2), Z_L:Z_ROWS]
            kt[at : at + 4, :] = shift_lanes(corner, 64 * i)[4:8]

    lane = lanes(8)
    sub = lax.broadcasted_iota(jnp.int32, (8, 128), 0)
    vertex = [
        (256 * row + lane).astype(F32),
        (256 * row + 128 + lane).astype(F32),
        jnp.where(lane < 32, 32 * p + lane, jnp.where(lane < 64, 32 * q + lane - 32, -1)).astype(F32),
    ]

    def relax(entries, vertices, tile, base):
        own = (base + sub).astype(F32)
        at, shift = 8 * (tile % 16), 16 * (tile // 16)
        turn = turned[at : at + 8, :]
        entries = list(entries)
        for k in range(NEIGHBORS):
            own_ids = sub_ids[tile, k]
            own_len = jnp.broadcast_to(turn[:, shift + k : shift + k + 1], (8, 128))
            for n, kind in enumerate(vertices):
                there = jnp.where(own_ids == vertex[kind], own_len, INF)
                back = jnp.where(lane_ids[kind, k : k + 1, :] == own, lane_len[kind, k : k + 1, :], INF)
                entries[n] = jnp.minimum(entries[n], jnp.minimum(there, back))
        return [jnp.where(own == vertex[kind], 0.0, e) for kind, e in zip(vertices, entries)]

    state = [[], [], []]
    for tile in range(8):
        at = 8 * tile
        base = (32 * p + at) if tile < 4 else (32 * q + at - 32)
        done = relax(
            [ct[at : at + 8, 0:128], ct[at : at + 8, 128:256], kt[at : at + 8, :]], (0, 1, 2), 16 + tile, base
        )
        for kind in range(3):
            state[kind].append(done[kind])
    for b in range(8):
        eliminate(state, b)
        if b < 4:
            for tile in range(4 * b, 4 * b + 4):
                at = 8 * tile
                entries = [mt[at : at + 8, 0:128], mt[at : at + 8, 128:256], rt[at : at + 8, :]]
                entries = relax(entries, (0, 1, 2), tile, 128 * col + at)
                new[at : at + 8, 0:128] = entries[0]
                new[at : at + 8, 128:256] = entries[1]
                rt[at : at + 8, :] = entries[2]
        else:
            if b == 4:
                parts = thirds(rt[...])
            for c in range(4):
                at = 2048 * (b - 4) + 512 * c
                spread[:, at : at + 512] = jnp.dot(
                    parts[b - 4], onehot[:, 512 * c : 512 * c + 512], preferred_element_type=F32
                )
    for tile in range(8):
        at = 8 * tile
        ct[at : at + 8, 0:128] = state[0][tile]
        ct[at : at + 8, 128:256] = state[1][tile]

    def body(i, carry):
        at = pl.multiple_of(32 * i, 32)
        for half in (0, 128):
            here = new[pl.ds(at, 32), half : half + 128]
            for t in range(2 * PIVOT):
                here = jnp.minimum(here, spread[pl.ds(at, 32), 128 * t : 128 * t + 128] + ct[t : t + 1, half : half + 128])
            new[pl.ds(at, 32), half : half + 128] = here
        return carry

    lax.fori_loop(0, COLS // 32, body, 0)
    for h in range(2):
        out[128 * h : 128 * h + 128, :] = new[:, 128 * h : 128 * h + 128].T


VM = pl.BlockSpec(memory_space=pltpu.VMEM)
SM = pl.BlockSpec(memory_space=pltpu.SMEM)
HBM = pl.BlockSpec(memory_space=pltpu.HBM)
MIB = 1024 * 1024


def call(kernel, shapes, scratch, ins, mib, outs=None):
    return pl.pallas_call(
        kernel,
        out_shape=[s if isinstance(s, jax.ShapeDtypeStruct) else jax.ShapeDtypeStruct(s, F32) for s in shapes],
        in_specs=ins,
        out_specs=outs or [VM] * len(shapes),
        scratch_shapes=[pltpu.VMEM(s, F32) if isinstance(s, tuple) else s for s in scratch],
        compiler_params=pltpu.CompilerParams(vmem_limit_bytes=mib * MIB),
    )


FINAL_SCRATCH = [(3, 16, 128), (128, 128), (64, 256), (64, 128), (128, 128), (128, 8192), (128, 256)]
ONEHOT = jax.ShapeDtypeStruct((64, 16 * 128), jnp.bfloat16)
PIVOTS = jax.ShapeDtypeStruct((2,), jnp.int32)


def on_device(distances, neighbor_ids, edge_lengths, pivots):
    piv, mt, scatter, panel, own_lengths = call(
        pack_kernel,
        [PIVOTS, (COLS, ROWS), (HOLDERS, 16, 128), (64, 128), (8, 128)],
        [(ROWS, COLS), (8, NEIGHBORS), pltpu.SemaphoreType.DMA((3,))],
        [HBM] * 3,
        8,
        [SM] + [VM] * 4,
    )(*[pltpu.with_memory_space_constraint(x, pltpu.HBM) for x in (pivots, distances, edge_lengths.T)])
    scatter = lax.all_to_all(scatter, ("z1", "z0", "core"), 0, 0)
    xy, keep, send = call(spread_kernel, [(NXY, XY_ROWS, 128), (8, 128), (8, 128)], [], [SM] + [VM] * 3, 8)(
        piv, scatter, own_lengths, panel
    )
    other_half = lax.ppermute(send, "z2", [(0, 1), (1, 0)])
    lane_ids, sub_ids, onehot = call(
        ids_kernel, [(3, 16, 128), (24, NEIGHBORS, 8, 128), ONEHOT], [(128, 128)], [SM, VM], 16
    )(piv, neighbor_ids)
    xy = lax.all_to_all(xy, "row", 0, 0)
    xy, lane_ids, sub_ids, onehot = lax.optimization_barrier((xy, lane_ids, sub_ids, onehot))
    zed, rows = call(gather_kernel, [(NZ, Z_ROWS, 128), (64, 128)], [], [SM] + [VM] * 3, 8)(
        piv, xy, keep, other_half
    )
    zed = lax.all_to_all(zed, ("z3", "z2", "z1", "z0"), 0, 0)
    zed = lax.all_gather(zed, "core")
    (out,) = call(final_kernel, [(ROWS, COLS)], FINAL_SCRATCH, [SM] + [VM] * 6, 24)(
        piv, mt, rows, zed, lane_ids, sub_ids, onehot
    )
    return out


def solution(mesh):
    fine = Mesh(mesh.devices.reshape(16, 2, 2, 2, 2, 2), ("row", "z3", "z2", "z1", "z0", "core"))
    cols = ("z3", "z2", "z1", "z0", "core")
    placed = (P("row", cols), P(), P(None, ("row", *cols)), P())
    return jax.shard_map(on_device, mesh=fine, in_specs=placed, out_specs=P("row", cols), check_vma=False)
```

```python
import jax
import jax.numpy as jnp
from jax import lax
from jax.experimental import pallas as pl
from jax.experimental.pallas import tpu as pltpu
from jax.sharding import Mesh, PartitionSpec as P

NEIGHBORS = 10
PIVOT = 32
ROWS = 256
COLS = 128
NXY = 16
NZ = 16
F32 = jnp.float32
INF = float("inf")

XY_P, XY_Q, XY_ROWS = 8, 24, 40
Z_L, Z_ROWS = 16, 24
HOLDERS = 8


def lanes(rows):
    return lax.broadcasted_iota(jnp.int32, (rows, 128), 1)


def shift_lanes(x, amount):
    if isinstance(amount, int):
        return pltpu.roll(x, amount % 128, 1) if amount % 128 else x
    return pltpu.roll(x, lax.rem(amount + 1024, 128), 1)


def place():
    z = 0
    for bit in ("z3", "z2", "z1", "z0"):
        z = 2 * z + lax.axis_index(bit)
    return lax.axis_index("row"), z, lax.axis_index("core")


def upper_half():
    return lax.broadcasted_iota(jnp.int32, (8, 128), 0) < 4


def pack_kernel(pivots, dist, lengths, piv, mt, scatter, panel, own_lengths, block, held, sems):
    copies = [
        pltpu.make_async_copy(dist, block, sems.at[0]),
        pltpu.make_async_copy(lengths, held, sems.at[1]),
        pltpu.make_async_copy(pivots, piv, sems.at[2]),
    ]
    for copy in copies:
        copy.start()
    for copy in copies:
        copy.wait()
    for h in range(2):
        mt[:, 128 * h : 128 * h + 128] = block[128 * h : 128 * h + 128, :].T
    for i in range(2):
        off = lax.rem(piv[i], 4) * PIVOT
        for n in range(0, HOLDERS, 2):
            lines = mt[pl.ds(pl.multiple_of(off + 4 * n, 8), 8), :]
            for m in range(2):
                for h in range(2):
                    at = 8 * i + 4 * h
                    scatter[n + m, at : at + 4, :] = lines[4 * m : 4 * m + 4, 128 * h : 128 * h + 128]
        panel[32 * i : 32 * i + 32, :] = block[pl.ds(pl.multiple_of(lax.rem(piv[i], 8) * PIVOT, 32), 32), :]
    spaced = jnp.concatenate([held[...], jnp.zeros((8, 128 - NEIGHBORS), F32)], 1)
    lines = jnp.concatenate([spaced, jnp.zeros((120, 128), F32)], 0).T
    low, high = lines[0:8], lines[8:16]
    own_lengths[...] = low + shift_lanes(pltpu.roll(low, 4, 0), 32) + shift_lanes(high, 64)


def spread_kernel(piv, got, own_lengths, panel, other_panel, xy, piece):
    p, q = piv[0], piv[1]
    row, _, _ = place()
    corner = None
    for i, pivot in enumerate((p, q)):
        holder = lax.rem(pivot // 4, HOLDERS)
        mine = got[holder, 8 * i : 8 * i + 8]
        piece[8 * i : 8 * i + 8, :] = mine
        for j, other in enumerate((p, q)):
            half = jnp.where(lax.rem(other // 4, 2) == 0, mine, pltpu.roll(mine, 4, 0))
            half = shift_lanes(half, 64 * i + 32 * j - lax.rem(other, 4) * PIVOT)
            corner = half if corner is None else jnp.where(lanes(8) // PIVOT == 2 * i + j, half, corner)
    small = jnp.where(upper_half(), own_lengths[...], pltpu.roll(corner, 4, 0))
    part = pl.multiple_of(16 * lax.rem(row, 2), 16)
    lines = [
        jnp.where(
            lax.rem(pivot // 8 + row, 2) == 0,
            panel[pl.ds(32 * i + part, 16), :],
            other_panel[pl.ds(32 * i + part, 16), :],
        )
        for i, pivot in enumerate((p, q))
    ]
    for d in range(NXY):
        xy[d, 0:XY_P] = small
        xy[d, XY_P:XY_Q] = lines[0]
        xy[d, XY_Q:XY_ROWS] = lines[1]


def gather_kernel(piv, xy, piece, zchunk, rows):
    p, q = piv[0], piv[1]
    row, z, core = place()
    row_p, row_q = p // 8, q // 8
    for b in range(2):
        rows[16 * b : 16 * b + 16] = xy[row_p // 2 * 2 + b, XY_P:XY_Q]
        rows[32 + 16 * b : 48 + 16 * b] = xy[row_q // 2 * 2 + b, XY_Q:XY_ROWS]
    upper = upper_half()
    corner = jnp.where(lax.rem(lanes(8) // PIVOT, 2) == 0, xy[row_p, 0:XY_P], xy[row_q, 0:XY_P])
    turn = 2 * lax.rem(z, 2) + core

    def take(device, at):
        return shift_lanes(xy[device, 0:XY_P], 8 * lax.rem(turn + at, 4))

    fixed = take(row, 0) + take(row_p, 2) + take(row_q, 3)
    for d in range(NZ):
        zchunk[d, 0:Z_L] = piece[...]
        zchunk[d, Z_L:Z_ROWS] = jnp.where(upper, fixed + take(d, 1), corner)


def ids_kernel(piv, ids, lane_ids, sub_ids, onehot, held):
    p, q = piv[0], piv[1]
    row, z, core = place()
    col = 2 * z + core

    def block(base):
        x = ids[:, pl.ds(pl.multiple_of(base, 128), 128)].astype(F32)
        return jnp.concatenate([x, jnp.zeros((6, 128), F32)], 0)

    for h in range(2):
        lane_ids[h] = block(256 * row + 128 * h)
    pivot_p = shift_lanes(block(p // 4 * 128), 0 - lax.rem(p, 4) * PIVOT)
    pivot_q = shift_lanes(block(q // 4 * 128), 32 - lax.rem(q, 4) * PIVOT)
    pivots = jnp.where(lanes(16) < 32, pivot_p, pivot_q)
    lane_ids[2] = pivots
    held[...] = jnp.zeros_like(held)
    held[0:16] = block(128 * col)
    held[16:32] = pivots
    turned = held[...].T
    for tile in range(24):
        at = 8 * (tile % 16)
        for k in range(NEIGHBORS):
            lane = 16 * (tile // 16) + k
            sub_ids[tile, k] = jnp.broadcast_to(turned[at : at + 8, lane : lane + 1], (8, 128))
    term = lax.broadcasted_iota(jnp.int32, (64, 128), 0)
    for t in range(16):
        picked = (lax.rem(term, 16) == t) & (term < 48)
        onehot[:, 128 * t : 128 * t + 128] = jnp.where(picked, 1.0, 0.0).astype(jnp.bfloat16)


def over_lanes(x, lane):
    return jnp.broadcast_to(x[:, lane : lane + 1], (8, 128))


def over_rows(x, row):
    return jnp.broadcast_to(x[row : row + 1, :], (8, 128))


def eliminate(state, b):
    corner = state[2]
    columns = [over_lanes(corner[b], 8 * b + j) for j in range(8)]
    rows = [state[kind][b] for kind in range(3)]
    for j in range(8):
        for u in range(j + 1, 8):
            columns[u] = jnp.minimum(columns[u], columns[j] + over_rows(columns[u], j))
        rows = [jnp.minimum(r, columns[j] + over_rows(r, j)) for r in rows]
    closed = [[over_rows(r, j) for j in range(8)] for r in rows]
    for i in range(8):
        if i == b:
            continue
        columns = [over_lanes(corner[i], 8 * b + j) for j in range(8)]
        for kind in range(3):
            paths = [columns[j] + closed[kind][j] for j in range(8)]
            while len(paths) > 1:
                paths = [jnp.minimum(paths[n], paths[n + 1]) for n in range(0, len(paths), 2)]
            state[kind][i] = jnp.minimum(state[kind][i], paths[0])
    for kind in range(3):
        state[kind][b] = rows[kind]


def thirds(x):
    high = x.astype(jnp.bfloat16)
    rest = x - high.astype(F32)
    mid = rest.astype(jnp.bfloat16)
    low = (rest - mid.astype(F32)).astype(jnp.bfloat16)
    return [
        jnp.concatenate([term[:, 16 * n : 16 * n + 16] for term in (high, mid, low, low)], 1) for n in range(4)
    ]


def final_kernel(piv, mt, rows, zed, lane_ids, sub_ids, onehot, out, lane_len, turned, ct, kt, rt, spread, new):
    p, q = piv[0], piv[1]
    row, z, core = place()
    col = 2 * z + core
    slot = lax.rem(lanes(8) // 8, 4)

    def lengths_at(first, count, at):
        parts = [None] * 3
        for v in range(count):
            merged = None
            for w in range(4):
                device = first + 4 * v + w
                tile = zed[w % 2, device // 2, Z_L:Z_ROWS]
                merged = tile if w == 0 else jnp.where(slot == (at + w) % 4, tile, merged)
            for g in range(3):
                moved = shift_lanes(merged, 32 * (v - g))
                parts[g] = moved if v == 0 else jnp.where(lanes(8) // 32 >= v, moved, parts[g])
        both = [jnp.where(upper_half(), parts[0], pltpu.roll(parts[1], 4, 0)), parts[2]]
        if at:
            both = [
                jnp.where(slot < 4 - at, shift_lanes(part, -8 * at), shift_lanes(part, 32 - 8 * at)) for part in both
            ]
        return jnp.concatenate(both, 0)

    lane_len[0] = lengths_at(0, 4, 0)
    lane_len[1] = lengths_at(16, 4, 0)
    lane_len[2] = jnp.where(
        lanes(16) < 32,
        lengths_at(lax.rem(p, 8) * 4, 1, 2),
        shift_lanes(lengths_at(lax.rem(q, 8) * 4, 1, 3), 32),
    )
    square = jnp.concatenate([lengths_at(16 * core, 4, 1), lane_len[2], jnp.zeros((96, 128), F32)], 0)
    turned[...] = square.T
    rt[:, 0:64] = rows[...].T

    for i, pivot in enumerate((p, q)):
        for n in range(HOLDERS):
            at = 32 * i + 4 * n
            holder = pivot // 32 * 4 + n // 2
            part = zed[n % 2, holder, 8 * i : 8 * i + 8]
            ct[at : at + 4, 0:128] = part[0:4]
            ct[at : at + 4, 128:256] = part[4:8]
            corner = zed[n % 2, holder, Z_L:Z_ROWS]
            kt[at : at + 4, :] = shift_lanes(corner, 64 * i)[4:8]

    lane = lanes(8)
    sub = lax.broadcasted_iota(jnp.int32, (8, 128), 0)
    vertex = [
        (256 * row + lane).astype(F32),
        (256 * row + 128 + lane).astype(F32),
        jnp.where(lane < 32, 32 * p + lane, jnp.where(lane < 64, 32 * q + lane - 32, -1)).astype(F32),
    ]

    def relax(entries, vertices, tile, base):
        own = (base + sub).astype(F32)
        at, shift = 8 * (tile % 16), 16 * (tile // 16)
        turn = turned[at : at + 8, :]
        entries = list(entries)
        for k in range(NEIGHBORS):
            own_ids = sub_ids[tile, k]
            own_len = jnp.broadcast_to(turn[:, shift + k : shift + k + 1], (8, 128))
            for n, kind in enumerate(vertices):
                there = jnp.where(own_ids == vertex[kind], own_len, INF)
                back = jnp.where(lane_ids[kind, k : k + 1, :] == own, lane_len[kind, k : k + 1, :], INF)
                entries[n] = jnp.minimum(entries[n], jnp.minimum(there, back))
        return [jnp.where(own == vertex[kind], 0.0, e) for kind, e in zip(vertices, entries)]

    state = [[], [], []]
    for tile in range(8):
        at = 8 * tile
        base = (32 * p + at) if tile < 4 else (32 * q + at - 32)
        done = relax(
            [ct[at : at + 8, 0:128], ct[at : at + 8, 128:256], kt[at : at + 8, :]], (0, 1, 2), 16 + tile, base
        )
        for kind in range(3):
            state[kind].append(done[kind])
    for b in range(8):
        eliminate(state, b)
        if b < 4:
            for tile in range(4 * b, 4 * b + 4):
                at = 8 * tile
                entries = [mt[at : at + 8, 0:128], mt[at : at + 8, 128:256], rt[at : at + 8, :]]
                entries = relax(entries, (0, 1, 2), tile, 128 * col + at)
                new[at : at + 8, 0:128] = entries[0]
                new[at : at + 8, 128:256] = entries[1]
                rt[at : at + 8, :] = entries[2]
        else:
            if b == 4:
                parts = thirds(rt[...])
            for c in range(4):
                at = 2048 * (b - 4) + 512 * c
                spread[:, at : at + 512] = jnp.dot(
                    parts[b - 4], onehot[:, 512 * c : 512 * c + 512], preferred_element_type=F32
                )
    for tile in range(8):
        at = 8 * tile
        ct[at : at + 8, 0:128] = state[0][tile]
        ct[at : at + 8, 128:256] = state[1][tile]

    def body(i, carry):
        at = pl.multiple_of(32 * i, 32)
        for half in (0, 128):
            here = new[pl.ds(at, 32), half : half + 128]
            for t in range(2 * PIVOT):
                here = jnp.minimum(here, spread[pl.ds(at, 32), 128 * t : 128 * t + 128] + ct[t : t + 1, half : half + 128])
            new[pl.ds(at, 32), half : half + 128] = here
        return carry

    lax.fori_loop(0, COLS // 32, body, 0)
    for h in range(2):
        out[128 * h : 128 * h + 128, :] = new[:, 128 * h : 128 * h + 128].T


VM = pl.BlockSpec(memory_space=pltpu.VMEM)
SM = pl.BlockSpec(memory_space=pltpu.SMEM)
HBM = pl.BlockSpec(memory_space=pltpu.HBM)
MIB = 1024 * 1024


def call(kernel, shapes, scratch, ins, mib, outs=None):
    return pl.pallas_call(
        kernel,
        out_shape=[s if isinstance(s, jax.ShapeDtypeStruct) else jax.ShapeDtypeStruct(s, F32) for s in shapes],
        in_specs=ins,
        out_specs=outs or [VM] * len(shapes),
        scratch_shapes=[pltpu.VMEM(s, F32) if isinstance(s, tuple) else s for s in scratch],
        compiler_params=pltpu.CompilerParams(vmem_limit_bytes=mib * MIB),
    )


FINAL_SCRATCH = [(3, 16, 128), (128, 128), (64, 256), (64, 128), (128, 128), (128, 8192), (128, 256)]
ONEHOT = jax.ShapeDtypeStruct((64, 16 * 128), jnp.bfloat16)
PIVOTS = jax.ShapeDtypeStruct((2,), jnp.int32)


def on_device(distances, neighbor_ids, edge_lengths, pivots):
    piv, mt, scatter, panel, own_lengths = call(
        pack_kernel,
        [PIVOTS, (COLS, ROWS), (HOLDERS, 16, 128), (64, 128), (8, 128)],
        [(ROWS, COLS), (8, NEIGHBORS), pltpu.SemaphoreType.DMA((3,))],
        [HBM] * 3,
        8,
        [SM] + [VM] * 4,
    )(*[pltpu.with_memory_space_constraint(x, pltpu.HBM) for x in (pivots, distances, edge_lengths.T)])
    lane_ids, sub_ids, onehot = call(
        ids_kernel, [(3, 16, 128), (24, NEIGHBORS, 8, 128), ONEHOT], [(128, 128)], [SM, VM], 16
    )(piv, neighbor_ids)
    other_panel = lax.ppermute(panel, "row", [(i, i ^ 1) for i in range(NXY)])
    scatter = lax.all_to_all(scatter, ("z1", "z0", "core"), 0, 0)
    scatter, lane_ids, sub_ids, onehot = lax.optimization_barrier((scatter, lane_ids, sub_ids, onehot))
    xy, piece = call(spread_kernel, [(NXY, XY_ROWS, 128), (16, 128)], [], [SM] + [VM] * 4, 8)(
        piv, scatter, own_lengths, panel, other_panel
    )
    xy = lax.all_to_all(xy, "row", 0, 0)
    zed, rows = call(gather_kernel, [(NZ, Z_ROWS, 128), (64, 128)], [], [SM] + [VM] * 2, 8)(piv, xy, piece)
    zed = lax.all_to_all(zed, ("z3", "z2", "z1", "z0"), 0, 0)
    zed = lax.all_gather(zed, "core")
    (out,) = call(final_kernel, [(ROWS, COLS)], FINAL_SCRATCH, [SM] + [VM] * 6, 24)(
        piv, mt, rows, zed, lane_ids, sub_ids, onehot
    )
    return out


def solution(mesh):
    fine = Mesh(mesh.devices.reshape(16, 2, 2, 2, 2, 2), ("row", "z3", "z2", "z1", "z0", "core"))
    cols = ("z3", "z2", "z1", "z0", "core")
    placed = (P("row", cols), P(), P(None, ("row", *cols)), P())
    return jax.shard_map(on_device, mesh=fine, in_specs=placed, out_specs=P("row", cols), check_vma=False)
```

```python
import jax
import jax.numpy as jnp
from jax import lax
from jax.experimental import pallas as pl
from jax.experimental.pallas import tpu as pltpu
from jax.sharding import Mesh, PartitionSpec as P

NEIGHBORS = 10
PIVOT = 32
ROWS = 256
COLS = 128
NXY = 16
NZ = 16
F32 = jnp.float32
INF = float("inf")

XY_P, XY_Q, XY_ROWS = 8, 24, 40
Z_L, Z_ROWS = 8, 16
HOLDERS = 8


def lanes(rows):
    return lax.broadcasted_iota(jnp.int32, (rows, 128), 1)


def shift_lanes(x, amount):
    if isinstance(amount, int):
        return pltpu.roll(x, amount % 128, 1) if amount % 128 else x
    return pltpu.roll(x, lax.rem(amount + 1024, 128), 1)


def place():
    z = 0
    for bit in ("z3", "z2", "z1", "z0"):
        z = 2 * z + lax.axis_index(bit)
    return lax.axis_index("row"), z, lax.axis_index("core")


def upper_half():
    return lax.broadcasted_iota(jnp.int32, (8, 128), 0) < 4


def pack_kernel(pivots, dist, lengths, piv, mt, scatter, panel, own_lengths, block, held, sems):
    copies = [
        pltpu.make_async_copy(dist, block, sems.at[0]),
        pltpu.make_async_copy(lengths, held, sems.at[1]),
        pltpu.make_async_copy(pivots, piv, sems.at[2]),
    ]
    for copy in copies:
        copy.start()
    for copy in copies:
        copy.wait()
    for h in range(2):
        mt[:, 128 * h : 128 * h + 128] = block[128 * h : 128 * h + 128, :].T
    for i in range(2):
        off = lax.rem(piv[i], 4) * PIVOT
        for n in range(0, HOLDERS, 2):
            lines = mt[pl.ds(pl.multiple_of(off + 4 * n, 8), 8), :]
            for m in range(2):
                for h in range(2):
                    at = 8 * i + 4 * h
                    scatter[n + m, at : at + 4, :] = lines[4 * m : 4 * m + 4, 128 * h : 128 * h + 128]
        panel[32 * i : 32 * i + 32, :] = block[pl.ds(pl.multiple_of(lax.rem(piv[i], 8) * PIVOT, 32), 32), :]
    spaced = jnp.concatenate([held[...], jnp.zeros((8, 128 - NEIGHBORS), F32)], 1)
    lines = jnp.concatenate([spaced, jnp.zeros((120, 128), F32)], 0).T
    low, high = lines[0:8], lines[8:16]
    own_lengths[...] = low + shift_lanes(pltpu.roll(low, 4, 0), 32) + shift_lanes(high, 64)


def spread_kernel(piv, got, own_lengths, panel, other_panel, xy, keep, send):
    p, q = piv[0], piv[1]
    row, z, _ = place()
    corner, halves = None, [[], []]
    for i, pivot in enumerate((p, q)):
        holder = lax.rem(pivot // 4, HOLDERS)
        mine = got[holder, 8 * i : 8 * i + 8]
        for b in range(2):
            halves[b] += [mine[2 * b : 2 * b + 2], mine[4 + 2 * b : 6 + 2 * b]]
        for j, other in enumerate((p, q)):
            half = jnp.where(lax.rem(other // 4, 2) == 0, mine, pltpu.roll(mine, 4, 0))
            half = shift_lanes(half, 64 * i + 32 * j - lax.rem(other, 4) * PIVOT)
            corner = half if corner is None else jnp.where(lanes(8) // PIVOT == 2 * i + j, half, corner)
    first, second = [jnp.concatenate(parts, 0) for parts in halves]
    even = lax.rem(z // 4, 2) == 0
    keep[...] = jnp.where(even, first, second)
    send[...] = jnp.where(even, second, first)
    small = jnp.where(upper_half(), own_lengths[...], pltpu.roll(corner, 4, 0))
    part = pl.multiple_of(16 * lax.rem(row, 2), 16)
    lines = [
        jnp.where(
            lax.rem(pivot // 8 + row, 2) == 0,
            panel[pl.ds(32 * i + part, 16), :],
            other_panel[pl.ds(32 * i + part, 16), :],
        )
        for i, pivot in enumerate((p, q))
    ]
    for d in range(NXY):
        xy[d, 0:XY_P] = small
        xy[d, XY_P:XY_Q] = lines[0]
        xy[d, XY_Q:XY_ROWS] = lines[1]


def gather_kernel(piv, xy, keep, other, zchunk, rows):
    p, q = piv[0], piv[1]
    row, z, core = place()
    row_p, row_q = p // 8, q // 8
    for b in range(2):
        rows[16 * b : 16 * b + 16] = xy[row_p // 2 * 2 + b, XY_P:XY_Q]
        rows[32 + 16 * b : 48 + 16 * b] = xy[row_q // 2 * 2 + b, XY_Q:XY_ROWS]
    upper = upper_half()
    bit = lax.rem(z // 4, 2)
    piece = jnp.where(
        upper,
        jnp.where(lax.rem(p // 32, 2) == bit, keep[...], other[...]),
        jnp.where(lax.rem(q // 32, 2) == bit, keep[...], other[...]),
    )
    corner = jnp.where(lax.rem(lanes(8) // PIVOT, 2) == 0, xy[row_p, 0:XY_P], xy[row_q, 0:XY_P])
    turn = 2 * lax.rem(z, 2) + core

    def take(device, at):
        return shift_lanes(xy[device, 0:XY_P], 8 * lax.rem(turn + at, 4))

    fixed = take(row, 0) + take(row_p, 2) + take(row_q, 3)
    for d in range(NZ):
        zchunk[d, 0:Z_L] = piece
        zchunk[d, Z_L:Z_ROWS] = jnp.where(upper, fixed + take(d, 1), corner)


def ids_kernel(piv, ids, lane_ids, sub_ids, onehot, held):
    p, q = piv[0], piv[1]
    row, z, core = place()
    col = 2 * z + core

    def block(base):
        x = ids[:, pl.ds(pl.multiple_of(base, 128), 128)].astype(F32)
        return jnp.concatenate([x, jnp.zeros((6, 128), F32)], 0)

    for h in range(2):
        lane_ids[h] = block(256 * row + 128 * h)
    pivot_p = shift_lanes(block(p // 4 * 128), 0 - lax.rem(p, 4) * PIVOT)
    pivot_q = shift_lanes(block(q // 4 * 128), 32 - lax.rem(q, 4) * PIVOT)
    pivots = jnp.where(lanes(16) < 32, pivot_p, pivot_q)
    lane_ids[2] = pivots
    held[...] = jnp.zeros_like(held)
    held[0:16] = block(128 * col)
    held[16:32] = pivots
    turned = held[...].T
    for tile in range(24):
        at = 8 * (tile % 16)
        for k in range(NEIGHBORS):
            lane = 16 * (tile // 16) + k
            sub_ids[tile, k] = jnp.broadcast_to(turned[at : at + 8, lane : lane + 1], (8, 128))
    term = lax.broadcasted_iota(jnp.int32, (64, 128), 0)
    for t in range(16):
        picked = (lax.rem(term, 16) == t) & (term < 48)
        onehot[:, 128 * t : 128 * t + 128] = jnp.where(picked, 1.0, 0.0).astype(jnp.bfloat16)


def over_lanes(x, lane):
    return jnp.broadcast_to(x[:, lane : lane + 1], (8, 128))


def over_rows(x, row):
    return jnp.broadcast_to(x[row : row + 1, :], (8, 128))


def eliminate(state, b):
    corner = state[2]
    columns = [over_lanes(corner[b], 8 * b + j) for j in range(8)]
    rows = [state[kind][b] for kind in range(3)]
    for j in range(8):
        for u in range(j + 1, 8):
            columns[u] = jnp.minimum(columns[u], columns[j] + over_rows(columns[u], j))
        rows = [jnp.minimum(r, columns[j] + over_rows(r, j)) for r in rows]
    closed = [[over_rows(r, j) for j in range(8)] for r in rows]
    for i in range(8):
        if i == b:
            continue
        columns = [over_lanes(corner[i], 8 * b + j) for j in range(8)]
        for kind in range(3):
            paths = [columns[j] + closed[kind][j] for j in range(8)]
            while len(paths) > 1:
                paths = [jnp.minimum(paths[n], paths[n + 1]) for n in range(0, len(paths), 2)]
            state[kind][i] = jnp.minimum(state[kind][i], paths[0])
    for kind in range(3):
        state[kind][b] = rows[kind]


def thirds(x):
    high = x.astype(jnp.bfloat16)
    rest = x - high.astype(F32)
    mid = rest.astype(jnp.bfloat16)
    low = (rest - mid.astype(F32)).astype(jnp.bfloat16)
    return [
        jnp.concatenate([term[:, 16 * n : 16 * n + 16] for term in (high, mid, low, low)], 1) for n in range(4)
    ]


def final_kernel(piv, mt, rows, zed, lane_ids, sub_ids, onehot, out, lane_len, turned, ct, kt, rt, spread, new):
    p, q = piv[0], piv[1]
    row, z, core = place()
    col = 2 * z + core
    slot = lax.rem(lanes(8) // 8, 4)

    def lengths_at(first, count, at):
        parts = [None] * 3
        for v in range(count):
            merged = None
            for w in range(4):
                device = first + 4 * v + w
                tile = zed[w % 2, device // 2, Z_L:Z_ROWS]
                merged = tile if w == 0 else jnp.where(slot == (at + w) % 4, tile, merged)
            for g in range(3):
                moved = shift_lanes(merged, 32 * (v - g))
                parts[g] = moved if v == 0 else jnp.where(lanes(8) // 32 >= v, moved, parts[g])
        both = [jnp.where(upper_half(), parts[0], pltpu.roll(parts[1], 4, 0)), parts[2]]
        if at:
            both = [
                jnp.where(slot < 4 - at, shift_lanes(part, -8 * at), shift_lanes(part, 32 - 8 * at)) for part in both
            ]
        return jnp.concatenate(both, 0)

    lane_len[0] = lengths_at(0, 4, 0)
    lane_len[1] = lengths_at(16, 4, 0)
    lane_len[2] = jnp.where(
        lanes(16) < 32,
        lengths_at(lax.rem(p, 8) * 4, 1, 2),
        shift_lanes(lengths_at(lax.rem(q, 8) * 4, 1, 3), 32),
    )
    square = jnp.concatenate([lengths_at(16 * core, 4, 1), lane_len[2], jnp.zeros((96, 128), F32)], 0)
    turned[...] = square.T
    rt[:, 0:64] = rows[...].T

    for i, pivot in enumerate((p, q)):
        home = pivot // 64 * 8
        for n in range(HOLDERS):
            at = 32 * i + 4 * n
            base = home + n // 2
            for b in range(2):
                part = zed[n % 2, base + 4 * b, 0:Z_L]
                ct[at + 2 * b : at + 2 * b + 2, 0:128] = part[4 * i : 4 * i + 2]
                ct[at + 2 * b : at + 2 * b + 2, 128:256] = part[4 * i + 2 : 4 * i + 4]
            corner = zed[n % 2, base + 4 * lax.rem(pivot // 32, 2), Z_L:Z_ROWS]
            kt[at : at + 4, :] = shift_lanes(corner, 64 * i)[4:8]

    lane = lanes(8)
    sub = lax.broadcasted_iota(jnp.int32, (8, 128), 0)
    vertex = [
        (256 * row + lane).astype(F32),
        (256 * row + 128 + lane).astype(F32),
        jnp.where(lane < 32, 32 * p + lane, jnp.where(lane < 64, 32 * q + lane - 32, -1)).astype(F32),
    ]

    def relax(entries, vertices, tile, base):
        own = (base + sub).astype(F32)
        at, shift = 8 * (tile % 16), 16 * (tile // 16)
        turn = turned[at : at + 8, :]
        entries = list(entries)
        for k in range(NEIGHBORS):
            own_ids = sub_ids[tile, k]
            own_len = jnp.broadcast_to(turn[:, shift + k : shift + k + 1], (8, 128))
            for n, kind in enumerate(vertices):
                there = jnp.where(own_ids == vertex[kind], own_len, INF)
                back = jnp.where(lane_ids[kind, k : k + 1, :] == own, lane_len[kind, k : k + 1, :], INF)
                entries[n] = jnp.minimum(entries[n], jnp.minimum(there, back))
        return [jnp.where(own == vertex[kind], 0.0, e) for kind, e in zip(vertices, entries)]

    state = [[], [], []]
    for tile in range(8):
        at = 8 * tile
        base = (32 * p + at) if tile < 4 else (32 * q + at - 32)
        done = relax(
            [ct[at : at + 8, 0:128], ct[at : at + 8, 128:256], kt[at : at + 8, :]], (0, 1, 2), 16 + tile, base
        )
        for kind in range(3):
            state[kind].append(done[kind])
    for b in range(8):
        eliminate(state, b)
        if b < 4:
            for tile in range(4 * b, 4 * b + 4):
                at = 8 * tile
                entries = [mt[at : at + 8, 0:128], mt[at : at + 8, 128:256], rt[at : at + 8, :]]
                entries = relax(entries, (0, 1, 2), tile, 128 * col + at)
                new[at : at + 8, 0:128] = entries[0]
                new[at : at + 8, 128:256] = entries[1]
                rt[at : at + 8, :] = entries[2]
        else:
            if b == 4:
                parts = thirds(rt[...])
            for c in range(4):
                at = 2048 * (b - 4) + 512 * c
                spread[:, at : at + 512] = jnp.dot(
                    parts[b - 4], onehot[:, 512 * c : 512 * c + 512], preferred_element_type=F32
                )
    for tile in range(8):
        at = 8 * tile
        ct[at : at + 8, 0:128] = state[0][tile]
        ct[at : at + 8, 128:256] = state[1][tile]

    def body(i, carry):
        at = pl.multiple_of(32 * i, 32)
        for half in (0, 128):
            here = new[pl.ds(at, 32), half : half + 128]
            for t in range(2 * PIVOT):
                here = jnp.minimum(here, spread[pl.ds(at, 32), 128 * t : 128 * t + 128] + ct[t : t + 1, half : half + 128])
            new[pl.ds(at, 32), half : half + 128] = here
        return carry

    lax.fori_loop(0, COLS // 32, body, 0)
    for h in range(2):
        out[128 * h : 128 * h + 128, :] = new[:, 128 * h : 128 * h + 128].T


VM = pl.BlockSpec(memory_space=pltpu.VMEM)
SM = pl.BlockSpec(memory_space=pltpu.SMEM)
HBM = pl.BlockSpec(memory_space=pltpu.HBM)
MIB = 1024 * 1024


def call(kernel, shapes, scratch, ins, mib, outs=None):
    return pl.pallas_call(
        kernel,
        out_shape=[s if isinstance(s, jax.ShapeDtypeStruct) else jax.ShapeDtypeStruct(s, F32) for s in shapes],
        in_specs=ins,
        out_specs=outs or [VM] * len(shapes),
        scratch_shapes=[pltpu.VMEM(s, F32) if isinstance(s, tuple) else s for s in scratch],
        compiler_params=pltpu.CompilerParams(vmem_limit_bytes=mib * MIB),
    )


FINAL_SCRATCH = [(3, 16, 128), (128, 128), (64, 256), (64, 128), (128, 128), (128, 8192), (128, 256)]
ONEHOT = jax.ShapeDtypeStruct((64, 16 * 128), jnp.bfloat16)
PIVOTS = jax.ShapeDtypeStruct((2,), jnp.int32)


def on_device(distances, neighbor_ids, edge_lengths, pivots):
    piv, mt, scatter, panel, own_lengths = call(
        pack_kernel,
        [PIVOTS, (COLS, ROWS), (HOLDERS, 16, 128), (64, 128), (8, 128)],
        [(ROWS, COLS), (8, NEIGHBORS), pltpu.SemaphoreType.DMA((3,))],
        [HBM] * 3,
        8,
        [SM] + [VM] * 4,
    )(*[pltpu.with_memory_space_constraint(x, pltpu.HBM) for x in (pivots, distances, edge_lengths.T)])
    lane_ids, sub_ids, onehot = call(
        ids_kernel, [(3, 16, 128), (24, NEIGHBORS, 8, 128), ONEHOT], [(128, 128)], [SM, VM], 16
    )(piv, neighbor_ids)
    other_panel = lax.ppermute(panel, "row", [(i, i ^ 1) for i in range(NXY)])
    scatter = lax.all_to_all(scatter, ("z1", "z0", "core"), 0, 0)
    scatter, lane_ids, sub_ids, onehot = lax.optimization_barrier((scatter, lane_ids, sub_ids, onehot))
    xy, keep, send = call(spread_kernel, [(NXY, XY_ROWS, 128), (8, 128), (8, 128)], [], [SM] + [VM] * 4, 8)(
        piv, scatter, own_lengths, panel, other_panel
    )
    other = lax.ppermute(send, "z2", [(0, 1), (1, 0)])
    xy = lax.all_to_all(xy, "row", 0, 0)
    zed, rows = call(gather_kernel, [(NZ, Z_ROWS, 128), (64, 128)], [], [SM] + [VM] * 3, 8)(piv, xy, keep, other)
    zed = lax.all_to_all(zed, ("z3", "z2", "z1", "z0"), 0, 0)
    zed = lax.all_gather(zed, "core")
    (out,) = call(final_kernel, [(ROWS, COLS)], FINAL_SCRATCH, [SM] + [VM] * 6, 24)(
        piv, mt, rows, zed, lane_ids, sub_ids, onehot
    )
    return out


def solution(mesh):
    fine = Mesh(mesh.devices.reshape(16, 2, 2, 2, 2, 2), ("row", "z3", "z2", "z1", "z0", "core"))
    cols = ("z3", "z2", "z1", "z0", "core")
    placed = (P("row", cols), P(), P(None, ("row", *cols)), P())
    return jax.shard_map(on_device, mesh=fine, in_specs=placed, out_specs=P("row", cols), check_vma=False)
```

```python
import jax
import jax.numpy as jnp
from jax import lax
from jax.experimental import pallas as pl
from jax.experimental.pallas import tpu as pltpu
from jax.sharding import Mesh, PartitionSpec as P

NEIGHBORS = 10
PIVOT = 32
ROWS = 256
COLS = 128
NXY = 16
NZ = 16
F32 = jnp.float32
INF = float("inf")

XY_P, XY_Q, XY_ROWS = 8, 24, 40
Z_L, Z_ROWS = 8, 16
HOLDERS = 8


def lanes(rows):
    return lax.broadcasted_iota(jnp.int32, (rows, 128), 1)


def shift_lanes(x, amount):
    if isinstance(amount, int):
        return pltpu.roll(x, amount % 128, 1) if amount % 128 else x
    return pltpu.roll(x, lax.rem(amount + 1024, 128), 1)


def place():
    z = 0
    for bit in ("z3", "z2", "z1", "z0"):
        z = 2 * z + lax.axis_index(bit)
    return lax.axis_index("row"), z, lax.axis_index("core")


def upper_half():
    return lax.broadcasted_iota(jnp.int32, (8, 128), 0) < 4


def pack_kernel(pivots, dist, lengths, piv, mt, scatter, panel, own_lengths, block, held, sems):
    copies = [
        pltpu.make_async_copy(dist, block, sems.at[0]),
        pltpu.make_async_copy(lengths, held, sems.at[1]),
        pltpu.make_async_copy(pivots, piv, sems.at[2]),
    ]
    for copy in copies:
        copy.start()
    for copy in copies:
        copy.wait()
    for h in range(2):
        mt[:, 128 * h : 128 * h + 128] = block[128 * h : 128 * h + 128, :].T
    for i in range(2):
        off = lax.rem(piv[i], 4) * PIVOT
        for n in range(0, HOLDERS, 2):
            lines = mt[pl.ds(pl.multiple_of(off + 4 * n, 8), 8), :]
            for m in range(2):
                for h in range(2):
                    at = 8 * i + 4 * h
                    scatter[n + m, at : at + 4, :] = lines[4 * m : 4 * m + 4, 128 * h : 128 * h + 128]
        panel[32 * i : 32 * i + 32, :] = block[pl.ds(pl.multiple_of(lax.rem(piv[i], 8) * PIVOT, 32), 32), :]
    spaced = jnp.concatenate([held[...], jnp.zeros((8, 128 - NEIGHBORS), F32)], 1)
    lines = jnp.concatenate([spaced, jnp.zeros((120, 128), F32)], 0).T
    low, high = lines[0:8], lines[8:16]
    own_lengths[...] = low + shift_lanes(pltpu.roll(low, 4, 0), 32) + shift_lanes(high, 64)


def spread_kernel(piv, got, own_lengths, panel, other_panel, xy, keep, send):
    p, q = piv[0], piv[1]
    row, z, _ = place()
    corner, halves = None, [[], []]
    for i, pivot in enumerate((p, q)):
        holder = lax.rem(pivot // 4, HOLDERS)
        mine = got[holder, 8 * i : 8 * i + 8]
        for b in range(2):
            halves[b] += [mine[2 * b : 2 * b + 2], mine[4 + 2 * b : 6 + 2 * b]]
        for j, other in enumerate((p, q)):
            half = jnp.where(lax.rem(other // 4, 2) == 0, mine, pltpu.roll(mine, 4, 0))
            half = shift_lanes(half, 64 * i + 32 * j - lax.rem(other, 4) * PIVOT)
            corner = half if corner is None else jnp.where(lanes(8) // PIVOT == 2 * i + j, half, corner)
    first, second = [jnp.concatenate(parts, 0) for parts in halves]
    even = lax.rem(z // 4, 2) == 0
    keep[...] = jnp.where(even, first, second)
    send[...] = jnp.where(even, second, first)
    small = jnp.where(upper_half(), own_lengths[...], pltpu.roll(corner, 4, 0))
    part = pl.multiple_of(16 * lax.rem(row, 2), 16)
    lines = [
        jnp.where(
            lax.rem(pivot // 8 + row, 2) == 0,
            panel[pl.ds(32 * i + part, 16), :],
            other_panel[pl.ds(32 * i + part, 16), :],
        )
        for i, pivot in enumerate((p, q))
    ]
    for d in range(NXY):
        xy[d, 0:XY_P] = small
        xy[d, XY_P:XY_Q] = lines[0]
        xy[d, XY_Q:XY_ROWS] = lines[1]


def gather_kernel(piv, xy, keep, other, zchunk, rows):
    p, q = piv[0], piv[1]
    row, z, core = place()
    row_p, row_q = p // 8, q // 8
    for b in range(2):
        rows[16 * b : 16 * b + 16] = xy[row_p // 2 * 2 + b, XY_P:XY_Q]
        rows[32 + 16 * b : 48 + 16 * b] = xy[row_q // 2 * 2 + b, XY_Q:XY_ROWS]
    upper = upper_half()
    bit = lax.rem(z // 4, 2)
    piece = jnp.where(
        upper,
        jnp.where(lax.rem(p // 32, 2) == bit, keep[...], other[...]),
        jnp.where(lax.rem(q // 32, 2) == bit, keep[...], other[...]),
    )
    corner = jnp.where(lax.rem(lanes(8) // PIVOT, 2) == 0, xy[row_p, 0:XY_P], xy[row_q, 0:XY_P])
    turn = 2 * lax.rem(z, 2) + core

    def take(device, at):
        return shift_lanes(xy[device, 0:XY_P], 8 * lax.rem(turn + at, 4))

    fixed = take(row, 0) + take(row_p, 2) + take(row_q, 3)
    for d in range(NZ):
        zchunk[d, 0:Z_L] = piece
        zchunk[d, Z_L:Z_ROWS] = jnp.where(upper, fixed + take(d, 1), corner)


def ids_kernel(piv, ids, lane_ids, sub_ids, onehot, held):
    p, q = piv[0], piv[1]
    row, z, core = place()
    col = 2 * z + core

    def block(base):
        x = ids[:, pl.ds(pl.multiple_of(base, 128), 128)].astype(F32)
        return jnp.concatenate([x, jnp.zeros((6, 128), F32)], 0)

    for h in range(2):
        lane_ids[h] = block(256 * row + 128 * h)
    pivot_p = shift_lanes(block(p // 4 * 128), 0 - lax.rem(p, 4) * PIVOT)
    pivot_q = shift_lanes(block(q // 4 * 128), 32 - lax.rem(q, 4) * PIVOT)
    pivots = jnp.where(lanes(16) < 32, pivot_p, pivot_q)
    lane_ids[2] = pivots
    held[...] = jnp.zeros_like(held)
    held[0:16] = block(128 * col)
    held[16:32] = pivots
    turned = held[...].T
    for tile in range(24):
        at = 8 * (tile % 16)
        for k in range(NEIGHBORS):
            lane = 16 * (tile // 16) + k
            sub_ids[tile, k] = jnp.broadcast_to(turned[at : at + 8, lane : lane + 1], (8, 128))
    term = lax.broadcasted_iota(jnp.int32, (64, 128), 0)
    for t in range(16):
        picked = (lax.rem(term, 16) == t) & (term < 48)
        onehot[:, 128 * t : 128 * t + 128] = jnp.where(picked, 1.0, 0.0).astype(jnp.bfloat16)


def over_lanes(x, lane):
    return jnp.broadcast_to(x[:, lane : lane + 1], (8, 128))


def over_rows(x, row):
    return jnp.broadcast_to(x[row : row + 1, :], (8, 128))


def eliminate(state, b):
    corner = state[2]
    columns = [over_lanes(corner[b], 8 * b + j) for j in range(8)]
    rows = [state[kind][b] for kind in range(3)]
    for j in range(8):
        for u in range(j + 1, 8):
            columns[u] = jnp.minimum(columns[u], columns[j] + over_rows(columns[u], j))
        rows = [jnp.minimum(r, columns[j] + over_rows(r, j)) for r in rows]
    closed = [[over_rows(r, j) for j in range(8)] for r in rows]
    for i in range(8):
        if i == b:
            continue
        columns = [over_lanes(corner[i], 8 * b + j) for j in range(8)]
        for kind in range(3):
            paths = [columns[j] + closed[kind][j] for j in range(8)]
            while len(paths) > 1:
                paths = [jnp.minimum(paths[n], paths[n + 1]) for n in range(0, len(paths), 2)]
            state[kind][i] = jnp.minimum(state[kind][i], paths[0])
    for kind in range(3):
        state[kind][b] = rows[kind]


def thirds(x):
    high = x.astype(jnp.bfloat16)
    rest = x - high.astype(F32)
    mid = rest.astype(jnp.bfloat16)
    low = (rest - mid.astype(F32)).astype(jnp.bfloat16)
    return [
        jnp.concatenate([term[:, 16 * n : 16 * n + 16] for term in (high, mid, low, low)], 1) for n in range(4)
    ]


def final_kernel(piv, mt, rows, zed, lane_ids, sub_ids, onehot, out, lane_len, turned, ct, kt, rt, spread, new):
    p, q = piv[0], piv[1]
    row, z, core = place()
    col = 2 * z + core
    slot = lax.rem(lanes(8) // 8, 4)

    def lengths_at(first, count, at):
        parts = [None] * 3
        for v in range(count):
            merged = None
            for w in range(4):
                device = first + 4 * v + w
                tile = zed[w % 2, device // 2, Z_L:Z_ROWS]
                merged = tile if w == 0 else jnp.where(slot == (at + w) % 4, tile, merged)
            for g in range(3):
                moved = shift_lanes(merged, 32 * (v - g))
                parts[g] = moved if v == 0 else jnp.where(lanes(8) // 32 >= v, moved, parts[g])
        both = [jnp.where(upper_half(), parts[0], pltpu.roll(parts[1], 4, 0)), parts[2]]
        if at:
            both = [
                jnp.where(slot < 4 - at, shift_lanes(part, -8 * at), shift_lanes(part, 32 - 8 * at)) for part in both
            ]
        return jnp.concatenate(both, 0)

    lane_len[0] = lengths_at(0, 4, 0)
    lane_len[1] = lengths_at(16, 4, 0)
    lane_len[2] = jnp.where(
        lanes(16) < 32,
        lengths_at(lax.rem(p, 8) * 4, 1, 2),
        shift_lanes(lengths_at(lax.rem(q, 8) * 4, 1, 3), 32),
    )
    square = jnp.concatenate([lengths_at(16 * core, 4, 1), lane_len[2], jnp.zeros((96, 128), F32)], 0)
    turned[...] = square.T
    rt[:, 0:64] = rows[...].T

    for i, pivot in enumerate((p, q)):
        home = pivot // 64 * 8
        for n in range(HOLDERS):
            at = 32 * i + 4 * n
            base = home + n // 2
            for b in range(2):
                part = zed[n % 2, base + 4 * b, 0:Z_L]
                ct[at + 2 * b : at + 2 * b + 2, 0:128] = part[4 * i : 4 * i + 2]
                ct[at + 2 * b : at + 2 * b + 2, 128:256] = part[4 * i + 2 : 4 * i + 4]
            corner = zed[n % 2, base + 4 * lax.rem(pivot // 32, 2), Z_L:Z_ROWS]
            kt[at : at + 4, :] = shift_lanes(corner, 64 * i)[4:8]

    lane = lanes(8)
    sub = lax.broadcasted_iota(jnp.int32, (8, 128), 0)
    vertex = [
        (256 * row + lane).astype(F32),
        (256 * row + 128 + lane).astype(F32),
        jnp.where(lane < 32, 32 * p + lane, jnp.where(lane < 64, 32 * q + lane - 32, -1)).astype(F32),
    ]

    def relax(entries, vertices, tile, base):
        own = (base + sub).astype(F32)
        at, shift = 8 * (tile % 16), 16 * (tile // 16)
        turn = turned[at : at + 8, :]
        entries = list(entries)
        for k in range(NEIGHBORS):
            own_ids = sub_ids[tile, k]
            own_len = jnp.broadcast_to(turn[:, shift + k : shift + k + 1], (8, 128))
            for n, kind in enumerate(vertices):
                there = jnp.where(own_ids == vertex[kind], own_len, INF)
                back = jnp.where(lane_ids[kind, k : k + 1, :] == own, lane_len[kind, k : k + 1, :], INF)
                entries[n] = jnp.minimum(entries[n], jnp.minimum(there, back))
        return [jnp.where(own == vertex[kind], 0.0, e) for kind, e in zip(vertices, entries)]

    state = [[], [], []]
    for tile in range(8):
        at = 8 * tile
        base = (32 * p + at) if tile < 4 else (32 * q + at - 32)
        done = relax(
            [ct[at : at + 8, 0:128], ct[at : at + 8, 128:256], kt[at : at + 8, :]], (0, 1, 2), 16 + tile, base
        )
        for kind in range(3):
            state[kind].append(done[kind])
    for b in range(8):
        eliminate(state, b)
        if b < 4:
            for tile in range(4 * b, 4 * b + 4):
                at = 8 * tile
                entries = [mt[at : at + 8, 0:128], mt[at : at + 8, 128:256], rt[at : at + 8, :]]
                entries = relax(entries, (0, 1, 2), tile, 128 * col + at)
                new[at : at + 8, 0:128] = entries[0]
                new[at : at + 8, 128:256] = entries[1]
                rt[at : at + 8, :] = entries[2]
        else:
            if b == 4:
                parts = thirds(rt[...])
            for c in range(4):
                at = 2048 * (b - 4) + 512 * c
                spread[:, at : at + 512] = jnp.dot(
                    parts[b - 4], onehot[:, 512 * c : 512 * c + 512], preferred_element_type=F32
                )
    for tile in range(8):
        at = 8 * tile
        ct[at : at + 8, 0:128] = state[0][tile]
        ct[at : at + 8, 128:256] = state[1][tile]

    for at in range(0, COLS, 8):
        one = new[at : at + 8, 0:128]
        two = new[at : at + 8, 128:256]
        for t in range(2 * PIVOT):
            wide = spread[at : at + 8, 128 * t : 128 * t + 128]
            one = jnp.minimum(one, wide + ct[t : t + 1, 0:128])
            two = jnp.minimum(two, wide + ct[t : t + 1, 128:256])
        new[at : at + 8, 0:128] = one
        new[at : at + 8, 128:256] = two
    for h in range(2):
        out[128 * h : 128 * h + 128, :] = new[:, 128 * h : 128 * h + 128].T


VM = pl.BlockSpec(memory_space=pltpu.VMEM)
SM = pl.BlockSpec(memory_space=pltpu.SMEM)
HBM = pl.BlockSpec(memory_space=pltpu.HBM)
MIB = 1024 * 1024


def call(kernel, shapes, scratch, ins, mib, outs=None):
    return pl.pallas_call(
        kernel,
        out_shape=[s if isinstance(s, jax.ShapeDtypeStruct) else jax.ShapeDtypeStruct(s, F32) for s in shapes],
        in_specs=ins,
        out_specs=outs or [VM] * len(shapes),
        scratch_shapes=[pltpu.VMEM(s, F32) if isinstance(s, tuple) else s for s in scratch],
        compiler_params=pltpu.CompilerParams(vmem_limit_bytes=mib * MIB),
    )


FINAL_SCRATCH = [(3, 16, 128), (128, 128), (64, 256), (64, 128), (128, 128), (128, 8192), (128, 256)]
ONEHOT = jax.ShapeDtypeStruct((64, 16 * 128), jnp.bfloat16)
PIVOTS = jax.ShapeDtypeStruct((2,), jnp.int32)


def on_device(distances, neighbor_ids, edge_lengths, pivots):
    piv, mt, scatter, panel, own_lengths = call(
        pack_kernel,
        [PIVOTS, (COLS, ROWS), (HOLDERS, 16, 128), (64, 128), (8, 128)],
        [(ROWS, COLS), (8, NEIGHBORS), pltpu.SemaphoreType.DMA((3,))],
        [HBM] * 3,
        8,
        [SM] + [VM] * 4,
    )(*[pltpu.with_memory_space_constraint(x, pltpu.HBM) for x in (pivots, distances, edge_lengths.T)])
    lane_ids, sub_ids, onehot = call(
        ids_kernel, [(3, 16, 128), (24, NEIGHBORS, 8, 128), ONEHOT], [(128, 128)], [SM, VM], 16
    )(piv, neighbor_ids)
    other_panel = lax.ppermute(panel, "row", [(i, i ^ 1) for i in range(NXY)])
    scatter = lax.all_to_all(scatter, ("z1", "z0", "core"), 0, 0)
    scatter, lane_ids, sub_ids, onehot = lax.optimization_barrier((scatter, lane_ids, sub_ids, onehot))
    xy, keep, send = call(spread_kernel, [(NXY, XY_ROWS, 128), (8, 128), (8, 128)], [], [SM] + [VM] * 4, 8)(
        piv, scatter, own_lengths, panel, other_panel
    )
    other = lax.ppermute(send, "z2", [(0, 1), (1, 0)])
    xy = lax.all_to_all(xy, "row", 0, 0)
    zed, rows = call(gather_kernel, [(NZ, Z_ROWS, 128), (64, 128)], [], [SM] + [VM] * 3, 8)(piv, xy, keep, other)
    zed = lax.all_to_all(zed, ("z3", "z2", "z1", "z0"), 0, 0)
    zed = lax.all_gather(zed, "core")
    (out,) = call(final_kernel, [(ROWS, COLS)], FINAL_SCRATCH, [SM] + [VM] * 6, 24)(
        piv, mt, rows, zed, lane_ids, sub_ids, onehot
    )
    return out


def solution(mesh):
    fine = Mesh(mesh.devices.reshape(16, 2, 2, 2, 2, 2), ("row", "z3", "z2", "z1", "z0", "core"))
    cols = ("z3", "z2", "z1", "z0", "core")
    placed = (P("row", cols), P(), P(None, ("row", *cols)), P())
    return jax.shard_map(on_device, mesh=fine, in_specs=placed, out_specs=P("row", cols), check_vma=False)
```

```python
import jax
import jax.numpy as jnp
from jax import lax
from jax.experimental import pallas as pl
from jax.experimental.pallas import tpu as pltpu
from jax.sharding import Mesh, PartitionSpec as P

NEIGHBORS = 10
PIVOT = 32
ROWS = 256
COLS = 128
NXY = 16
NZ = 16
F32 = jnp.float32
INF = float("inf")

XY_P, XY_Q, XY_ROWS = 8, 24, 40
Z_L, Z_ROWS = 8, 16
HOLDERS = 8


def lanes(rows):
    return lax.broadcasted_iota(jnp.int32, (rows, 128), 1)


def shift_lanes(x, amount):
    if isinstance(amount, int):
        return pltpu.roll(x, amount % 128, 1) if amount % 128 else x
    return pltpu.roll(x, lax.rem(amount + 1024, 128), 1)


def place():
    z = 0
    for bit in ("z3", "z2", "z1", "z0"):
        z = 2 * z + lax.axis_index(bit)
    return lax.axis_index("row"), z, lax.axis_index("core")


def upper_half():
    return lax.broadcasted_iota(jnp.int32, (8, 128), 0) < 4


def pack_kernel(pivots, dist, lengths, piv, mt, scatter, panel, own_lengths, block, held, sems):
    halves = [pl.ds(128 * h, 128) for h in range(2)]
    parts = [pltpu.make_async_copy(dist.at[half], block.at[half], sems.at[h]) for h, half in enumerate(halves)]
    others = [
        pltpu.make_async_copy(pivots, piv, sems.at[2]),
        pltpu.make_async_copy(lengths, held, sems.at[3]),
    ]
    for copy in parts + others:
        copy.start()
    for h in range(2):
        parts[h].wait()
        mt[:, 128 * h : 128 * h + 128] = block[128 * h : 128 * h + 128, :].T
    for copy in others:
        copy.wait()
    for i in range(2):
        off = lax.rem(piv[i], 4) * PIVOT
        for n in range(0, HOLDERS, 2):
            lines = mt[pl.ds(pl.multiple_of(off + 4 * n, 8), 8), :]
            for m in range(2):
                for h in range(2):
                    at = 8 * i + 4 * h
                    scatter[n + m, at : at + 4, :] = lines[4 * m : 4 * m + 4, 128 * h : 128 * h + 128]
        panel[32 * i : 32 * i + 32, :] = block[pl.ds(pl.multiple_of(lax.rem(piv[i], 8) * PIVOT, 32), 32), :]
    spaced = jnp.concatenate([held[...], jnp.zeros((8, 128 - NEIGHBORS), F32)], 1)
    lines = jnp.concatenate([spaced, jnp.zeros((120, 128), F32)], 0).T
    low, high = lines[0:8], lines[8:16]
    own_lengths[...] = low + shift_lanes(pltpu.roll(low, 4, 0), 32) + shift_lanes(high, 64)


def spread_kernel(piv, got, own_lengths, panel, other_panel, xy, keep, send):
    p, q = piv[0], piv[1]
    row, z, _ = place()
    corner, halves = None, [[], []]
    for i, pivot in enumerate((p, q)):
        holder = lax.rem(pivot // 4, HOLDERS)
        mine = got[holder, 8 * i : 8 * i + 8]
        for b in range(2):
            halves[b] += [mine[2 * b : 2 * b + 2], mine[4 + 2 * b : 6 + 2 * b]]
        for j, other in enumerate((p, q)):
            half = jnp.where(lax.rem(other // 4, 2) == 0, mine, pltpu.roll(mine, 4, 0))
            half = shift_lanes(half, 64 * i + 32 * j - lax.rem(other, 4) * PIVOT)
            corner = half if corner is None else jnp.where(lanes(8) // PIVOT == 2 * i + j, half, corner)
    first, second = [jnp.concatenate(parts, 0) for parts in halves]
    even = lax.rem(z // 4, 2) == 0
    keep[...] = jnp.where(even, first, second)
    send[...] = jnp.where(even, second, first)
    small = jnp.where(upper_half(), own_lengths[...], pltpu.roll(corner, 4, 0))
    part = pl.multiple_of(16 * lax.rem(row, 2), 16)
    lines = [
        jnp.where(
            lax.rem(pivot // 8 + row, 2) == 0,
            panel[pl.ds(32 * i + part, 16), :],
            other_panel[pl.ds(32 * i + part, 16), :],
        )
        for i, pivot in enumerate((p, q))
    ]
    for d in range(NXY):
        xy[d, 0:XY_P] = small
        xy[d, XY_P:XY_Q] = lines[0]
        xy[d, XY_Q:XY_ROWS] = lines[1]


def gather_kernel(piv, xy, keep, other, zchunk, rows):
    p, q = piv[0], piv[1]
    row, z, core = place()
    row_p, row_q = p // 8, q // 8
    for b in range(2):
        rows[16 * b : 16 * b + 16] = xy[row_p // 2 * 2 + b, XY_P:XY_Q]
        rows[32 + 16 * b : 48 + 16 * b] = xy[row_q // 2 * 2 + b, XY_Q:XY_ROWS]
    upper = upper_half()
    bit = lax.rem(z // 4, 2)
    piece = jnp.where(
        upper,
        jnp.where(lax.rem(p // 32, 2) == bit, keep[...], other[...]),
        jnp.where(lax.rem(q // 32, 2) == bit, keep[...], other[...]),
    )
    corner = jnp.where(lax.rem(lanes(8) // PIVOT, 2) == 0, xy[row_p, 0:XY_P], xy[row_q, 0:XY_P])
    turn = 2 * lax.rem(z, 2) + core

    def take(device, at):
        return shift_lanes(xy[device, 0:XY_P], 8 * lax.rem(turn + at, 4))

    fixed = take(row, 0) + take(row_p, 2) + take(row_q, 3)
    for d in range(NZ):
        zchunk[d, 0:Z_L] = piece
        zchunk[d, Z_L:Z_ROWS] = jnp.where(upper, fixed + take(d, 1), corner)


def ids_kernel(piv, ids, lane_ids, sub_ids, onehot, held):
    p, q = piv[0], piv[1]
    row, z, core = place()
    col = 2 * z + core

    def block(base):
        x = ids[:, pl.ds(pl.multiple_of(base, 128), 128)].astype(F32)
        return jnp.concatenate([x, jnp.zeros((6, 128), F32)], 0)

    for h in range(2):
        lane_ids[h] = block(256 * row + 128 * h)
    pivot_p = shift_lanes(block(p // 4 * 128), 0 - lax.rem(p, 4) * PIVOT)
    pivot_q = shift_lanes(block(q // 4 * 128), 32 - lax.rem(q, 4) * PIVOT)
    pivots = jnp.where(lanes(16) < 32, pivot_p, pivot_q)
    lane_ids[2] = pivots
    held[...] = jnp.zeros_like(held)
    held[0:16] = block(128 * col)
    held[16:32] = pivots
    turned = held[...].T
    for tile in range(24):
        at = 8 * (tile % 16)
        for k in range(NEIGHBORS):
            lane = 16 * (tile // 16) + k
            sub_ids[tile, k] = jnp.broadcast_to(turned[at : at + 8, lane : lane + 1], (8, 128))
    term = lax.broadcasted_iota(jnp.int32, (64, 128), 0)
    for t in range(16):
        picked = (lax.rem(term, 16) == t) & (term < 48)
        onehot[:, 128 * t : 128 * t + 128] = jnp.where(picked, 1.0, 0.0).astype(jnp.bfloat16)


def over_lanes(x, lane):
    return jnp.broadcast_to(x[:, lane : lane + 1], (8, 128))


def over_rows(x, row):
    return jnp.broadcast_to(x[row : row + 1, :], (8, 128))


def eliminate(state, b):
    corner = state[2]
    columns = [over_lanes(corner[b], 8 * b + j) for j in range(8)]
    rows = [state[kind][b] for kind in range(3)]
    for j in range(8):
        for u in range(j + 1, 8):
            columns[u] = jnp.minimum(columns[u], columns[j] + over_rows(columns[u], j))
        rows = [jnp.minimum(r, columns[j] + over_rows(r, j)) for r in rows]
    closed = [[over_rows(r, j) for j in range(8)] for r in rows]
    for i in range(8):
        if i == b:
            continue
        columns = [over_lanes(corner[i], 8 * b + j) for j in range(8)]
        for kind in range(3):
            paths = [columns[j] + closed[kind][j] for j in range(8)]
            while len(paths) > 1:
                paths = [jnp.minimum(paths[n], paths[n + 1]) for n in range(0, len(paths), 2)]
            state[kind][i] = jnp.minimum(state[kind][i], paths[0])
    for kind in range(3):
        state[kind][b] = rows[kind]


def thirds(x):
    high = x.astype(jnp.bfloat16)
    rest = x - high.astype(F32)
    mid = rest.astype(jnp.bfloat16)
    low = (rest - mid.astype(F32)).astype(jnp.bfloat16)
    return [
        jnp.concatenate([term[:, 16 * n : 16 * n + 16] for term in (high, mid, low, low)], 1) for n in range(4)
    ]


def final_kernel(piv, mt, rows, zed, lane_ids, sub_ids, onehot, out, lane_len, turned, ct, kt, rt, spread, new):
    p, q = piv[0], piv[1]
    row, z, core = place()
    col = 2 * z + core
    slot = lax.rem(lanes(8) // 8, 4)

    def lengths_at(first, count, at):
        parts = [None] * 3
        for v in range(count):
            merged = None
            for w in range(4):
                device = first + 4 * v + w
                tile = zed[w % 2, device // 2, Z_L:Z_ROWS]
                merged = tile if w == 0 else jnp.where(slot == (at + w) % 4, tile, merged)
            for g in range(3):
                moved = shift_lanes(merged, 32 * (v - g))
                parts[g] = moved if v == 0 else jnp.where(lanes(8) // 32 >= v, moved, parts[g])
        both = [jnp.where(upper_half(), parts[0], pltpu.roll(parts[1], 4, 0)), parts[2]]
        if at:
            both = [
                jnp.where(slot < 4 - at, shift_lanes(part, -8 * at), shift_lanes(part, 32 - 8 * at)) for part in both
            ]
        return jnp.concatenate(both, 0)

    lane_len[0] = lengths_at(0, 4, 0)
    lane_len[1] = lengths_at(16, 4, 0)
    lane_len[2] = jnp.where(
        lanes(16) < 32,
        lengths_at(lax.rem(p, 8) * 4, 1, 2),
        shift_lanes(lengths_at(lax.rem(q, 8) * 4, 1, 3), 32),
    )
    square = jnp.concatenate([lengths_at(16 * core, 4, 1), lane_len[2], jnp.zeros((96, 128), F32)], 0)
    turned[...] = square.T
    rt[:, 0:64] = rows[...].T

    for i, pivot in enumerate((p, q)):
        home = pivot // 64 * 8
        for n in range(HOLDERS):
            at = 32 * i + 4 * n
            base = home + n // 2
            for b in range(2):
                part = zed[n % 2, base + 4 * b, 0:Z_L]
                ct[at + 2 * b : at + 2 * b + 2, 0:128] = part[4 * i : 4 * i + 2]
                ct[at + 2 * b : at + 2 * b + 2, 128:256] = part[4 * i + 2 : 4 * i + 4]
            corner = zed[n % 2, base + 4 * lax.rem(pivot // 32, 2), Z_L:Z_ROWS]
            kt[at : at + 4, :] = shift_lanes(corner, 64 * i)[4:8]

    lane = lanes(8)
    sub = lax.broadcasted_iota(jnp.int32, (8, 128), 0)
    vertex = [
        (256 * row + lane).astype(F32),
        (256 * row + 128 + lane).astype(F32),
        jnp.where(lane < 32, 32 * p + lane, jnp.where(lane < 64, 32 * q + lane - 32, -1)).astype(F32),
    ]

    def relax(entries, vertices, tile, base):
        own = (base + sub).astype(F32)
        at, shift = 8 * (tile % 16), 16 * (tile // 16)
        turn = turned[at : at + 8, :]
        entries = list(entries)
        for k in range(NEIGHBORS):
            own_ids = sub_ids[tile, k]
            own_len = jnp.broadcast_to(turn[:, shift + k : shift + k + 1], (8, 128))
            for n, kind in enumerate(vertices):
                there = jnp.where(own_ids == vertex[kind], own_len, INF)
                back = jnp.where(lane_ids[kind, k : k + 1, :] == own, lane_len[kind, k : k + 1, :], INF)
                entries[n] = jnp.minimum(entries[n], jnp.minimum(there, back))
        return [jnp.where(own == vertex[kind], 0.0, e) for kind, e in zip(vertices, entries)]

    state = [[], [], []]
    for tile in range(8):
        at = 8 * tile
        base = (32 * p + at) if tile < 4 else (32 * q + at - 32)
        done = relax(
            [ct[at : at + 8, 0:128], ct[at : at + 8, 128:256], kt[at : at + 8, :]], (0, 1, 2), 16 + tile, base
        )
        for kind in range(3):
            state[kind].append(done[kind])
    for b in range(8):
        eliminate(state, b)
        if b < 4:
            for tile in range(4 * b, 4 * b + 4):
                at = 8 * tile
                entries = [mt[at : at + 8, 0:128], mt[at : at + 8, 128:256], rt[at : at + 8, :]]
                entries = relax(entries, (0, 1, 2), tile, 128 * col + at)
                new[at : at + 8, 0:128] = entries[0]
                new[at : at + 8, 128:256] = entries[1]
                rt[at : at + 8, :] = entries[2]
        else:
            if b == 4:
                parts = thirds(rt[...])
            for c in range(8):
                at = 2048 * (b - 4) + 256 * c
                spread[:, at : at + 256] = jnp.dot(
                    parts[b - 4], onehot[:, 256 * c : 256 * c + 256], preferred_element_type=F32
                )
    for tile in range(8):
        at = 8 * tile
        ct[at : at + 8, 0:128] = state[0][tile]
        ct[at : at + 8, 128:256] = state[1][tile]

    for at in range(0, COLS, 8):
        one = new[at : at + 8, 0:128]
        two = new[at : at + 8, 128:256]
        for t in range(2 * PIVOT):
            wide = spread[at : at + 8, 128 * t : 128 * t + 128]
            one = jnp.minimum(one, wide + ct[t : t + 1, 0:128])
            two = jnp.minimum(two, wide + ct[t : t + 1, 128:256])
        new[at : at + 8, 0:128] = one
        new[at : at + 8, 128:256] = two
    for h in range(2):
        out[128 * h : 128 * h + 128, :] = new[:, 128 * h : 128 * h + 128].T


VM = pl.BlockSpec(memory_space=pltpu.VMEM)
SM = pl.BlockSpec(memory_space=pltpu.SMEM)
HBM = pl.BlockSpec(memory_space=pltpu.HBM)
MIB = 1024 * 1024


def call(kernel, shapes, scratch, ins, mib, outs=None):
    return pl.pallas_call(
        kernel,
        out_shape=[s if isinstance(s, jax.ShapeDtypeStruct) else jax.ShapeDtypeStruct(s, F32) for s in shapes],
        in_specs=ins,
        out_specs=outs or [VM] * len(shapes),
        scratch_shapes=[pltpu.VMEM(s, F32) if isinstance(s, tuple) else s for s in scratch],
        compiler_params=pltpu.CompilerParams(vmem_limit_bytes=mib * MIB),
    )


FINAL_SCRATCH = [(3, 16, 128), (128, 128), (64, 256), (64, 128), (128, 128), (128, 8192), (128, 256)]
ONEHOT = jax.ShapeDtypeStruct((64, 16 * 128), jnp.bfloat16)
PIVOTS = jax.ShapeDtypeStruct((2,), jnp.int32)


def on_device(distances, neighbor_ids, edge_lengths, pivots):
    piv, mt, scatter, panel, own_lengths = call(
        pack_kernel,
        [PIVOTS, (COLS, ROWS), (HOLDERS, 16, 128), (64, 128), (8, 128)],
        [(ROWS, COLS), (8, NEIGHBORS), pltpu.SemaphoreType.DMA((4,))],
        [HBM] * 3,
        8,
        [SM] + [VM] * 4,
    )(*[pltpu.with_memory_space_constraint(x, pltpu.HBM) for x in (pivots, distances, edge_lengths.T)])
    lane_ids, sub_ids, onehot = call(
        ids_kernel, [(3, 16, 128), (24, NEIGHBORS, 8, 128), ONEHOT], [(128, 128)], [SM, VM], 16
    )(piv, neighbor_ids)
    other_panel = lax.ppermute(panel, "row", [(i, i ^ 1) for i in range(NXY)])
    scatter = lax.all_to_all(scatter, ("z1", "z0", "core"), 0, 0)
    scatter, lane_ids, sub_ids, onehot = lax.optimization_barrier((scatter, lane_ids, sub_ids, onehot))
    xy, keep, send = call(spread_kernel, [(NXY, XY_ROWS, 128), (8, 128), (8, 128)], [], [SM] + [VM] * 4, 8)(
        piv, scatter, own_lengths, panel, other_panel
    )
    other = lax.ppermute(send, "z2", [(0, 1), (1, 0)])
    xy = lax.all_to_all(xy, "row", 0, 0)
    zed, rows = call(gather_kernel, [(NZ, Z_ROWS, 128), (64, 128)], [], [SM] + [VM] * 3, 8)(piv, xy, keep, other)
    zed = lax.all_to_all(zed, ("z3", "z2", "z1", "z0"), 0, 0)
    zed = lax.all_gather(zed, "core")
    (out,) = call(final_kernel, [(ROWS, COLS)], FINAL_SCRATCH, [SM] + [VM] * 6, 24)(
        piv, mt, rows, zed, lane_ids, sub_ids, onehot
    )
    return out


def solution(mesh):
    fine = Mesh(mesh.devices.reshape(16, 2, 2, 2, 2, 2), ("row", "z3", "z2", "z1", "z0", "core"))
    cols = ("z3", "z2", "z1", "z0", "core")
    placed = (P("row", cols), P(), P(None, ("row", *cols)), P())
    return jax.shard_map(on_device, mesh=fine, in_specs=placed, out_specs=P("row", cols), check_vma=False)
```

```python
import jax
import jax.numpy as jnp
from jax import lax
from jax.experimental import pallas as pl
from jax.experimental.pallas import tpu as pltpu
from jax.sharding import Mesh, PartitionSpec as P

NEIGHBORS = 10
PIVOT = 32
ROWS = 256
COLS = 128
NXY = 16
NZ = 16
F32 = jnp.float32
INF = float("inf")

XY_P, XY_Q, XY_ROWS = 8, 24, 40
Z_L, Z_ROWS = 8, 16
HOLDERS = 8


def lanes(rows):
    return lax.broadcasted_iota(jnp.int32, (rows, 128), 1)


def shift_lanes(x, amount):
    if isinstance(amount, int):
        return pltpu.roll(x, amount % 128, 1) if amount % 128 else x
    return pltpu.roll(x, lax.rem(amount + 1024, 128), 1)


def place():
    z = 0
    for bit in ("z3", "z2", "z1", "z0"):
        z = 2 * z + lax.axis_index(bit)
    return lax.axis_index("row"), z, lax.axis_index("core")


def rank(z):
    return z // 8 * 8 + z // 2 % 2 * 4 + z // 4 % 2 * 2 + z % 2


def upper_half():
    return lax.broadcasted_iota(jnp.int32, (8, 128), 0) < 4


def pack_kernel(pivots, dist, lengths, piv, mt, scatter, panel, own_lengths, block, held, sems):
    copies = [
        pltpu.make_async_copy(dist, block, sems.at[0]),
        pltpu.make_async_copy(lengths, held, sems.at[1]),
        pltpu.make_async_copy(pivots, piv, sems.at[2]),
    ]
    for copy in copies:
        copy.start()
    for copy in copies:
        copy.wait()
    for h in range(2):
        mt[:, 128 * h : 128 * h + 128] = block[128 * h : 128 * h + 128, :].T
    for i in range(2):
        off = lax.rem(piv[i], 4) * PIVOT
        for n in range(0, HOLDERS, 2):
            lines = mt[pl.ds(pl.multiple_of(off + 4 * n, 8), 8), :]
            for m in range(2):
                for h in range(2):
                    at = 8 * i + 4 * h
                    scatter[n + m, at : at + 4, :] = lines[4 * m : 4 * m + 4, 128 * h : 128 * h + 128]
        panel[32 * i : 32 * i + 32, :] = block[pl.ds(pl.multiple_of(lax.rem(piv[i], 8) * PIVOT, 32), 32), :]
    spaced = jnp.concatenate([held[...], jnp.zeros((8, 128 - NEIGHBORS), F32)], 1)
    lines = jnp.concatenate([spaced, jnp.zeros((120, 128), F32)], 0).T
    low, high = lines[0:8], lines[8:16]
    own_lengths[...] = low + shift_lanes(pltpu.roll(low, 4, 0), 32) + shift_lanes(high, 64)


def spread_kernel(piv, got, own_lengths, panel, other_panel, xy, keep, send):
    p, q = piv[0], piv[1]
    row, z, _ = place()
    corner, halves = None, [[], []]
    for i, pivot in enumerate((p, q)):
        holder = lax.rem(pivot // 4, HOLDERS)
        mine = got[holder, 8 * i : 8 * i + 8]
        for b in range(2):
            halves[b] += [mine[2 * b : 2 * b + 2], mine[4 + 2 * b : 6 + 2 * b]]
        for j, other in enumerate((p, q)):
            half = jnp.where(lax.rem(other // 4, 2) == 0, mine, pltpu.roll(mine, 4, 0))
            half = shift_lanes(half, 64 * i + 32 * j - lax.rem(other, 4) * PIVOT)
            corner = half if corner is None else jnp.where(lanes(8) // PIVOT == 2 * i + j, half, corner)
    first, second = [jnp.concatenate(parts, 0) for parts in halves]
    even = lax.rem(z // 4, 2) == 0
    keep[...] = jnp.where(even, first, second)
    send[...] = jnp.where(even, second, first)
    small = jnp.where(upper_half(), own_lengths[...], pltpu.roll(corner, 4, 0))
    part = pl.multiple_of(16 * lax.rem(row, 2), 16)
    lines = [
        jnp.where(
            lax.rem(pivot // 8 + row, 2) == 0,
            panel[pl.ds(32 * i + part, 16), :],
            other_panel[pl.ds(32 * i + part, 16), :],
        )
        for i, pivot in enumerate((p, q))
    ]
    for d in range(NXY):
        xy[d, 0:XY_P] = small
        xy[d, XY_P:XY_Q] = lines[0]
        xy[d, XY_Q:XY_ROWS] = lines[1]


def gather_kernel(piv, xy, keep, other, zchunk, rows):
    p, q = piv[0], piv[1]
    row, z, core = place()
    row_p, row_q = p // 8, q // 8
    for b in range(2):
        rows[16 * b : 16 * b + 16] = xy[row_p // 2 * 2 + b, XY_P:XY_Q]
        rows[32 + 16 * b : 48 + 16 * b] = xy[row_q // 2 * 2 + b, XY_Q:XY_ROWS]
    upper = upper_half()
    bit = lax.rem(z // 4, 2)
    piece = jnp.where(
        upper,
        jnp.where(lax.rem(p // 32, 2) == bit, keep[...], other[...]),
        jnp.where(lax.rem(q // 32, 2) == bit, keep[...], other[...]),
    )
    corner = jnp.where(lax.rem(lanes(8) // PIVOT, 2) == 0, xy[row_p, 0:XY_P], xy[row_q, 0:XY_P])
    turn = 2 * lax.rem(z, 2) + core

    def take(device, at):
        return shift_lanes(xy[device, 0:XY_P], 8 * lax.rem(turn + at, 4))

    fixed = take(row, 0) + take(row_p, 2) + take(row_q, 3)
    for d in range(NZ):
        zchunk[rank(d), 0:Z_L] = piece
        zchunk[rank(d), Z_L:Z_ROWS] = jnp.where(upper, fixed + take(d, 1), corner)


def ids_kernel(piv, ids, lane_ids, sub_ids, onehot, held):
    p, q = piv[0], piv[1]
    row, z, core = place()
    col = 2 * z + core

    def block(base):
        x = ids[:, pl.ds(pl.multiple_of(base, 128), 128)].astype(F32)
        return jnp.concatenate([x, jnp.zeros((6, 128), F32)], 0)

    for h in range(2):
        lane_ids[h] = block(256 * row + 128 * h)
    pivot_p = shift_lanes(block(p // 4 * 128), 0 - lax.rem(p, 4) * PIVOT)
    pivot_q = shift_lanes(block(q // 4 * 128), 32 - lax.rem(q, 4) * PIVOT)
    pivots = jnp.where(lanes(16) < 32, pivot_p, pivot_q)
    lane_ids[2] = pivots
    held[...] = jnp.zeros_like(held)
    held[0:16] = block(128 * col)
    held[16:32] = pivots
    turned = held[...].T
    for tile in range(24):
        at = 8 * (tile % 16)
        for k in range(NEIGHBORS):
            lane = 16 * (tile // 16) + k
            sub_ids[tile, k] = jnp.broadcast_to(turned[at : at + 8, lane : lane + 1], (8, 128))
    term = lax.broadcasted_iota(jnp.int32, (64, 128), 0)
    for t in range(16):
        picked = (lax.rem(term, 16) == t) & (term < 48)
        onehot[:, 128 * t : 128 * t + 128] = jnp.where(picked, 1.0, 0.0).astype(jnp.bfloat16)


def over_lanes(x, lane):
    return jnp.broadcast_to(x[:, lane : lane + 1], (8, 128))


def over_rows(x, row):
    return jnp.broadcast_to(x[row : row + 1, :], (8, 128))


def eliminate(state, b):
    corner = state[2]
    columns = [over_lanes(corner[b], 8 * b + j) for j in range(8)]
    rows = [state[kind][b] for kind in range(3)]
    for j in range(8):
        for u in range(j + 1, 8):
            columns[u] = jnp.minimum(columns[u], columns[j] + over_rows(columns[u], j))
        rows = [jnp.minimum(r, columns[j] + over_rows(r, j)) for r in rows]
    closed = [[over_rows(r, j) for j in range(8)] for r in rows]
    for i in range(8):
        if i == b:
            continue
        columns = [over_lanes(corner[i], 8 * b + j) for j in range(8)]
        for kind in range(3):
            paths = [columns[j] + closed[kind][j] for j in range(8)]
            while len(paths) > 1:
                paths = [jnp.minimum(paths[n], paths[n + 1]) for n in range(0, len(paths), 2)]
            state[kind][i] = jnp.minimum(state[kind][i], paths[0])
    for kind in range(3):
        state[kind][b] = rows[kind]


def thirds(x):
    high = x.astype(jnp.bfloat16)
    rest = x - high.astype(F32)
    mid = rest.astype(jnp.bfloat16)
    low = (rest - mid.astype(F32)).astype(jnp.bfloat16)
    return [
        jnp.concatenate([term[:, 16 * n : 16 * n + 16] for term in (high, mid, low, low)], 1) for n in range(4)
    ]


def final_kernel(piv, mt, rows, zed, lane_ids, sub_ids, onehot, out, lane_len, turned, ct, kt, rt, spread, new):
    p, q = piv[0], piv[1]
    row, z, core = place()
    col = 2 * z + core
    slot = lax.rem(lanes(8) // 8, 4)

    def lengths_at(first, count, at):
        parts = [None] * 3
        for v in range(count):
            merged = None
            for w in range(4):
                device = first + 4 * v + w
                tile = zed[w % 2, rank(device // 2), Z_L:Z_ROWS]
                merged = tile if w == 0 else jnp.where(slot == (at + w) % 4, tile, merged)
            for g in range(3):
                moved = shift_lanes(merged, 32 * (v - g))
                parts[g] = moved if v == 0 else jnp.where(lanes(8) // 32 >= v, moved, parts[g])
        both = [jnp.where(upper_half(), parts[0], pltpu.roll(parts[1], 4, 0)), parts[2]]
        if at:
            both = [
                jnp.where(slot < 4 - at, shift_lanes(part, -8 * at), shift_lanes(part, 32 - 8 * at)) for part in both
            ]
        return jnp.concatenate(both, 0)

    lane_len[0] = lengths_at(0, 4, 0)
    lane_len[1] = lengths_at(16, 4, 0)
    lane_len[2] = jnp.where(
        lanes(16) < 32,
        lengths_at(lax.rem(p, 8) * 4, 1, 2),
        shift_lanes(lengths_at(lax.rem(q, 8) * 4, 1, 3), 32),
    )
    square = jnp.concatenate([lengths_at(16 * core, 4, 1), lane_len[2], jnp.zeros((96, 128), F32)], 0)
    turned[...] = square.T
    rt[:, 0:64] = rows[...].T

    for i, pivot in enumerate((p, q)):
        home = pivot // 64 * 8
        for n in range(HOLDERS):
            at = 32 * i + 4 * n
            base = home + n // 2
            for b in range(2):
                part = zed[n % 2, rank(base + 4 * b), 0:Z_L]
                ct[at + 2 * b : at + 2 * b + 2, 0:128] = part[4 * i : 4 * i + 2]
                ct[at + 2 * b : at + 2 * b + 2, 128:256] = part[4 * i + 2 : 4 * i + 4]
            corner = zed[n % 2, rank(base + 4 * lax.rem(pivot // 32, 2)), Z_L:Z_ROWS]
            kt[at : at + 4, :] = shift_lanes(corner, 64 * i)[4:8]

    lane = lanes(8)
    sub = lax.broadcasted_iota(jnp.int32, (8, 128), 0)
    vertex = [
        (256 * row + lane).astype(F32),
        (256 * row + 128 + lane).astype(F32),
        jnp.where(lane < 32, 32 * p + lane, jnp.where(lane < 64, 32 * q + lane - 32, -1)).astype(F32),
    ]

    def relax(entries, vertices, tile, base):
        own = (base + sub).astype(F32)
        at, shift = 8 * (tile % 16), 16 * (tile // 16)
        turn = turned[at : at + 8, :]
        entries = list(entries)
        for k in range(NEIGHBORS):
            own_ids = sub_ids[tile, k]
            own_len = jnp.broadcast_to(turn[:, shift + k : shift + k + 1], (8, 128))
            for n, kind in enumerate(vertices):
                there = jnp.where(own_ids == vertex[kind], own_len, INF)
                back = jnp.where(lane_ids[kind, k : k + 1, :] == own, lane_len[kind, k : k + 1, :], INF)
                entries[n] = jnp.minimum(entries[n], jnp.minimum(there, back))
        return [jnp.where(own == vertex[kind], 0.0, e) for kind, e in zip(vertices, entries)]

    state = [[], [], []]
    for tile in range(8):
        at = 8 * tile
        base = (32 * p + at) if tile < 4 else (32 * q + at - 32)
        done = relax(
            [ct[at : at + 8, 0:128], ct[at : at + 8, 128:256], kt[at : at + 8, :]], (0, 1, 2), 16 + tile, base
        )
        for kind in range(3):
            state[kind].append(done[kind])
    for b in range(8):
        eliminate(state, b)
        if b < 4:
            for tile in range(4 * b, 4 * b + 4):
                at = 8 * tile
                entries = [mt[at : at + 8, 0:128], mt[at : at + 8, 128:256], rt[at : at + 8, :]]
                entries = relax(entries, (0, 1, 2), tile, 128 * col + at)
                new[at : at + 8, 0:128] = entries[0]
                new[at : at + 8, 128:256] = entries[1]
                rt[at : at + 8, :] = entries[2]
        else:
            if b == 4:
                parts = thirds(rt[...])
            for c in range(4):
                at = 2048 * (b - 4) + 512 * c
                spread[:, at : at + 512] = jnp.dot(
                    parts[b - 4], onehot[:, 512 * c : 512 * c + 512], preferred_element_type=F32
                )
    for tile in range(8):
        at = 8 * tile
        ct[at : at + 8, 0:128] = state[0][tile]
        ct[at : at + 8, 128:256] = state[1][tile]

    for at in range(0, COLS, 8):
        one = new[at : at + 8, 0:128]
        two = new[at : at + 8, 128:256]
        for t in range(2 * PIVOT):
            wide = spread[at : at + 8, 128 * t : 128 * t + 128]
            one = jnp.minimum(one, wide + ct[t : t + 1, 0:128])
            two = jnp.minimum(two, wide + ct[t : t + 1, 128:256])
        new[at : at + 8, 0:128] = one
        new[at : at + 8, 128:256] = two
    for h in range(2):
        out[128 * h : 128 * h + 128, :] = new[:, 128 * h : 128 * h + 128].T


VM = pl.BlockSpec(memory_space=pltpu.VMEM)
SM = pl.BlockSpec(memory_space=pltpu.SMEM)
HBM = pl.BlockSpec(memory_space=pltpu.HBM)
MIB = 1024 * 1024


def call(kernel, shapes, scratch, ins, mib, outs=None):
    return pl.pallas_call(
        kernel,
        out_shape=[s if isinstance(s, jax.ShapeDtypeStruct) else jax.ShapeDtypeStruct(s, F32) for s in shapes],
        in_specs=ins,
        out_specs=outs or [VM] * len(shapes),
        scratch_shapes=[pltpu.VMEM(s, F32) if isinstance(s, tuple) else s for s in scratch],
        compiler_params=pltpu.CompilerParams(vmem_limit_bytes=mib * MIB),
    )


FINAL_SCRATCH = [(3, 16, 128), (128, 128), (64, 256), (64, 128), (128, 128), (128, 8192), (128, 256)]
ONEHOT = jax.ShapeDtypeStruct((64, 16 * 128), jnp.bfloat16)
PIVOTS = jax.ShapeDtypeStruct((2,), jnp.int32)


def on_device(distances, neighbor_ids, edge_lengths, pivots):
    piv, mt, scatter, panel, own_lengths = call(
        pack_kernel,
        [PIVOTS, (COLS, ROWS), (HOLDERS, 16, 128), (64, 128), (8, 128)],
        [(ROWS, COLS), (8, NEIGHBORS), pltpu.SemaphoreType.DMA((3,))],
        [HBM] * 3,
        8,
        [SM] + [VM] * 4,
    )(*[pltpu.with_memory_space_constraint(x, pltpu.HBM) for x in (pivots, distances, edge_lengths.T)])
    lane_ids, sub_ids, onehot = call(
        ids_kernel, [(3, 16, 128), (24, NEIGHBORS, 8, 128), ONEHOT], [(128, 128)], [SM, VM], 16
    )(piv, neighbor_ids)
    other_panel = lax.ppermute(panel, "row", [(i, i ^ 1) for i in range(NXY)])
    scatter = lax.all_to_all(scatter, ("z1", "z0", "core"), 0, 0)
    scatter, lane_ids, sub_ids, onehot = lax.optimization_barrier((scatter, lane_ids, sub_ids, onehot))
    xy, keep, send = call(spread_kernel, [(NXY, XY_ROWS, 128), (8, 128), (8, 128)], [], [SM] + [VM] * 4, 8)(
        piv, scatter, own_lengths, panel, other_panel
    )
    other = lax.ppermute(send, "z2", [(0, 1), (1, 0)])
    xy = lax.all_to_all(xy, "row", 0, 0)
    zed, rows = call(gather_kernel, [(NZ, Z_ROWS, 128), (64, 128)], [], [SM] + [VM] * 3, 8)(piv, xy, keep, other)
    zed = lax.all_to_all(zed, ("z3", "z1", "z2", "z0"), 0, 0)
    zed = lax.all_gather(zed, "core")
    (out,) = call(final_kernel, [(ROWS, COLS)], FINAL_SCRATCH, [SM] + [VM] * 6, 24)(
        piv, mt, rows, zed, lane_ids, sub_ids, onehot
    )
    return out


def solution(mesh):
    fine = Mesh(mesh.devices.reshape(16, 2, 2, 2, 2, 2), ("row", "z3", "z2", "z1", "z0", "core"))
    cols = ("z3", "z2", "z1", "z0", "core")
    placed = (P("row", cols), P(), P(None, ("row", *cols)), P())
    return jax.shard_map(on_device, mesh=fine, in_specs=placed, out_specs=P("row", cols), check_vma=False)
```
